32 devices in a mesh: group: 16 (over z, y, core), item: 2 (over x).
Axes of the slice: x: 2, y: 2, z: 4, core: 2. Of those that a mesh axis runs over, the one named last changes fastest.
Arguments:
- tokens: bfloat16 [16, 2048, 384], P('group', 'item'), may hold values from -6 to 6
- cotangent: bfloat16 [16, 2048, 384], P('group', 'item'), may hold values from -6 to 6
- params: bfloat16 [1774080], P(('group', 'item')), as said below
- subnets: int32 [16, 3], P('group'), may hold values from 4 to 1536, as said below
- lengths: int32 [16, 2, 4], P('group', 'item'), may hold values from 1 to 480, 960 in all within a row
Outputs:
- layer_out: bfloat16 [16, 2048, 384], P('group', 'item')
- input_grad: float32 [16, 2048, 384], P('group', 'item')
- param_grad: float32 [1774080], P(('group', 'item'))
The draws below stay inside these ranges and needn't reach their ends.
Inputs may be any that keep to these rules, and one draw needn't show every extreme that they name: `subnets`: column 0 is a width among 384, 5/6 of 384 and 2/3 of 384; column 1 is a head count from 4 to 6; column 2 is the width times 3, 3.5 or 4. One group takes the largest subnet and another the smallest. `params`: the matrices' entries are scaled by their fan-in (a few hundredths to a few tenths); the width vectors g1 and g2 lie near 1; the other vectors and the hidden bias have entries of a few tenths.
All inputs are finite; a program needn't handle non-finite values.
Results may differ from the reference program's by a relative error of at most 0.012.
Values may be sent and summed in bfloat16 or wider, within the bound.
A program may use at most 128 MiB of HBM per device.

```python
import math
import jax
import jax.numpy as jnp
import numpy as np
from jax import lax

HD = 64
HEADS = 6
D = 384
FF = 1536
ROWS = 1024
UTTS = 4
LIVE = 960
MOSTLEN = 480
GROUPS = 16
NPARAM = 1774080
N_ITEM = 2


def draw_params(key, part):
    key = jax.random.fold_in(key, 3)
    base = jnp.clip(jax.random.normal(key, (NPARAM,), jnp.float32), -4.0, 4.0)
    root_width = D ** (-0.5)
    root_hidden = FF ** (-0.5)
    layout = [(D * D, 1.5 * root_width, 0.0), (D * D, 1.5 * root_width, 0.0), (D * D, root_width, 0.0), (D * D, 4.0 * root_width, 0.0), (D * FF, root_width, 0.0), (FF * D, 1.5 * root_hidden, 0.0), (FF, 0.3, 0.0), (D, 0.3, 0.0), (D, 0.3, 0.0), (D, 0.3, 0.0), (D, 0.15, 1.0), (D, 0.3, 0.0), (D, 0.3, 0.0), (D, 0.15, 1.0), (D, 0.3, 0.0)]
    scales = jnp.concatenate([jnp.full((count_entries,), factor, jnp.float32) for count_entries, factor, shift in layout])
    shifts = jnp.concatenate([jnp.full((count_entries,), shift, jnp.float32) for count_entries, factor, shift in layout])
    return (base * scales + shifts).astype(jnp.bfloat16)


def draw_subnets(key, part):
    key = jax.random.fold_in(key, 7)
    key_list = jax.random.split(key, 5)
    shrink_level = jax.random.randint(key_list[0], (GROUPS,), 0, 3)
    heads_drawn = jax.random.randint(key_list[1], (GROUPS,), HEADS - 2, HEADS + 1)
    ratio_drawn = jax.random.randint(key_list[2], (GROUPS,), 6, 9)
    largest = jax.random.randint(key_list[3], (), 0, GROUPS)
    smallest = (largest + 1 + jax.random.randint(key_list[4], (), 0, GROUPS - 1)) % GROUPS
    position_ids = jnp.arange(GROUPS)
    shrink_level = jnp.where(position_ids == largest, 0, jnp.where(position_ids == smallest, 2, shrink_level))
    heads_drawn = jnp.where(position_ids == largest, HEADS, jnp.where(position_ids == smallest, HEADS - 2, heads_drawn))
    ratio_drawn = jnp.where(position_ids == largest, 8, jnp.where(position_ids == smallest, 6, ratio_drawn))
    width = D - shrink_level * (D // 6)
    hidden = width * ratio_drawn // 2
    return jnp.stack([width, heads_drawn, hidden], axis=1).astype(jnp.int32)


def block_scale(rng, shape, cuts, least, top_value):
    loudness, own = 1.0, jax.random.fold_in(rng, 6)
    for position, shards_of in cuts:
        steps = jnp.exp(jax.random.uniform(jax.random.fold_in(own, position), (shards_of,), jnp.float32, least / len(cuts), top_value / len(cuts)))
        loudness = loudness * jnp.repeat(steps, shape[position] // shards_of).reshape([-1 if axis == position else 1 for axis in range(len(shape))])
    return loudness


def length_profile(count, total, most, lean):
    weights = [(1 << 20) // math.isqrt(grade ** lean) + 1 for grade in range(2, count + 1)]
    surplus, counts = total - most - (count - 1), [1] * (count - 1)
    while surplus > 0:
        candidates = [i for i in range(count - 1) if counts[i] < most]
        whole, remaining = sum([weights[i] for i in candidates]), surplus
        for i in candidates:
            addition = min(most - counts[i], max(1, remaining * weights[i] // whole), surplus)
            counts[i] = counts[i] + addition
            surplus = surplus - addition
    return np.array([most] + counts)


def ragged(stream_key, amount, total, most, skew):
    if amount == 2:
        one = jax.random.randint(stream_key, (), max(1, total - most), min(most, total - 1) + 1)
        return jnp.stack([one, total - one])
    sizes = jnp.asarray(length_profile(amount, total, most, skew), jnp.int32)
    pairs = (amount - 1) // 2
    giver, taker = sizes[1:1 + 2 * pairs:2], sizes[2:2 + 2 * pairs:2]
    room = jnp.minimum(giver - 1, most - taker)
    passed = jax.random.randint(jax.random.fold_in(stream_key, 1), (pairs,), 0, 1 << 20) % (room + 1)
    sizes = sizes.at[1:1 + 2 * pairs:2].set(giver - passed).at[2:2 + 2 * pairs:2].set(taker + passed)
    return sizes[jax.random.permutation(jax.random.fold_in(stream_key, 2), amount)]


def bell_draw(stream_key, shape, deviation, most, cuts=(), held_as=jnp.bfloat16):
    drawn = deviation * jax.random.normal(stream_key, shape, jnp.float32)
    if cuts:
        drawn = drawn * block_scale(stream_key, shape, cuts, -0.22, 0.18)
    return jnp.clip(drawn, -most, most).astype(held_as)


def setup_inputs(seed: int = 0) -> dict:
    arg_keys = jax.random.split(jax.random.key(seed), 6)
    return {
        "tokens": bell_draw(arg_keys[0], (GROUPS, N_ITEM * ROWS, D), 1.0, 6.0, ((0, 16), (1, 2))),
        "cotangent": bell_draw(arg_keys[1], (GROUPS, N_ITEM * ROWS, D), 1.0, 6.0, ((0, 16), (1, 2))),
        "params": draw_params(jax.random.fold_in(arg_keys[5], 71), 0),
        "subnets": draw_subnets(jax.random.fold_in(arg_keys[5], 71), 0),
        "lengths": jax.vmap(lambda own: ragged(own, UTTS, LIVE, MOSTLEN, 2))(jax.random.split(arg_keys[4], GROUPS * N_ITEM)).reshape((GROUPS, N_ITEM, UTTS)).astype(jnp.int32),
    }


@jax.custom_vjp
def low(v):
    return lax.optimization_barrier(v.astype(jnp.bfloat16)).astype(jnp.float32)

@jax.custom_vjp
def low_back(v):
    return v

def low_keep(v):
    return (low(v), None)

def low_pass(kept, grad):
    return (grad,)

def back_keep(v):
    return (v, None)

def back_low(kept, grad):
    return (low(grad),)
low.defvjp(low_keep, low_pass)
low_back.defvjp(back_keep, back_low)

def matmul(left, right):
    return jnp.dot(left, right, precision=lax.Precision.HIGHEST)

def unpack(flat):
    square = D * D
    up_start = 4 * square
    down_start = up_start + D * FF
    bias_start = down_start + FF * D
    return (flat[0:square].reshape(D, D), flat[square:2 * square].reshape(D, D), flat[2 * square:3 * square].reshape(D, D), flat[3 * square:up_start].reshape(D, D), flat[up_start:down_start].reshape(D, FF), flat[down_start:bias_start].reshape(FF, D), flat[bias_start:bias_start + FF], flat[bias_start + FF:].reshape(8, D))

def layer_norm(hidden, gain, shift, feature_mask, count):
    center = (hidden - lax.optimization_barrier(jnp.sum(hidden * feature_mask, axis=-1, keepdims=True)) / count) * feature_mask
    spread = lax.optimization_barrier(jnp.sum(center * center, axis=-1, keepdims=True)) / count
    return center * lax.rsqrt(spread + 1e-05) * gain + shift

def forward(inputs, flat, feature_mask, attend_mask, hidden_mask, count, allowed, row_mask):
    w_query, w_key, w_value, w_out, w_up, w_down, bias_hidden, vectors = unpack(flat)
    mask_in = feature_mask[:, None] * attend_mask[None, :]
    w_query = w_query * mask_in
    w_key = w_key * mask_in
    w_value = w_value * mask_in
    w_out = w_out * (attend_mask[:, None] * feature_mask[None, :])
    w_up = w_up * (feature_mask[:, None] * hidden_mask[None, :])
    w_down = w_down * (hidden_mask[:, None] * feature_mask[None, :])
    bias_hidden = bias_hidden * hidden_mask
    row_masks = jnp.stack([attend_mask, attend_mask] + [feature_mask] * 6)
    vectors = vectors * row_masks
    masked_in = inputs * feature_mask
    queries = low(low_back(matmul(masked_in, w_query) + vectors[0]))
    keys_rows = low(low_back(matmul(masked_in, w_key)))
    value_rows = low(low_back(matmul(masked_in, w_value) + vectors[1]))
    query_heads = queries.reshape(ROWS, HEADS, HD)
    key_heads = keys_rows.reshape(ROWS, HEADS, HD)
    value_heads = value_rows.reshape(ROWS, HEADS, HD)
    scores = low_back(jnp.einsum('qhd,khd->hqk', query_heads, key_heads, precision=lax.Precision.HIGHEST) * 0.125)
    scores = jnp.where(allowed[None], scores, -1e+30)
    probs = low(jax.nn.softmax(scores, axis=-1))
    mixed = jnp.einsum('hqk,khd->qhd', probs, value_heads, precision=lax.Precision.HIGHEST).reshape(ROWS, D)
    mixed = low(low_back(mixed))
    attended = low_back(matmul(mixed, w_out) + vectors[2])
    norm_one = layer_norm(masked_in + attended, vectors[3], vectors[4], feature_mask, count)
    pre_act = low_back(matmul(low(norm_one), w_up) + bias_hidden)
    activated = low(jax.nn.gelu(pre_act, approximate=False))
    branch = low_back(matmul(activated, w_down) + vectors[5])
    result = layer_norm(norm_one + branch, vectors[6], vectors[7], feature_mask, count)
    return result * row_mask[:, None]

def reference(tokens, cotangent, params, subnets, lengths):
    buffers = GROUPS * N_ITEM
    token_rows = tokens.astype(jnp.float32).reshape(buffers, ROWS, D)
    cot_rows = cotangent.astype(jnp.float32).reshape(buffers, ROWS, D)
    length_rows = lengths.reshape(buffers, UTTS)
    subnet_rows = jnp.repeat(subnets, N_ITEM, axis=0)
    flat = params.astype(jnp.float32)

    def step(carry, pieces):
        inputs, cot_piece, length_piece, subnet_piece = pieces
        width = subnet_piece[0]
        feature_mask = (jnp.arange(D, dtype=jnp.int32) < width).astype(jnp.float32)
        attend_mask = (jnp.arange(D, dtype=jnp.int32) < subnet_piece[1] * HD).astype(jnp.float32)
        hidden_mask = (jnp.arange(FF, dtype=jnp.int32) < subnet_piece[2]).astype(jnp.float32)
        count = width.astype(jnp.float32)
        ends = jnp.cumsum(length_piece)
        segment = lax.optimization_barrier(jnp.sum((jnp.arange(ROWS, dtype=jnp.int32)[:, None] >= ends[None, :]).astype(jnp.int32), axis=1))
        allowed = segment[:, None] == segment[None, :]
        row_mask = (segment < UTTS).astype(jnp.float32)

        def local_forward(input_value, flat_value):
            return forward(input_value, flat_value, feature_mask, attend_mask, hidden_mask, count, allowed, row_mask)
        output, pull = jax.vjp(local_forward, inputs, flat)
        grad_input, grad_flat = pull(cot_piece)
        return (carry + grad_flat, (output.astype(jnp.bfloat16), grad_input))
    total, (outputs, grads) = lax.scan(step, jnp.zeros((NPARAM,), jnp.float32), (token_rows, cot_rows, length_rows, subnet_rows))
    shape = (GROUPS, N_ITEM * ROWS, D)
    return (outputs.reshape(shape), grads.reshape(shape), total)
```

```python
import functools

import jax
import jax.numpy as jnp
from jax import lax
from jax.experimental import pallas as pl
from jax.experimental.pallas import tpu as pltpu
from jax.sharding import PartitionSpec as P

HD = 64
HEADS = 6
D = 384
FF = 1536
LIVE = 960
PAIRS = HEADS // 2
CHUNKS = FF // D
BLOCK = 256
TILE = 192
BIG = 1e30
BF = jnp.bfloat16
F32 = jnp.float32
ROW_Q, ROW_K, ROW_V, ROW_O, ROW_UP, ROW_DOWN, ROW_VEC = 0, 384, 768, 1152, 1536, 3072, 4608
ALL_ROWS = 4624
STEP, FRAME, TWO = 144, 160, 304
PLANES = 4
MESH = pl.DeviceIdType.MESH


def dot(left, right):
    return jnp.dot(left, right, preferred_element_type=F32)


def dot_nt(left, right):
    return lax.dot_general(left, right, (((1,), (1,)), ((), ())), preferred_element_type=F32)


def dot_tn(left, right):
    return lax.dot_general(left, right, (((0,), (0,)), ((), ())), preferred_element_type=F32)


def iota(shape, axis):
    return lax.broadcasted_iota(jnp.int32, shape, axis)


def below(shape, axis, bound):
    return jnp.where(iota(shape, axis) < bound, 1.0, 0.0).astype(F32)


def key_range(block, lanes):
    first = max(0, block * BLOCK - 479) // 32 * 32
    last = min(LIVE, -(-(block * BLOCK + BLOCK - 1 + 480) // 32) * 32)
    if block * BLOCK - 479 < 64:
        first = 0
    return first, last


def gelu_parts(z):
    size = jnp.abs(z)
    t = pl.reciprocal(1.0 + (0.3275911 * 0.7071067811865476) * size, approx=False)
    poly = t * (
        0.5 * 0.254829592
        + t
        * (0.5 * -0.284496736 + t * (0.5 * 1.421413741 + t * (0.5 * -1.453152027 + t * (0.5 * 1.061405429))))
    )
    bell = jnp.exp(-0.5 * (z * z))
    tail = poly * bell
    cdf = jnp.where(z >= 0.0, 1.0 - tail, tail)
    return z * cdf, cdf + z * (bell * 0.3989422804014327)


def norm_forward(hidden, gain, shift, feature, inv_count):
    center = (hidden - jnp.sum(hidden * feature, axis=-1, keepdims=True) * inv_count) * feature
    inverse = lax.rsqrt(jnp.sum(center * center, axis=-1, keepdims=True) * inv_count + 1e-05)
    normed = center * inverse
    return normed * gain + shift, normed, inverse


def norm_backward(grad, normed, inverse, gain, feature, inv_count):
    scaled = grad * gain
    first = jnp.sum(scaled, axis=-1, keepdims=True) * inv_count
    second = jnp.sum(scaled * normed, axis=-1, keepdims=True) * inv_count
    return inverse * (scaled - first - normed * second) * feature


def col_sum(value):
    return jnp.sum(value, axis=0, keepdims=True)


class Layer:
    def __init__(self, refs):
        self.__dict__.update(refs)
        self.lanes = self.expo.shape[2]
        width, heads, hidden = self.subnets[0, 0], self.subnets[0, 1], self.subnets[0, 2]
        self.width, self.attend, self.hidden = width, heads * HD, hidden
        self.inv_count = 1.0 / jnp.full((1, 1), width, jnp.int32).astype(F32)

    def row_mask(self, cols, bound, offset=0):
        return jnp.where(iota((1, cols), 1) + offset < bound, 1.0, 0.0).astype(F32)

    def col_mask(self, rows, bound, offset=0):
        return jnp.where(iota((rows, 1), 0) + offset < bound, 1.0, 0.0).astype(F32)

    def feature(self):
        return self.row_mask(D, self.width)

    def vector(self, index):
        mask = self.attend if index < 2 else self.width
        return self.vecs[4 + index : 5 + index, :] * self.row_mask(D, mask)

    def add_sum(self, index, value, lanes=slice(None)):
        rows = value.shape[0]
        part = value[:8, :]
        for start in range(8, rows, 8):
            part = part + value[start : start + 8, :]
        self.sums[index, :, lanes] += part

    def start(self):
        fe = self.feature().astype(BF)
        self.sums[...] = jnp.zeros(self.sums.shape, F32)

        @pl.loop(0, LIVE // TILE)
        def _(tile):
            rows = pl.ds(pl.multiple_of(tile * TILE, TILE), TILE)
            self.xm[rows, :] = self.tokens[rows, :] * fe

        for part in range(PAIRS):
            lanes = slice(part * 128, part * 128 + 128)
            self.xt[lanes, :] = self.xm[:, lanes].T
        pad = self.lanes - LIVE
        self.dot_t[:, :, LIVE:] = jnp.zeros((HEADS, HD, pad), BF)
        self.q_t[:, :, LIVE:] = jnp.zeros((HEADS, HD, pad), BF)
        self.delta[:, :, LIVE:] = jnp.zeros((HEADS, 1, pad), F32)
        self.do_s[LIVE:, :] = jnp.zeros((pad, D), BF)
        self.q_rows[LIVE:, :] = jnp.zeros((pad, D), BF)
        ends = []
        total = 0
        for index in range(4):
            total = total + self.lengths[0, index]
            ends.append(total)
        lane = iota((HD, self.lanes), 1)
        seg = sum((lane >= end).astype(jnp.int32) for end in ends)
        part = iota((HD, self.lanes), 0)
        self.far[...] = jnp.where((part < 4) & (part != seg), -BIG, 0.0).astype(BF)

        @pl.loop(0, LIVE // TILE)
        def _(tile):
            first = pl.multiple_of(tile * TILE, TILE)
            row = iota((TILE, 128), 0) + first
            seg = sum((row >= end).astype(jnp.int32) for end in ends[:3])
            self.hot[pl.ds(first, TILE), :] = jnp.where(iota((TILE, 128), 1) - HD == seg, 1.0, 0.0).astype(BF)

    def load_vectors(self):
        for part in range(PAIRS):
            lanes = slice(part * 128, part * 128 + 128)
            self.vecs[:, lanes] = self.vec_par[part].astype(F32)

    def query_key_value(self, pair):
        lanes = slice(pair * 128, pair * 128 + 128)
        mask = self.col_mask(D, self.width) * self.row_mask(128, self.attend, pair * 128)
        for index, row in enumerate((ROW_Q, ROW_K, ROW_V)):
            weight = (self.flat[pair, row : row + D, :].astype(F32) * mask).astype(BF)
            self.w_qkv[pair, :, index * 128 : index * 128 + 128] = weight
        bias_q, bias_v = self.vector(0)[:, lanes], self.vector(1)[:, lanes]
        even = iota((TILE, 128), 1) < HD

        @pl.loop(0, LIVE // TILE)
        def _(tile):
            rows = pl.ds(pl.multiple_of(tile * TILE, TILE), TILE)
            out = dot(self.xm[rows, :], self.w_qkv[pair])
            self.q_rows[rows, lanes] = (out[:, :128] + bias_q).astype(BF)
            k = out[:, 128:256].astype(BF)
            self.k_rows[rows, :] = k
            k32 = k.astype(F32)
            hot = self.hot[rows, :].astype(F32)
            self.k_ext[2 * pair, rows, :] = jnp.where(even, k32, hot).astype(BF)
            self.k_ext[2 * pair + 1, rows, :] = jnp.where(even, pltpu.roll(k32, HD, 1), hot).astype(BF)
            self.v_rows[rows, lanes] = (out[:, 256:] + bias_v).astype(BF)

        for target, source, factor in (
            (self.q_t, self.q_rows[:LIVE, lanes], 0.125),
            (self.k_t, self.k_rows[...], None),
            (self.v_t, self.v_rows[:, lanes], None),
        ):
            turned = source.T
            if factor is not None:
                turned = turned * jnp.asarray(factor, BF)
            target[2 * pair, :, :LIVE] = turned[:HD, :]
            target[2 * pair + 1, :, :LIVE] = turned[HD:, :]

    def attend_forward(self, head):
        for block in range(self.lanes // BLOCK):
            cols = slice(block * BLOCK, block * BLOCK + BLOCK)
            first, last = key_range(block, self.lanes)
            right = jnp.concatenate([self.q_t[head, :, cols], self.far[:, cols]], axis=0)
            scores = dot(self.k_ext[head, first:last, :], right)
            top = jnp.max(scores, axis=0, keepdims=True)
            expo = jnp.exp(scores - top)
            inv = 1.0 / jnp.sum(expo, axis=0, keepdims=True)
            expo = expo.astype(BF)
            self.expo[head, first:last, cols] = expo
            self.inv[head, :, cols] = inv
            mixed = dot(self.v_t[head, :, first:last], expo) * inv
            self.o_t[head, :, cols] = mixed.astype(BF)

    def after_attention(self):
        mask = self.col_mask(D, self.attend) * self.feature()
        for part in range(PAIRS):
            lanes = slice(part * 128, part * 128 + 128)
            rows = self.flat[part, ROW_O : ROW_O + D, :].astype(F32)
            self.w_out[:, lanes] = (rows * mask[:, lanes]).astype(BF)
        fe, bias, gain, shift = self.feature(), self.vector(2), self.vector(3), self.vector(4)
        for start in range(0, LIVE, BLOCK):
            size = min(BLOCK, LIVE - start)
            rows = slice(start, start + size)
            mixed = self.o_t[:, :, start : start + BLOCK].reshape(D, BLOCK)
            attended = dot_tn(mixed, self.w_out[...])[:size, :]
            hidden = self.xm[rows, :].astype(F32) + attended + bias
            norm, normed, inverse = norm_forward(hidden, gain, shift, fe, self.inv_count)
            self.norm_one[rows, :] = norm
            self.normed_one[rows, :] = normed
            self.inverse_one[rows, :] = jnp.broadcast_to(inverse, (size, 128))
            self.norm_low[rows, :] = norm.astype(BF)

    def up_weights(self):
        for part in range(PAIRS):
            lanes = slice(part * 128, part * 128 + 128)
            self.wide[part] = self.flat[part, ROW_UP : ROW_UP + FF, :].astype(F32)
        for chunk in range(CHUNKS):
            mask = self.col_mask(D, self.width) * self.row_mask(D, self.hidden, chunk * D)
            for part in range(PAIRS):
                lanes = slice(part * 128, part * 128 + 128)
                piece = self.wide[part, pl.ds(chunk, D, stride=CHUNKS), :]
                self.w_up[:, chunk * D + part * 128 : chunk * D + part * 128 + 128] = (
                    piece * mask[:, lanes]
                ).astype(BF)

    def down_weights(self):
        mask = self.feature()

        @pl.loop(0, FF // D)
        def _(chunk):
            first = pl.multiple_of(chunk * D, D)
            for part in range(PAIRS):
                lanes = slice(part * 128, part * 128 + 128)
                rows = self.flat[part, pl.ds(ROW_DOWN + first, D), :].astype(F32)
                both = self.col_mask(D, self.hidden, first) * mask[:, lanes]
                self.w_down[pl.ds(first, D), lanes] = (rows * both).astype(BF)

    def feed_forward(self):
        biases = [
            self.vecs[chunk : chunk + 1, :] * self.row_mask(D, self.hidden, chunk * D) for chunk in range(CHUNKS)
        ]

        @pl.loop(0, LIVE // TILE)
        def _(tile):
            rows = pl.ds(pl.multiple_of(tile * TILE, TILE), TILE)
            low = self.norm_low[rows, :]
            for chunk in range(CHUNKS):
                cols = slice(chunk * D, chunk * D + D)
                z = dot(low, self.w_up[:, cols]) + biases[chunk]
                act, slope = gelu_parts(z)
                self.act[rows, cols] = act.astype(BF)
                self.slope[rows, cols] = slope.astype(BF)

    def finish_forward(self):
        fe = self.feature()
        bias, gain, shift = self.vector(5), self.vector(6), self.vector(7)

        @pl.loop(0, LIVE // TILE)
        def _(tile):
            rows = pl.ds(pl.multiple_of(tile * TILE, TILE), TILE)
            second = self.norm_one[rows, :] + dot(self.act[rows, :], self.w_down[...]) + bias
            result, normed, inverse = norm_forward(second, gain, shift, fe, self.inv_count)
            self.layer_out[rows, :] = result.astype(BF)
            grad = self.cotangent[rows, :].astype(F32)
            grad_second = norm_backward(grad, normed, inverse, gain, fe, self.inv_count)
            self.grad_second[rows, :] = grad_second
            low = grad_second.astype(BF)
            self.d_f[rows, :] = low
            self.add_sum(10, grad * normed)
            self.add_sum(11, grad)
            self.add_sum(9, low.astype(F32))

        self.layer_out[LIVE:, :] = jnp.zeros((self.layer_out.shape[0] - LIVE, D), BF)

    def down_grad(self):
        fe = self.feature()

        @pl.loop(0, FF // BLOCK)
        def _(chunk):
            first = pl.multiple_of(chunk * BLOCK, BLOCK)
            mask = self.col_mask(BLOCK, self.hidden, first) * fe
            grad = dot_tn(self.act[:, pl.ds(first, BLOCK)], self.d_f[...]) * mask
            for part in range(PAIRS):
                lanes = slice(part * 128, part * 128 + 128)
                self.grads[part, pl.ds(ROW_DOWN + first, BLOCK), :] = grad[:, lanes].astype(BF)

    def hidden_grad(self):
        fe = self.feature()
        gain = self.vector(3)

        @pl.loop(0, LIVE // TILE)
        def _(tile):
            rows = pl.ds(pl.multiple_of(tile * TILE, TILE), TILE)
            d_f = self.d_f[rows, :]
            for chunk in range(CHUNKS):
                cols = slice(chunk * D, chunk * D + D)
                grad = dot_nt(d_f, self.w_down[cols, :])
                dz = (grad * self.slope[rows, cols].astype(F32)).astype(BF)
                self.slope[rows, cols] = dz
                self.add_sum(chunk, dz.astype(F32))
            normed = self.normed_one[rows, :]
            grad = self.grad_second[rows, :] + dot_nt(self.slope[rows, :], self.w_up[...])
            grad_first = norm_backward(grad, normed, self.inverse_one[rows, :1], gain, fe, self.inv_count)
            self.norm_one[rows, :] = grad_first
            low = grad_first.astype(BF)
            self.d_a[rows, :] = low
            self.add_sum(7, grad * normed)
            self.add_sum(8, grad)
            self.add_sum(6, low.astype(F32))

    def up_grad(self):
        @pl.loop(0, CHUNKS)
        def _(chunk):
            first = pl.multiple_of(chunk * D, D)
            mask = self.col_mask(D, self.width) * self.row_mask(D, self.hidden, first)
            grad = dot_tn(self.norm_low[...], self.slope[:, pl.ds(first, D)]) * mask
            for part in range(PAIRS):
                lanes = slice(part * 128, part * 128 + 128)
                self.wide[part, pl.ds(chunk, D, stride=CHUNKS), :] = grad[:, lanes]

        for part in range(PAIRS):
            lanes = slice(part * 128, part * 128 + 128)
            self.grads[part, ROW_UP : ROW_UP + FF, :] = self.wide[part].astype(BF)

    def out_grad(self):
        fe = self.feature()
        d_a = self.d_a[...]
        for head in range(HEADS):
            rows = slice(head * HD, head * HD + HD)
            mask = self.col_mask(HD, self.attend, head * HD) * fe
            grad = dot(self.o_t[head, :, :LIVE], d_a) * mask
            for part in range(PAIRS):
                lanes = slice(part * 128, part * 128 + 128)
                self.grads[part, ROW_O + head * HD : ROW_O + head * HD + HD, :] = grad[:, lanes].astype(BF)
            mixed = dot_nt(self.w_out[rows, :], d_a) * self.inv[head, :, :LIVE]
            self.delta[head, :, :LIVE] = col_sum(mixed * self.o_t[head, :, :LIVE].astype(F32))
            self.dot_t[head, :, :LIVE] = mixed.astype(BF)
        for pair in range(PAIRS):
            both = self.dot_t[2 * pair : 2 * pair + 2, :, :LIVE].reshape(128, LIVE)
            self.do_s[:LIVE, pair * 128 : pair * 128 + 128] = both.T

    def attend_backward(self, pair, odd):
        head = 2 * pair + odd
        lanes = slice(pair * 128, pair * 128 + 128)
        upper = iota((128, BLOCK), 0) >= HD
        own_rows = upper == (odd == 1)
        for block in range(self.lanes // BLOCK):
            cols = slice(block * BLOCK, block * BLOCK + BLOCK)
            first, last = key_range(block, self.lanes)
            right = self.dot_t[head, :, cols].astype(F32)
            right = jnp.where(own_rows, jnp.concatenate([right, right], axis=0), 0.0).astype(BF)
            grad = dot(self.v_rows[first:last, lanes], right)
            grad = self.expo[head, first:last, cols].astype(F32) * (grad - self.delta[head, :, cols])
            grad = grad.astype(BF)
            self.act[first:last, cols] = grad
            dq = dot(self.k_t[head, :, first:last], grad) * 0.125
            self.q_t[head, :, cols] = dq.astype(BF)
        own = (iota((1, 128), 1) >= HD) == (odd == 1)
        own = jnp.where(own, 1.0, 0.0).astype(BF)
        self.own[0] = self.do_s[:, lanes] * own
        self.own[1] = self.q_rows[:, lanes] * own
        blocks = self.lanes // BLOCK
        ranges = [key_range(block, self.lanes) for block in range(blocks)]
        cuts = sorted({edge for pair_of in ranges for edge in pair_of})
        for low, high in zip(cuts[:-1], cuts[1:]):
            used = [b for b in range(blocks) if ranges[b][0] <= low and high <= ranges[b][1]]
            span = slice(used[0] * BLOCK, used[-1] * BLOCK + BLOCK)
            self.wide[0, low:high, :] += dot(self.expo[head, low:high, span], self.own[0, span, :])
            self.wide[1, low:high, :] += dot(self.act[low:high, span], self.own[1, span, :])

    def pair_backward(self, pair, after_head):
        lanes = slice(pair * 128, pair * 128 + 128)
        self.wide[:2, :LIVE, :] = jnp.zeros((2, LIVE, 128), F32)

        @pl.loop(0, 2)
        def _(odd):
            self.attend_backward(pair, odd)
            after_head(odd)

        self.slope[:, pair * D : pair * D + 128] = self.q_t[2 * pair : 2 * pair + 2, :, :LIVE].reshape(128, LIVE).T
        self.slope[:, pair * D + 128 : pair * D + 256] = (self.wide[1, :LIVE, :] * 0.125).astype(BF)
        self.slope[:, pair * D + 256 : pair * D + 384] = self.wide[0, :LIVE, :].astype(BF)
        mask = self.col_mask(D, self.width) * self.row_mask(128, self.attend, pair * 128)
        grad = dot(self.xt[...], self.slope[:, pair * D : pair * D + D])
        for index, row in enumerate((ROW_Q, ROW_K, ROW_V)):
            self.grads[pair, row : row + D, :] = (grad[:, index * 128 : index * 128 + 128] * mask).astype(BF)
        totals = dot(jnp.ones((8, LIVE), BF), self.slope[:, pair * D : pair * D + D])
        self.sums[4, 0:1, lanes] = totals[:1, :128]
        self.sums[5, 0:1, lanes] = totals[:1, 256:]

    def input_grad_step(self):
        fe = self.feature()

        @pl.loop(0, LIVE // TILE)
        def _(tile):
            rows = pl.ds(pl.multiple_of(tile * TILE, TILE), TILE)
            total = self.norm_one[rows, :]
            for pair in range(PAIRS):
                total = total + dot_nt(self.slope[rows, pair * D : pair * D + D], self.w_qkv[pair])
            self.input_grad[rows, :] = total * fe

        self.input_grad[LIVE:, :] = jnp.zeros((self.input_grad.shape[0] - LIVE, D), F32)

    def vector_grads(self):
        for index in range(12):
            total = jnp.sum(self.sums[index], axis=0, keepdims=True)
            if index < CHUNKS:
                mask = self.row_mask(D, self.hidden, index * D)
            else:
                mask = self.row_mask(D, self.attend if index < 6 else self.width)
            self.grad_vecs[index : index + 1, :] = total * mask
        self.grad_vecs[12:, :] = jnp.zeros((4, D), F32)


def scratch_refs(lanes):
    vmem = pltpu.VMEM
    return {
        "xm": vmem((LIVE, D), BF),
        "xt": vmem((D, LIVE), BF),
        "hot": vmem((LIVE, 128), BF),
        "far": vmem((HD, lanes), BF),
        "vecs": vmem((16, D), F32),
        "sums": vmem((12, 8, D), F32),
        "w_qkv": vmem((PAIRS, D, D), BF),
        "w_out": vmem((D, D), BF),
        "w_up": vmem((D, FF), BF),
        "w_down": vmem((FF, D), BF),
        "wide": vmem((PAIRS, FF, 128), F32),
        "q_rows": vmem((lanes, D), BF),
        "k_rows": vmem((LIVE, 128), BF),
        "q_t": vmem((HEADS, HD, lanes), BF),
        "k_t": vmem((HEADS, HD, LIVE), BF),
        "k_ext": vmem((HEADS, LIVE, 128), BF),
        "v_rows": vmem((LIVE, D), BF),
        "v_t": vmem((HEADS, HD, LIVE), BF),
        "expo": vmem((HEADS, LIVE, lanes), BF),
        "inv": vmem((HEADS, 1, lanes), F32),
        "o_t": vmem((HEADS, HD, lanes), BF),
        "norm_one": vmem((LIVE, D), F32),
        "normed_one": vmem((LIVE, D), F32),
        "inverse_one": vmem((LIVE, 128), F32),
        "norm_low": vmem((LIVE, D), BF),
        "act": vmem((LIVE, FF), BF),
        "slope": vmem((LIVE, FF), BF),
        "grad_second": vmem((LIVE, D), F32),
        "d_f": vmem((LIVE, D), BF),
        "d_a": vmem((LIVE, D), BF),
        "dot_t": vmem((HEADS, HD, lanes), BF),
        "do_s": vmem((lanes, D), BF),
        "delta": vmem((HEADS, 1, lanes), F32),
        "own": vmem((2, lanes, 128), BF),
    }


class Exchange:
    def __init__(self, refs):
        self.__dict__.update(refs)
        group, self.x = lax.axis_index("group"), lax.axis_index("item")
        self.z, self.y, self.c = group // 4, (group // 2) % 2, group % 2
        self.spot = 2 * self.y + self.x
        self.shard = 2 * group + self.x

    def device(self, z, y, c, x):
        return (z * 4 + y * 2 + c, x)

    def line(self, step):
        return self.device((self.z + step) % PLANES, self.y, self.c, self.x)

    def flat_peer(self, step):
        y, x = (self.y + step // 2) % 2, (self.x + step % 2) % 2
        return self.device(self.z, y, self.c, x)

    def plane_peer(self, step):
        y, x = (self.y + step // 4) % 2, (self.x + step % 2) % 2
        return self.device(self.z, y, (self.c + step // 2 % 2) % 2, x)

    def core_peer(self):
        return self.device(self.z, self.y, 1 - self.c, self.x)

    def greet(self):
        barrier = pltpu.get_barrier_semaphore()
        peers = [self.line(step) for step in (1, 2, 3)] + [self.plane_peer(step) for step in range(1, 8)]
        for peer in peers:
            pl.semaphore_signal(barrier, inc=1, device_id=peer, device_id_type=MESH)

    def greeted(self):
        pl.semaphore_wait(pltpu.get_barrier_semaphore(), 10)

    def copy(self, source, target, send, recv, peer):
        return pltpu.make_async_remote_copy(
            src_ref=source, dst_ref=target, send_sem=send, recv_sem=recv, device_id=peer, device_id_type=MESH
        )


    def offsets(self):
        shift = STEP * self.shard
        return shift // 128, shift % 128

    def frame_own(self):
        rows = self.own_params.shape[0]
        up, across = self.offsets()
        turned = pltpu.roll(self.own_params[...].astype(F32), across, 1)
        late = iota((rows, 128), 1) >= across
        same = jnp.where(late, turned, 0.0).astype(BF)
        carried = jnp.where(late, 0.0, turned).astype(BF)
        gap = 3 * iota((FRAME, rows), 0) - up - iota((FRAME, rows), 1)
        for part in range(PAIRS):
            here = jnp.where(gap == -part, 1.0, 0.0).astype(BF)
            after = jnp.where(gap == 1 - part, 1.0, 0.0).astype(BF)
            frame = dot(here, same) + dot(after, carried)
            self.land[self.z, part, self.c, self.spot] = frame.astype(BF)


    def corner(self):
        return (self.c == 1) & (self.spot == 3)

    def vectors_line(self, step):
        sems = self.par_send.at[step - 1], self.par_recv.at[0]
        return self.copy(self.vec_par, self.vec_par, *sems, self.line(step))

    def vectors_plane(self, step):
        sems = self.par_send.at[step + 2], self.par_recv.at[1]
        return self.copy(self.vec_par, self.vec_par, *sems, self.plane_peer(step))

    def send_vectors_line(self):
        @pl.when(self.corner() & (self.z == PLANES - 1))
        def _():
            self.vec_par[...] = self.land[PLANES - 1, :, 1, 3, STEP:, :]
            for step in (1, 2, 3):
                self.vectors_line(step).start()

    def send_vectors_plane(self):
        @pl.when(self.corner() & (self.z != PLANES - 1))
        def _():
            self.vectors_line(1).wait_recv()

        @pl.when(self.corner())
        def _():
            for step in range(1, 8):
                self.vectors_plane(step).start()

    def finish_vectors_plane(self):
        @pl.when(jnp.logical_not(self.corner()))
        def _():
            self.vectors_plane(1).wait_recv()

    def parts(self, plane, part):
        return pl.ds(part, 1) if plane == 0 else slice(None)

    def gather_line(self, plane, part, step):
        piece = self.land.at[plane, self.parts(plane, part), self.c, self.spot]
        send, recv = self.line_send.at[plane, part, step - 1], self.line_recv.at[plane, part]
        return self.copy(piece, piece, send, recv, self.line(step))

    def gather_flat(self, plane, part, step):
        piece = self.land.at[plane, self.parts(plane, part), self.c, self.spot]
        send, recv = self.flat_send.at[plane, part, step - 1], self.flat_recv.at[plane, part, step - 1]
        return self.copy(piece, piece, send, recv, self.flat_peer(step))

    def arrived_flat(self, plane, part, step):
        y, x = (self.y + step // 2) % 2, (self.x + step % 2) % 2
        piece = self.land.at[plane, self.parts(plane, part), self.c, 2 * y + x]
        send, recv = self.flat_send.at[plane, part, step - 1], self.flat_recv.at[plane, part, step - 1]
        return self.copy(piece, piece, send, recv, self.flat_peer(step))

    def gather_core(self, plane, part, core):
        piece = self.land.at[plane, self.parts(plane, part), core]
        return self.copy(
            piece, piece, self.core_send.at[plane, part], self.core_recv.at[plane, part], self.core_peer()
        )

    def send_line(self, plane, part):
        @pl.when(self.z == plane)
        def _():
            for step in (3, 2, 1):
                self.gather_line(plane, part, step).start()

    def send_flat(self, plane, part):
        @pl.when(self.z != plane)
        def _():
            self.gather_line(plane, part, 1).wait_recv()

        for step in (3, 2, 1):
            self.gather_flat(plane, part, step).start()

    def send_core(self, plane, part):
        for step in (3, 2, 1):
            self.arrived_flat(plane, part, step).wait_recv()
        self.gather_core(plane, part, self.c).start()

    def finish_gather(self, plane, part):
        self.gather_core(plane, part, 1 - self.c).wait_recv()
        for place in range(8):
            y, c, x = place // 4, (place // 2) % 2, place % 2
            chunk = 8 * plane + place
            for block in [part] if plane == 0 else range(PAIRS):
                frame = self.land[plane, block, c, 2 * y + x]
                self.flat[block, chunk * STEP : chunk * STEP + STEP, :] = frame[:STEP, :]
                if chunk:
                    before = (chunk - 1) % 8
                    spot = 2 * (before // 4) + before % 2
                    tail = self.land[(chunk - 1) // 8, block, (before // 2) % 2, spot, STEP:, :]
                    both = tail.astype(F32) + frame[: FRAME - STEP, :].astype(F32)
                    self.flat[block, chunk * STEP : chunk * STEP + FRAME - STEP, :] = both.astype(BF)
                if chunk == 8 * PLANES - 1:
                    self.flat[block, chunk * STEP + STEP : chunk * STEP + FRAME, :] = frame[STEP:, :]

    def drain_gather(self):
        @pl.when(self.corner() & (self.z == PLANES - 1))
        def _():
            for step in (1, 2, 3):
                self.vectors_line(step).wait_send()

        @pl.when(self.corner())
        def _():
            for step in range(1, 8):
                self.vectors_plane(step).wait_send()

        for plane in range(PLANES):
            for part in range(PAIRS if plane == 0 else 1):

                @pl.when(self.z == plane)
                def _():
                    for step in (1, 2, 3):
                        self.gather_line(plane, part, step).wait_send()

                for step in (1, 2, 3):
                    self.gather_flat(plane, part, step).wait_send()
                self.gather_core(plane, part, self.c).wait_send()


    def sum_core(self, plane, part, y):
        row = pl.multiple_of(STEP * (8 * plane + 4 * y + 2 * (1 - self.c)), 16)
        blocks = self.parts(plane, part)
        return self.copy(
            self.grads.at[blocks, pl.ds(row, TWO)],
            self.core_land.at[plane, y, blocks],
            self.sum_core_send.at[plane, part, y],
            self.sum_core_recv.at[plane, part, y],
            self.core_peer(),
        )

    def sum_flat(self, plane, part, step):
        y, x = (self.y + step // 2) % 2, (self.x + step % 2) % 2
        blocks = self.parts(plane, part)
        return self.copy(
            self.chip_sum.at[plane, 2 * y + x, blocks],
            self.flat_land.at[plane, step - 1, blocks],
            self.sum_flat_send.at[plane, part, step - 1],
            self.sum_flat_recv.at[plane, part, step - 1],
            self.flat_peer(step),
        )

    def sum_line(self, plane, part, slot):
        blocks = self.parts(plane, part)
        return self.copy(
            self.plane_sum.at[plane, blocks],
            self.line_land.at[slot, blocks],
            self.sum_line_send.at[plane, part],
            self.sum_line_recv.at[plane, part, slot],
            self.device(plane, self.y, self.c, self.x),
        )

    def reduce_core(self, plane, part=0):
        for y in (0, 1):
            self.sum_core(plane, part, y).start()

    def reduce_flat(self, plane, part=0):
        for y in (0, 1):
            self.sum_core(plane, part, y).wait_recv()
            for block in [part] if plane == 0 else range(PAIRS):
                for x in (0, 1):
                    row = pl.multiple_of(STEP * (8 * plane + 4 * y + 2 * self.c + x), 16)
                    own = self.grads[block, pl.ds(row, FRAME), :].astype(F32)
                    other = self.core_land[plane, y, block, x * STEP : x * STEP + FRAME, :].astype(F32)
                    self.chip_sum[plane, 2 * y + x, block] = (own + other).astype(BF)
        for step in (3, 2, 1):
            self.sum_flat(plane, part, step).start()

    def reduce_line(self, plane, part=0):
        for step in (1, 2, 3):
            self.sum_flat(plane, part, step).wait_recv()
        for block in [part] if plane == 0 else range(PAIRS):
            total = self.chip_sum[plane, self.spot, block].astype(F32)
            for step in (1, 2, 3):
                total = total + self.flat_land[plane, step - 1, block].astype(F32)
            self.plane_sum[plane, block] = total.astype(BF)

            @pl.when(self.z == plane)
            def _():
                self.total[block] = total

        @pl.when(self.z != plane)
        def _():
            self.sum_line(plane, part, (self.z - plane + 2 * PLANES - 1) % PLANES).start()

    def vector_core(self):
        peer = self.core_peer()
        return self.copy(self.grad_vecs, self.vec_core, self.vec_send.at[0], self.vec_recv.at[0], peer)

    def vector_flat(self, slot):
        peer = self.device(self.z, 1, 1, 1)
        return self.copy(self.vec_sum, self.vec_flat.at[slot], self.vec_send.at[1], self.vec_recv.at[1 + slot], peer)

    def vector_line(self, slot):
        peer = self.device(PLANES - 1, 1, 1, 1)
        return self.copy(self.vec_sum, self.vec_line.at[slot], self.vec_send.at[2], self.vec_recv.at[4 + slot], peer)

    def reduce_vectors_core(self):
        @pl.when(self.c == 0)
        def _():
            self.vector_core().start()

    def reduce_vectors_flat(self):
        @pl.when(self.c == 1)
        def _():
            self.vector_core().wait_recv()
            self.vec_sum[...] = self.grad_vecs[...] + self.vec_core[...]

            @pl.when(self.spot != 3)
            def _():
                self.vector_flat(2 - self.spot).start()

    def reduce_vectors_line(self):
        @pl.when((self.c == 1) & (self.spot == 3))
        def _():
            for slot in range(3):
                self.vector_flat(slot).wait_recv()
            self.vec_sum[...] = self.vec_sum[...] + self.vec_flat[0] + self.vec_flat[1] + self.vec_flat[2]

            @pl.when(self.z != PLANES - 1)
            def _():
                self.vector_line(self.z).start()

    def finish_vectors(self):
        corner = (self.c == 1) & (self.spot == 3)

        @pl.when(corner & (self.z == PLANES - 1))
        def _():
            total = self.vec_sum[...]
            for slot in range(3):
                self.vector_line(slot).wait_recv()
                total = total + self.vec_line[slot]
            for block in range(PAIRS):
                self.total[block, STEP:, :] = total[:, block * 128 : block * 128 + 128]

        @pl.when(self.c == 0)
        def _():
            self.vector_core().wait_send()

        @pl.when((self.c == 1) & (self.spot != 3))
        def _():
            self.vector_flat(0).wait_send()

        @pl.when(corner & (self.z != PLANES - 1))
        def _():
            self.vector_line(0).wait_send()

    def finish_sum(self):
        for plane in range(PLANES):

            @pl.when(self.z == plane)
            def _():
                for part in range(PAIRS if plane == 0 else 1):
                    for slot in range(3):
                        self.sum_line(plane, part, slot).wait_recv()
                        blocks = self.parts(plane, part)
                        self.total[blocks] += self.line_land[slot, blocks].astype(F32)

            for part in range(PAIRS if plane == 0 else 1):

                @pl.when(self.z != plane)
                def _():
                    self.sum_line(plane, part, 0).wait_send()

                for step in (1, 2, 3):
                    self.sum_flat(plane, part, step).wait_send()
                for y in (0, 1):
                    self.sum_core(plane, part, y).wait_send()

    def unframe(self):
        rows = self.own_grad.shape[0]
        up, across = self.offsets()
        gap = iota((rows, FRAME), 0) + up - 3 * iota((rows, FRAME), 1)
        same = jnp.zeros((rows, 256), F32)
        carried = jnp.zeros((rows, 256), F32)
        for block in range(PAIRS):
            total = self.total[block]
            high = total.astype(BF)
            both = jnp.concatenate([high, (total - high.astype(F32)).astype(BF)], axis=1)
            same = same + dot(jnp.where(gap == block, 1.0, 0.0).astype(BF), both)
            carried = carried + dot(jnp.where(gap == block - 1, 1.0, 0.0).astype(BF), both)
        same = same[:, :128] + same[:, 128:]
        carried = carried[:, :128] + carried[:, 128:]
        mixed = jnp.where(iota((rows, 128), 1) >= across, same, carried)
        self.own_grad[...] = pltpu.roll(mixed, (128 - across) % 128, 1)


def exchange_refs():
    vmem, dma = pltpu.VMEM, pltpu.SemaphoreType.DMA
    return {
        "grads": vmem((PAIRS, ALL_ROWS, 128), BF),
        "grad_vecs": vmem((16, D), F32),
        "land": vmem((PLANES, PAIRS, 2, 4, FRAME, 128), BF),
        "core_land": vmem((PLANES, 2, PAIRS, TWO, 128), BF),
        "chip_sum": vmem((PLANES, 4, PAIRS, FRAME, 128), BF),
        "flat_land": vmem((PLANES, 3, PAIRS, FRAME, 128), BF),
        "plane_sum": vmem((PLANES, PAIRS, FRAME, 128), BF),
        "line_land": vmem((3, PAIRS, FRAME, 128), BF),
        "total": vmem((PAIRS, FRAME, 128), F32),
        "vec_par": vmem((PAIRS, 16, 128), BF),
        "vec_core": vmem((16, D), F32),
        "vec_sum": vmem((16, D), F32),
        "vec_flat": vmem((3, 16, D), F32),
        "vec_line": vmem((3, 16, D), F32),
        "line_send": dma((PLANES, PAIRS, 3)),
        "line_recv": dma((PLANES, PAIRS)),
        "flat_send": dma((PLANES, PAIRS, 3)),
        "flat_recv": dma((PLANES, PAIRS, 3)),
        "core_send": dma((PLANES, PAIRS)),
        "core_recv": dma((PLANES, PAIRS)),
        "sum_core_send": dma((PLANES, PAIRS, 2)),
        "sum_core_recv": dma((PLANES, PAIRS, 2)),
        "sum_flat_send": dma((PLANES, PAIRS, 3)),
        "sum_flat_recv": dma((PLANES, PAIRS, 3)),
        "sum_line_send": dma((PLANES, PAIRS)),
        "sum_line_recv": dma((PLANES, PAIRS, 3)),
        "par_send": dma((10,)),
        "par_recv": dma((2,)),
        "vec_send": dma((3,)),
        "vec_recv": dma((7,)),
    }


def at_head(odd, value, action):
    @pl.when(odd == value)
    def _():
        action()


def whole_kernel(names, *refs):
    refs = dict(zip(names, refs))
    refs["flat"] = refs["grads"]
    layer, swap = Layer(refs), Exchange(refs)
    swap.greet()
    swap.frame_own()
    layer.start()
    swap.greeted()
    swap.send_vectors_line()
    for part in range(PAIRS):
        swap.send_line(0, part)
    swap.send_flat(0, 0)
    swap.send_vectors_plane()
    swap.send_flat(0, 1)
    swap.send_core(0, 0)
    swap.send_flat(0, 2)
    for plane in (1, 2, 3):
        swap.send_line(plane, 0)
    swap.finish_vectors_plane()
    layer.load_vectors()
    swap.finish_gather(0, 0)

    def after_first(odd):
        at_head(odd, 0, lambda: swap.send_core(0, 1))
        at_head(odd, 1, lambda: swap.send_core(0, 2))

    def after_second(odd):
        at_head(odd, 0, lambda: swap.send_flat(1, 0))
        at_head(odd, 1, lambda: swap.send_flat(2, 0))

    def after_third(odd):
        at_head(odd, 0, lambda: swap.send_core(1, 0))
        at_head(odd, 1, lambda: swap.send_flat(3, 0))

    for pair, hook in enumerate((after_first, after_second, after_third)):
        if pair:
            swap.finish_gather(0, pair)
        layer.query_key_value(pair)

        @pl.loop(0, 2)
        def _(odd):
            layer.attend_forward(2 * pair + odd)
            hook(odd)

    swap.finish_gather(1, 0)
    swap.send_core(2, 0)
    swap.send_core(3, 0)
    swap.finish_gather(2, 0)
    swap.finish_gather(3, 0)
    layer.after_attention()
    layer.up_weights()
    layer.feed_forward()
    layer.down_weights()
    layer.finish_forward()
    layer.down_grad()
    for block in range(PAIRS):
        layer.grads[block, ROW_VEC:, :] = jnp.zeros((ALL_ROWS - ROW_VEC, 128), BF)
    swap.reduce_core(3)
    layer.hidden_grad()
    swap.reduce_flat(3)
    layer.up_grad()
    swap.reduce_core(2)
    layer.out_grad()
    swap.reduce_core(1)
    swap.reduce_flat(2)

    def back_first(odd):
        def first():
            swap.reduce_line(3)
            swap.reduce_flat(1)

        at_head(odd, 0, first)
        at_head(odd, 1, lambda: swap.reduce_line(2))

    def back_second(odd):
        at_head(odd, 0, lambda: swap.reduce_flat(0, 0))

        def second():
            swap.reduce_line(1)
            swap.reduce_line(0, 0)

        at_head(odd, 1, second)

    def back_third(odd):
        at_head(odd, 0, lambda: swap.reduce_flat(0, 1))
        at_head(odd, 1, lambda: swap.reduce_line(0, 1))

    for pair, hook in enumerate((back_first, back_second, back_third)):
        layer.pair_backward(pair, hook)
        swap.reduce_core(0, pair)
    layer.vector_grads()
    swap.reduce_vectors_core()
    swap.reduce_flat(0, 2)
    swap.reduce_vectors_flat()
    layer.input_grad_step()
    swap.reduce_line(0, 2)
    swap.reduce_vectors_line()
    swap.drain_gather()
    swap.finish_sum()
    swap.finish_vectors()
    swap.unframe()


def whole_layer(tokens, cotangent, own_params, subnets, lengths):
    rows = tokens.shape[0]
    scratch = scratch_refs(-(-LIVE // BLOCK) * BLOCK) | exchange_refs()
    inputs = ["tokens", "cotangent", "own_params", "subnets", "lengths"]
    outputs = ["layer_out", "input_grad", "own_grad"]
    spaces = [pltpu.VMEM] * 3 + [pltpu.SMEM] * 2
    return pl.pallas_call(
        functools.partial(whole_kernel, inputs + outputs + list(scratch)),
        out_shape=(
            jax.ShapeDtypeStruct((rows, D), BF),
            jax.ShapeDtypeStruct((rows, D), F32),
            jax.ShapeDtypeStruct(own_params.shape, F32),
        ),
        in_specs=[pl.BlockSpec(memory_space=space) for space in spaces],
        out_specs=[pl.BlockSpec(memory_space=pltpu.VMEM)] * 3,
        scratch_shapes=list(scratch.values()),
        compiler_params=pltpu.CompilerParams(
            vmem_limit_bytes=60 * 2**20, collective_id=0, has_side_effects=True
        ),
    )(tokens, cotangent, own_params, subnets, lengths)


def local_kernel(names, *refs):
    refs = dict(zip(names, refs))
    refs["vec_par"] = refs["flat"].at[:, ROW_VEC:, :]
    layer = Layer(refs)
    layer.start()
    layer.load_vectors()
    for pair in range(PAIRS):
        layer.query_key_value(pair)

        @pl.loop(0, 2)
        def _(odd):
            layer.attend_forward(2 * pair + odd)

    layer.after_attention()
    layer.up_weights()
    layer.feed_forward()
    layer.down_weights()
    layer.finish_forward()
    layer.down_grad()
    layer.hidden_grad()
    layer.up_grad()
    layer.out_grad()
    for pair in range(PAIRS):
        layer.pair_backward(pair, lambda odd: None)
    layer.input_grad_step()
    layer.vector_grads()
    for block in range(PAIRS):
        layer.grads[block, ROW_VEC:, :] = layer.grad_vecs[:, block * 128 : block * 128 + 128].astype(BF)


def local_layer(tokens, cotangent, flat, subnets, lengths):
    rows = tokens.shape[0]
    lanes = -(-LIVE // BLOCK) * BLOCK
    scratch = scratch_refs(lanes)
    inputs = ["tokens", "cotangent", "flat", "subnets", "lengths"]
    outputs = ["layer_out", "input_grad", "grads", "grad_vecs"]
    spaces = [pltpu.VMEM] * 3 + [pltpu.SMEM] * 2
    return pl.pallas_call(
        functools.partial(local_kernel, inputs + outputs + list(scratch)),
        out_shape=(
            jax.ShapeDtypeStruct((rows, D), BF),
            jax.ShapeDtypeStruct((rows, D), F32),
            jax.ShapeDtypeStruct((PAIRS, ALL_ROWS, 128), BF),
            jax.ShapeDtypeStruct((16, D), F32),
        ),
        in_specs=[pl.BlockSpec(memory_space=space) for space in spaces],
        out_specs=[pl.BlockSpec(memory_space=pltpu.VMEM)] * 4,
        scratch_shapes=list(scratch.values()),
        compiler_params=pltpu.CompilerParams(vmem_limit_bytes=60 * 2**20),
    )(tokens, cotangent, flat, subnets, lengths)


def on_device(tokens, cotangent, params, subnets, lengths):
    flat = lax.all_gather(params, ("group", "item"), axis=0, tiled=True)
    flat = flat.reshape(-1, D)
    whole = flat.shape[0]
    flat = jnp.pad(flat, ((0, ALL_ROWS - whole), (0, 0)))
    flat = jnp.swapaxes(flat.reshape(ALL_ROWS, PAIRS, 128), 0, 1)
    layer_out, input_grad, grads, _ = local_layer(tokens[0], cotangent[0], flat, subnets, lengths[0])
    grad = jnp.swapaxes(grads[:, :whole], 0, 1).astype(F32).reshape(-1)
    param_grad = lax.psum_scatter(grad, ("group", "item"), scatter_dimension=0, tiled=True)
    return layer_out[None], input_grad[None], param_grad


def on_known_device(tokens, cotangent, params, subnets, lengths):
    count = params.shape[0]
    rows = -(-count // 1024) * 8
    own = jnp.pad(params, (0, rows * 128 - count)).reshape(rows, 128)
    layer_out, input_grad, own_grad = whole_layer(tokens[0], cotangent[0], own, subnets, lengths[0])
    return layer_out[None], input_grad[None], own_grad.reshape(-1)[:count]


def solution(mesh):
    in_specs = (
        P("group", "item", None),
        P("group", "item", None),
        P(("group", "item")),
        P("group", None),
        P("group", "item", None),
    )
    out_specs = (P("group", "item", None), P("group", "item", None), P(("group", "item")))
    known = mesh.shape["group"] == 16 and mesh.shape["item"] == 2
    return jax.shard_map(
        on_known_device if known else on_device, mesh=mesh, in_specs=in_specs, out_specs=out_specs, check_vma=False
    )
```

```python
import functools

import jax
import jax.numpy as jnp
from jax import lax
from jax.experimental import pallas as pl
from jax.experimental.pallas import tpu as pltpu
from jax.sharding import PartitionSpec as P

HD = 64
HEADS = 6
D = 384
FF = 1536
LIVE = 960
PAIRS = HEADS // 2
CHUNKS = FF // D
BLOCK = 256
TILE = 192
BIG = 1e30
BF = jnp.bfloat16
F32 = jnp.float32
ROW_Q, ROW_K, ROW_V, ROW_O, ROW_UP, ROW_DOWN, ROW_VEC = 0, 384, 768, 1152, 1536, 3072, 4608
ALL_ROWS = 4624
STEP, FRAME, TWO, HALF = 144, 160, 304, 80
PLANES = 4
MESH = pl.DeviceIdType.MESH
VMEM_LIMIT = 62 * 2**20


def dot(left, right):
    return jnp.dot(left, right, preferred_element_type=F32)


def dot_nt(left, right):
    return lax.dot_general(left, right, (((1,), (1,)), ((), ())), preferred_element_type=F32)


def dot_tn(left, right):
    return lax.dot_general(left, right, (((0,), (0,)), ((), ())), preferred_element_type=F32)


def iota(shape, axis):
    return lax.broadcasted_iota(jnp.int32, shape, axis)


def below(shape, axis, bound):
    return jnp.where(iota(shape, axis) < bound, 1.0, 0.0).astype(F32)


def key_range(block):
    first = max(0, block * BLOCK - 479) // 32 * 32
    last = min(LIVE, -(-(block * BLOCK + BLOCK + 479) // 32) * 32)
    return first, last


def gelu_parts(z):
    cdf = 0.5 + 0.5 * lax.erf(z * 0.7071067811865476)
    bell = jnp.exp(-0.5 * (z * z)) * 0.3989422804014327
    return z * cdf, cdf + z * bell


def norm_forward(hidden, gain, shift, feature, inv_count):
    center = (hidden - jnp.sum(hidden * feature, axis=-1, keepdims=True) * inv_count) * feature
    inverse = lax.rsqrt(jnp.sum(center * center, axis=-1, keepdims=True) * inv_count + 1e-05)
    normed = center * inverse
    return normed * gain + shift, normed, inverse


def norm_backward(grad, normed, inverse, gain, feature, inv_count):
    scaled = grad * gain
    first = jnp.sum(scaled, axis=-1, keepdims=True) * inv_count
    second = jnp.sum(scaled * normed, axis=-1, keepdims=True) * inv_count
    return inverse * (scaled - first - normed * second) * feature


def col_sum(value):
    return jnp.sum(value, axis=0, keepdims=True)


class Layer:
    def __init__(self, refs):
        self.__dict__.update(refs)
        self.d_a, self.dot_t = self.xm, self.v_t
        for index, name in enumerate(("norm_one", "normed_one", "grad_second")):
            setattr(self, name, self.hold.at[:, index * D : index * D + D])
        self.lanes = self.expo.shape[2]
        width, heads, hidden = self.subnets[0, 0], self.subnets[0, 1], self.subnets[0, 2]
        self.width, self.attend, self.hidden = width, heads * HD, hidden
        self.inv_count = 1.0 / jnp.full((1, 1), width, jnp.int32).astype(F32)

    def row_mask(self, cols, bound, offset=0):
        return jnp.where(iota((1, cols), 1) + offset < bound, 1.0, 0.0).astype(F32)

    def col_mask(self, rows, bound, offset=0):
        return jnp.where(iota((rows, 1), 0) + offset < bound, 1.0, 0.0).astype(F32)

    def feature(self):
        return self.row_mask(D, self.width)

    def vector(self, index):
        mask = self.attend if index < 2 else self.width
        return self.vecs[4 + index : 5 + index, :] * self.row_mask(D, mask)

    def add_sum(self, index, value, first):
        part = value[:8, :]
        for start in range(8, value.shape[0], 8):
            part = part + value[start : start + 8, :]
        if first:
            self.sums[index] = part
        else:
            self.sums[index] += part


    def tokens_copy(self):
        return pltpu.make_async_copy(self.tokens.at[pl.ds(0, LIVE)], self.xm, self.io_sem.at[0])

    def cotangent_copy(self):
        return pltpu.make_async_copy(self.cotangent.at[pl.ds(0, LIVE)], self.cot, self.io_sem.at[1])

    def layer_out_copy(self):
        return pltpu.make_async_copy(self.cot, self.layer_out.at[pl.ds(0, LIVE)], self.io_sem.at[2])

    def layer_rest_copy(self):
        rest = self.layer_out.shape[0] - LIVE
        return pltpu.make_async_copy(self.none, self.layer_out.at[pl.ds(LIVE, rest)], self.io_sem.at[5])

    def input_grad_copy(self, start, size):
        rows = pl.ds(start, size)
        return pltpu.make_async_copy(self.normed_one.at[rows], self.input_grad.at[rows], self.io_sem.at[3])

    def input_rest_copy(self):
        rest = self.input_grad.shape[0] - LIVE
        return pltpu.make_async_copy(self.nothing, self.input_grad.at[pl.ds(LIVE, rest)], self.io_sem.at[4])

    def load(self):
        self.tokens_copy().start()
        self.cotangent_copy().start()

    def start(self):
        pad = self.lanes - LIVE
        self.nothing[...] = jnp.zeros(self.nothing.shape, F32)
        self.input_rest_copy().start()
        self.none[...] = jnp.zeros(self.none.shape, BF)
        self.layer_rest_copy().start()
        self.dot_t[:, :, LIVE:] = jnp.zeros((HEADS, HD, pad), BF)
        self.q_t[:, :, LIVE:] = jnp.zeros((HEADS, HD, pad), BF)
        self.delta[:, :, LIVE:] = jnp.zeros((HEADS, 1, pad), F32)
        self.do_s[LIVE:, :] = jnp.zeros((pad, D), BF)
        self.q_rows[LIVE:, :] = jnp.zeros((pad, D), BF)
        ends = []
        total = 0
        for index in range(4):
            total = total + self.lengths[0, index]
            ends.append(total)
        lane = iota((HD, self.lanes), 1)
        seg = sum((lane >= end).astype(jnp.int32) for end in ends)
        part = iota((HD, self.lanes), 0)
        self.far[...] = jnp.where((part < 4) & (part != seg), -BIG, 0.0).astype(BF)
        row = iota((LIVE, 128), 0)
        seg = sum((row >= end).astype(jnp.int32) for end in ends[:3])
        self.hot[...] = jnp.where(iota((LIVE, 128), 1) - HD == seg, 1.0, 0.0).astype(BF)
        fe = self.feature().astype(BF)
        self.tokens_copy().wait()
        for rows in row_tiles():
            self.xm[rows, :] = self.xm[rows, :] * fe
        for part in range(PAIRS):
            lanes = slice(part * 128, part * 128 + 128)
            self.xt[lanes, :] = self.xm[:, lanes].T

    def load_vectors(self):
        for part in range(PAIRS):
            lanes = slice(part * 128, part * 128 + 128)
            self.vecs[:, lanes] = self.vec_par[part].astype(F32)


    def query_key_value(self, pair):
        lanes = slice(pair * 128, pair * 128 + 128)
        mask = self.col_mask(D, self.width) * self.row_mask(128, self.attend, pair * 128)
        for index, row in enumerate((ROW_Q, ROW_K, ROW_V)):
            weight = (self.flat[pair, row : row + D, :].astype(F32) * mask).astype(BF)
            self.w_qkv[:, pair * D + index * 128 : pair * D + index * 128 + 128] = weight
        bias_q, bias_v = self.vector(0)[:, lanes], self.vector(1)[:, lanes]
        weight = self.w_qkv[:, pair * D : pair * D + D]
        for start in range(0, LIVE, BLOCK):
            rows = slice(start, min(start + BLOCK, LIVE))
            size = rows.stop - rows.start
            even = iota((size, 128), 1) < HD
            out = dot(self.xm[rows, :], weight)
            q = (out[:, :128] + bias_q).astype(BF)
            self.q_rows[rows, lanes] = q
            k32 = out[:, 128:256]
            k = k32.astype(BF)
            hot = self.hot[rows, :]
            self.k_ext[2 * pair, rows, :] = jnp.where(even, k32, hot.astype(F32)).astype(BF)
            self.k_ext[2 * pair + 1, rows, :] = jnp.where(even, pltpu.roll(k32, HD, 1), hot.astype(F32)).astype(BF)
            v = (out[:, 256:] + bias_v).astype(BF)
            self.v_rows[rows, lanes] = v
            turned = (q * jnp.asarray(0.125, BF)).T
            self.q_t[2 * pair, :, rows] = turned[:HD, :]
            self.q_t[2 * pair + 1, :, rows] = turned[HD:, :]
            turned = k.T
            self.k_t[2 * pair, :, rows] = turned[:HD, :]
            self.k_t[2 * pair + 1, :, rows] = turned[HD:, :]
            turned = v.T
            self.v_t[2 * pair, :, rows] = turned[:HD, :]
            self.v_t[2 * pair + 1, :, rows] = turned[HD:, :]

    def score(self, head, block):
        cols = slice(block * BLOCK, block * BLOCK + BLOCK)
        first, last = key_range(block)
        right = jnp.concatenate([self.q_t[head, :, cols], self.far[:, cols]], axis=0)
        self.hold[first:last, cols] = dot(self.k_ext[head, first:last, :], right)

    def soft(self, head, block):
        cols = slice(block * BLOCK, block * BLOCK + BLOCK)
        first, last = key_range(block)
        scores = self.hold[first:last, cols]
        expo = jnp.exp(scores - jnp.max(scores, axis=0, keepdims=True))
        inv = 1.0 / jnp.sum(expo, axis=0, keepdims=True)
        expo = expo.astype(BF)
        self.expo[head, first:last, cols] = expo
        self.inv[head, :, cols] = inv
        return expo, inv

    def attend_first(self, head):
        for block in range(self.lanes // BLOCK):
            self.score(head, block)

    def attend_step(self, head, after):
        for block in range(self.lanes // BLOCK):
            cols = slice(block * BLOCK, block * BLOCK + BLOCK)
            first, last = key_range(block)
            expo, inv = self.soft(head, block)
            if after is not None:
                self.score(after, block)
            mixed = dot(self.v_t[head, :, first:last], expo) * inv
            self.o_t[head, :, cols] = mixed.astype(BF)

    def after_attention(self):
        mask = self.col_mask(D, self.attend) * self.feature()
        for part in range(PAIRS):
            lanes = slice(part * 128, part * 128 + 128)
            rows = self.flat[part, ROW_O : ROW_O + D, :].astype(F32)
            self.w_out[:, lanes] = (rows * mask[:, lanes]).astype(BF)
        fe, bias, gain, shift = self.feature(), self.vector(2), self.vector(3), self.vector(4)
        for start in range(0, LIVE, BLOCK):
            size = min(BLOCK, LIVE - start)
            rows = slice(start, start + size)
            mixed = self.o_t[:, :, start : start + BLOCK].reshape(D, BLOCK)
            attended = dot_tn(mixed, self.w_out[...])[:size, :]
            hidden = self.xm[rows, :].astype(F32) + attended + bias
            norm, normed, inverse = norm_forward(hidden, gain, shift, fe, self.inv_count)
            self.norm_one[rows, :] = norm
            self.normed_one[rows, :] = normed
            self.inverse_one[rows, :] = jnp.broadcast_to(inverse, (size, 128))
            self.norm_low[rows, :] = norm.astype(BF)

    def up_weights(self):
        for part in range(PAIRS):
            self.wide[part] = self.flat[part, ROW_UP : ROW_UP + FF, :].astype(F32)
        for chunk in range(CHUNKS):
            mask = self.col_mask(D, self.width) * self.row_mask(D, self.hidden, chunk * D)
            for part in range(PAIRS):
                lanes = slice(part * 128, part * 128 + 128)
                piece = self.wide[part, pl.ds(chunk, D, stride=CHUNKS), :]
                self.w_up[:, chunk * D + part * 128 : chunk * D + part * 128 + 128] = (
                    piece * mask[:, lanes]
                ).astype(BF)

    def down_weights(self):
        mask = self.feature()
        for chunk in range(CHUNKS):
            rows = slice(chunk * D, chunk * D + D)
            hidden = self.col_mask(D, self.hidden, chunk * D)
            for part in range(PAIRS):
                lanes = slice(part * 128, part * 128 + 128)
                piece = self.flat[part, ROW_DOWN + chunk * D : ROW_DOWN + chunk * D + D, :].astype(F32)
                self.w_down[rows, lanes] = (piece * (hidden * mask[:, lanes])).astype(BF)

    def up_tile(self, rows):
        low = self.norm_low[rows, :]
        for chunk in range(CHUNKS):
            cols = slice(chunk * D, chunk * D + D)
            bias = self.vecs[chunk : chunk + 1, :] * self.row_mask(D, self.hidden, chunk * D)
            act, slope = gelu_parts(dot(low, self.w_up[:, cols]) + bias)
            self.act[rows, cols] = act.astype(BF)
            self.slope[rows, cols] = slope.astype(BF)

    def down_tile(self, rows):
        fe = self.feature()
        bias, gain, shift = self.vector(5), self.vector(6), self.vector(7)
        second = self.norm_one[rows, :] + dot(self.act[rows, :FF], self.w_down[...]) + bias
        result, normed, inverse = norm_forward(second, gain, shift, fe, self.inv_count)
        grad = self.cot[rows, :].astype(F32)
        self.cot[rows, :] = result.astype(BF)
        grad_second = norm_backward(grad, normed, inverse, gain, fe, self.inv_count)
        self.grad_second[rows, :] = grad_second
        low = grad_second.astype(BF)
        self.d_f[rows, :] = low
        first = rows.start == 0
        self.add_sum(10, grad * normed, first)
        self.add_sum(11, grad, first)
        self.add_sum(9, low.astype(F32), first)

    def feed_forward(self, before_down):
        tiles = row_tiles()
        self.up_tile(tiles[0])
        before_down()
        self.cotangent_copy().wait()
        for rows, after in zip(tiles, tiles[1:] + [None]):
            if after is not None:
                self.up_tile(after)
            self.down_tile(rows)
        self.layer_out_copy().start()


    def down_grad(self):
        fe = self.feature()
        for chunk in range(CHUNKS):
            cols = slice(chunk * D, chunk * D + D)
            mask = self.col_mask(D, self.hidden, chunk * D) * fe
            grad = (dot_tn(self.act[:, cols], self.d_f[...]) * mask).astype(BF)
            for part in range(PAIRS):
                lanes = slice(part * 128, part * 128 + 128)
                self.grads[part, ROW_DOWN + chunk * D : ROW_DOWN + chunk * D + D, :] = grad[:, lanes]

    def hidden_tile(self, rows):
        d_f = self.d_f[rows, :]
        for chunk in range(CHUNKS):
            cols = slice(chunk * D, chunk * D + D)
            grad = dot_nt(d_f, self.w_down[cols, :])
            dz = (grad * self.slope[rows, cols].astype(F32)).astype(BF)
            self.slope[rows, cols] = dz
            self.add_sum(chunk, dz.astype(F32), rows.start == 0)

    def first_norm_tile(self, rows):
        gain, fe = self.vector(3), self.feature()
        normed = self.normed_one[rows, :]
        grad = self.grad_second[rows, :] + dot_nt(self.slope[rows, :], self.w_up[...])
        grad_first = norm_backward(grad, normed, self.inverse_one[rows, :1], gain, fe, self.inv_count)
        self.norm_one[rows, :] = grad_first
        low = grad_first.astype(BF)
        self.d_a[rows, :] = low
        first = rows.start == 0
        self.add_sum(7, grad * normed, first)
        self.add_sum(8, grad, first)
        self.add_sum(6, low.astype(F32), first)

    def hidden_grad(self, hooks):
        tiles = row_tiles()
        self.hidden_tile(tiles[0])
        for index, rows in enumerate(tiles):
            if index + 1 < len(tiles):
                self.hidden_tile(tiles[index + 1])
            self.first_norm_tile(rows)
            if index in hooks:
                hooks[index]()

    def up_grad(self):
        for chunk in range(CHUNKS):
            cols = slice(chunk * D, chunk * D + D)
            mask = self.col_mask(D, self.width) * self.row_mask(D, self.hidden, chunk * D)
            grad = dot_tn(self.norm_low[...], self.slope[:, cols]) * mask
            for part in range(PAIRS):
                lanes = slice(part * 128, part * 128 + 128)
                self.wide[part, pl.ds(chunk, D, stride=CHUNKS), :] = grad[:, lanes]
        for part in range(PAIRS):
            self.grads[part, ROW_UP : ROW_UP + FF, :] = self.wide[part].astype(BF)

    def out_grad(self):
        fe = self.feature()
        d_a = self.d_a[...]
        half = D // 2
        for start in (0, half):
            rows = slice(start, start + half)
            heads = range(start // HD, (start + half) // HD)
            mask = self.col_mask(half, self.attend, start) * fe
            o_t = self.o_t[heads.start : heads.stop, :, :LIVE].reshape(half, LIVE)
            grad = (dot(o_t, d_a) * mask).astype(BF)
            for part in range(PAIRS):
                lanes = slice(part * 128, part * 128 + 128)
                self.grads[part, ROW_O + start : ROW_O + start + half, :] = grad[:, lanes]
            mixed = dot_nt(self.w_out[rows, :], d_a)
            for head in heads:
                own = mixed[head * HD - start : head * HD - start + HD, :] * self.inv[head, :, :LIVE]
                self.delta[head, :, :LIVE] = col_sum(own * self.o_t[head, :, :LIVE].astype(F32))
                self.dot_t[head, :, :LIVE] = own.astype(BF)
        for pair in range(PAIRS):
            both = self.dot_t[2 * pair : 2 * pair + 2, :, :LIVE].reshape(128, LIVE)
            self.do_s[:LIVE, pair * 128 : pair * 128 + 128] = both.T

    def score_place(self, odd, block):
        if not odd:
            return self.act, block * BLOCK
        return ((self.act, 4 * BLOCK), (self.act, 5 * BLOCK), (self.slope, PAIRS * D), (self.d_f, 0))[block]

    def prob_grad(self, pair, odd, block):
        cols = slice(block * BLOCK, block * BLOCK + BLOCK)
        first, last = key_range(block)
        right = self.dot_t[2 * pair + odd, :, cols]
        none = jnp.zeros_like(right)
        right = jnp.concatenate([none, right] if odd else [right, none], axis=0)
        return dot(self.v_rows[first:last, pair * 128 : pair * 128 + 128], right)

    def score_grad(self, pair, odd, block, grad):
        head = 2 * pair + odd
        cols = slice(block * BLOCK, block * BLOCK + BLOCK)
        first, last = key_range(block)
        grad = self.expo[head, first:last, cols].astype(F32) * (grad - self.delta[head, :, cols])
        grad = grad.astype(BF)
        place, start = self.score_place(odd, block)
        place[first:last, start : start + BLOCK] = grad
        return grad

    def query_grad(self, pair, odd, block, grad):
        head = 2 * pair + odd
        cols = slice(block * BLOCK, block * BLOCK + BLOCK)
        first, last = key_range(block)
        dq = dot(self.k_t[head, :, first:last], grad) * 0.125
        self.dq_t[odd * HD : odd * HD + HD, cols] = dq.astype(BF)

    def pair_backward(self, pair, middle):
        lanes = slice(pair * 128, pair * 128 + 128)
        blocks = self.lanes // BLOCK
        ranges = [key_range(block) for block in range(blocks)]
        edges = sorted({edge for both in ranges for edge in both})
        cuts = []
        for low, high in zip(edges[:-1], edges[1:]):
            used = [b for b in range(blocks) if ranges[b][0] <= low and high <= ranges[b][1]]
            cuts.append((slice(low, high), slice(used[0] * BLOCK, used[-1] * BLOCK + BLOCK)))
        own = [jnp.where((iota((1, 128), 1) >= HD) == bool(odd), 1.0, 0.0).astype(BF) for odd in (0, 1)]
        d_out = [self.do_s[:, lanes] * own[odd] for odd in (0, 1)]
        items = [(odd, block) for odd in (0, 1) for block in range(blocks)]
        grad = self.prob_grad(pair, *items[0])
        for index, (odd, block) in enumerate(items):
            if index % 2 == 0 and index // 2 < len(cuts):
                rows, span = cuts[index // 2]
                dv = sum(dot(self.expo[2 * pair + odd_, rows, span], d_out[odd_][span]) for odd_ in (0, 1))
                self.slope[rows, pair * D + 256 : pair * D + 384] = dv.astype(BF)
            after = self.prob_grad(pair, *items[index + 1]) if index + 1 < len(items) else None
            low = self.score_grad(pair, odd, block, grad)
            grad = after
            self.query_grad(pair, odd, block, low)
            if index == blocks - 1:
                middle()
        queries = [self.q_rows[:, lanes] * own[odd] for odd in (0, 1)]
        for rows, span in cuts:
            dk = 0.0
            for odd in (0, 1):
                places = [self.score_place(odd, block) for block in range(span.start // BLOCK, span.stop // BLOCK)]
                first = 0
                for last in range(1, len(places) + 1):
                    if last == len(places) or places[last][0] is not places[first][0]:
                        place, start = places[first]
                        begin, size = span.start + first * BLOCK, (last - first) * BLOCK
                        dk = dk + dot(place[rows, start : start + size], queries[odd][begin : begin + size])
                        first = last
            self.slope[rows, pair * D + 128 : pair * D + 256] = (dk * 0.125).astype(BF)
        self.slope[:, pair * D : pair * D + 128] = self.dq_t[:, :LIVE].T
        mask = self.col_mask(D, self.width) * self.row_mask(128, self.attend, pair * 128)
        all_three = self.slope[:, pair * D : pair * D + D]
        grad = dot(self.xt[...], all_three)
        for index, row in enumerate((ROW_Q, ROW_K, ROW_V)):
            self.grads[pair, row : row + D, :] = (grad[:, index * 128 : index * 128 + 128] * mask).astype(BF)
        totals = dot(jnp.ones((8, LIVE), BF), all_three)
        self.sums[4, :, lanes] = totals[:, :128] * 0.125
        self.sums[5, :, lanes] = totals[:, 256:] * 0.125

    def input_grad_step(self, hooks):
        fe = self.feature()
        for index, rows in enumerate(row_tiles()):
            total = self.norm_one[rows, :] + dot_nt(self.slope[rows, : PAIRS * D], self.w_qkv[...])
            self.normed_one[rows, :] = total * fe
            self.input_grad_copy(rows.start, rows.stop - rows.start).start()
            if index in hooks:
                hooks[index]()

    def finish(self):
        self.input_grad_copy(0, LIVE).wait()
        self.input_rest_copy().wait()
        self.layer_out_copy().wait()
        self.layer_rest_copy().wait()

    def vector_grads(self):
        for index in range(12):
            total = jnp.sum(self.sums[index], axis=0, keepdims=True)
            if index < CHUNKS:
                mask = self.row_mask(D, self.hidden, index * D)
            else:
                mask = self.row_mask(D, self.attend if index < 6 else self.width)
            self.grad_vecs[index : index + 1, :] = total * mask
        self.grad_vecs[12:, :] = jnp.zeros((4, D), F32)


def row_tiles():
    return [slice(start, min(start + TILE, LIVE)) for start in range(0, LIVE, TILE)]


def scratch_refs(rows):
    vmem = pltpu.VMEM
    lanes = -(-LIVE // BLOCK) * BLOCK
    return {
        "xm": vmem((LIVE, D), BF),
        "cot": vmem((LIVE, D), BF),
        "none": vmem((rows - LIVE, D), BF),
        "nothing": vmem((rows - LIVE, D), F32),
        "hold": vmem((LIVE, 3 * D), F32),
        "xt": vmem((D, LIVE), BF),
        "hot": vmem((LIVE, 128), BF),
        "far": vmem((HD, lanes), BF),
        "vecs": vmem((16, D), F32),
        "sums": vmem((12, 8, D), F32),
        "w_qkv": vmem((D, PAIRS * D), BF),
        "w_out": vmem((D, D), BF),
        "w_up": vmem((D, FF), BF),
        "w_down": vmem((FF, D), BF),
        "wide": vmem((PAIRS, FF, 128), F32),
        "q_rows": vmem((lanes, D), BF),
        "q_t": vmem((HEADS, HD, lanes), BF),
        "k_t": vmem((HEADS, HD, LIVE), BF),
        "k_ext": vmem((HEADS, LIVE, 128), BF),
        "v_rows": vmem((LIVE, D), BF),
        "v_t": vmem((HEADS, HD, lanes), BF),
        "expo": vmem((HEADS, LIVE, lanes), BF),
        "inv": vmem((HEADS, 1, lanes), F32),
        "o_t": vmem((HEADS, HD, lanes), BF),
        "inverse_one": vmem((LIVE, 128), F32),
        "norm_low": vmem((LIVE, D), BF),
        "act": vmem((LIVE, FF), BF),
        "slope": vmem((LIVE, FF), BF),
        "d_f": vmem((LIVE, D), BF),
        "do_s": vmem((lanes, D), BF),
        "delta": vmem((HEADS, 1, lanes), F32),
        "dq_t": vmem((128, lanes), BF),
        "io_sem": pltpu.SemaphoreType.DMA((6,)),
    }


class Exchange:
    def __init__(self, refs):
        self.__dict__.update(refs)
        group, self.x = lax.axis_index("group"), lax.axis_index("item")
        self.z, self.y, self.c = group // 4, (group // 2) % 2, group % 2
        self.spot = 2 * self.y + self.x
        self.shard = 2 * group + self.x
        self.corner = (self.c == 1) & (self.spot == 3)

    def device(self, z, y, c, x):
        return (z * 4 + y * 2 + c, x)

    def line(self, step):
        return self.device((self.z + step) % PLANES, self.y, self.c, self.x)

    def plane_peer(self, step):
        y, x = (self.y + step // 4) % 2, (self.x + step % 2) % 2
        return self.device(self.z, y, (self.c + step // 2 % 2) % 2, x)

    def chip_peer(self, step):
        y, x = (self.y + step // 2) % 2, (self.x + step % 2) % 2
        return self.device(self.z, y, self.c, x)

    def spot_of(self, step):
        return 2 * ((self.y + step // 2) % 2) + (self.x + step % 2) % 2

    def core_peer(self):
        return self.device(self.z, self.y, 1 - self.c, self.x)

    def greet(self):
        barrier = pltpu.get_barrier_semaphore()
        peers = [self.line(step) for step in (1, 2, 3)] + [self.plane_peer(step) for step in range(1, 8)]
        for peer in peers:
            pl.semaphore_signal(barrier, inc=1, device_id=peer, device_id_type=MESH)

    def greeted(self):
        pl.semaphore_wait(pltpu.get_barrier_semaphore(), 10)

    def copy(self, source, target, send, recv, peer):
        return pltpu.make_async_remote_copy(
            src_ref=source, dst_ref=target, send_sem=send, recv_sem=recv, device_id=peer, device_id_type=MESH
        )


    def offsets(self):
        shift = STEP * self.shard
        return shift // 128, shift % 128

    def frame_own(self):
        rows = self.own_params.shape[0]
        up, across = self.offsets()
        turned = pltpu.roll(self.own_params[...].astype(F32), across, 1)
        late = iota((rows, 128), 1) >= across
        same = jnp.where(late, turned, 0.0).astype(BF)
        carried = jnp.where(late, 0.0, turned).astype(BF)
        gap = 3 * iota((FRAME, rows), 0) - up - iota((FRAME, rows), 1)
        for part in range(PAIRS):
            here = jnp.where(gap == -part, 1.0, 0.0).astype(BF)
            after = jnp.where(gap == 1 - part, 1.0, 0.0).astype(BF)
            frame = dot(here, same) + dot(after, carried)
            self.land[self.z, part, self.c, self.spot] = frame.astype(BF)

    def vectors_line(self, step):
        sems = self.par_send.at[step - 1], self.par_recv.at[0]
        return self.copy(self.vec_par, self.vec_par, *sems, self.line(step))

    def vectors_plane(self, step):
        sems = self.par_send.at[step + 2], self.par_recv.at[1]
        return self.copy(self.vec_par, self.vec_par, *sems, self.plane_peer(step))

    def send_vectors_line(self):
        @pl.when(self.corner & (self.z == PLANES - 1))
        def _():
            self.vec_par[...] = self.land[PLANES - 1, :, 1, 3, STEP:, :]
            for step in (1, 2, 3):
                self.vectors_line(step).start()

    def send_vectors_plane(self):
        @pl.when(self.corner & (self.z != PLANES - 1))
        def _():
            self.vectors_line(1).wait_recv()

        @pl.when(self.corner)
        def _():
            for step in range(1, 8):
                self.vectors_plane(step).start()

    def finish_vectors_plane(self):
        @pl.when(jnp.logical_not(self.corner))
        def _():
            self.vectors_plane(1).wait_recv()

    def parts(self, plane, part):
        return pl.ds(part, 1) if plane == 0 else slice(None)

    def blocks(self, plane, part):
        return [part] if plane == 0 else range(PAIRS)

    def item(self, plane, part):
        return part if plane == 0 else 2 + plane

    def gather_line(self, plane, part, step):
        piece = self.land.at[plane, self.parts(plane, part), self.c, self.spot]
        sems = self.line_send.at[part, step - 1], self.line_recv.at[self.item(plane, part)]
        return self.copy(piece, piece, *sems, self.line(step))

    def send_line(self, plane, part, steps):
        @pl.when(self.z == plane)
        def _():
            for step in steps:
                self.gather_line(plane, part, step).start()

    def gather_all(self, part, step, spot):
        piece = self.land.at[0, pl.ds(part, 1), self.c, spot]
        sems = self.flat_send.at[3 * part + step - 1], self.flat_recv.at[3 * part + step - 1]
        return self.copy(piece, piece, *sems, self.chip_peer(step))

    def gather_next(self, plane, step, spot):
        piece = self.land.at[plane, :, self.c, spot]
        index = 5 + 4 * plane + step - 1
        return self.copy(piece, piece, self.flat_send.at[index], self.flat_recv.at[index], self.chip_peer(step))

    def gather_half(self, plane, step, spot):
        rows = pl.ds((2 - step) * HALF, HALF)
        piece = self.land.at[plane, :, self.c, spot, rows]
        index = 5 + 4 * plane + step + 1
        return self.copy(piece, piece, self.flat_send.at[index], self.flat_recv.at[index], self.chip_peer(step))

    def wait_line(self, plane, part):
        @pl.when(self.z != plane)
        def _():
            self.gather_line(plane, part, 1).wait_recv()

    def send_all(self, part):
        self.wait_line(0, part)
        for step in (3, 2, 1):
            self.gather_all(part, step, self.spot).start()

    def send_next(self, plane):
        self.wait_line(plane, 0)
        for step in (2, 1):
            self.gather_next(plane, step, self.spot).start()

    def send_halves(self, plane):
        self.gather_next(plane, 1, self.spot_of(1)).wait_recv()
        self.gather_half(plane, 2, self.spot_of(1)).start()
        self.gather_next(plane, 2, self.spot_of(2)).wait_recv()
        self.gather_half(plane, 1, self.spot_of(2)).start()

    def gather_core(self, plane, part, core):
        piece = self.land.at[plane, self.parts(plane, part), core]
        item = self.item(plane, part)
        return self.copy(piece, piece, self.core_send.at[item], self.core_recv.at[item], self.core_peer())

    def send_core(self, plane, part=0):
        if plane == 0:
            for step in (3, 2, 1):
                self.gather_all(part, step, self.spot_of(step)).wait_recv()
        else:
            for step in (2, 1):
                self.gather_half(plane, step, self.spot_of(3)).wait_recv()
        self.gather_core(plane, part, self.c).start()

    def finish_gather(self, plane, part=0):
        self.gather_core(plane, part, 1 - self.c).wait_recv()
        for place in range(8):
            y, c, x = place // 4, (place // 2) % 2, place % 2
            chunk = 8 * plane + place
            for block in self.blocks(plane, part):
                frame = self.land[plane, block, c, 2 * y + x]
                self.flat[block, chunk * STEP : chunk * STEP + STEP, :] = frame[:STEP, :]
                if chunk:
                    before = (chunk - 1) % 8
                    spot = 2 * (before // 4) + before % 2
                    tail = self.land[(chunk - 1) // 8, block, (before // 2) % 2, spot, STEP:, :]
                    both = tail.astype(F32) + frame[: FRAME - STEP, :].astype(F32)
                    self.flat[block, chunk * STEP : chunk * STEP + FRAME - STEP, :] = both.astype(BF)

    def drain_gather(self):
        @pl.when(self.corner & (self.z == PLANES - 1))
        def _():
            for step in (1, 2, 3):
                self.vectors_line(step).wait_send()

        @pl.when(self.corner)
        def _():
            for step in range(1, 8):
                self.vectors_plane(step).wait_send()

        for plane in range(PLANES):
            for part in range(PAIRS if plane == 0 else 1):

                @pl.when(self.z == plane)
                def _():
                    for step in (1, 2, 3):
                        self.gather_line(plane, part, step).wait_send()

                if plane == 0:
                    for step in (1, 2, 3):
                        self.gather_all(part, step, self.spot).wait_send()
                else:
                    for step in (1, 2):
                        self.gather_next(plane, step, self.spot).wait_send()
                        self.gather_half(plane, step, self.spot).wait_send()
                self.gather_core(plane, part, self.c).wait_send()


    def sum_core(self, plane, part, y):
        row = pl.multiple_of(STEP * (8 * plane + 4 * y + 2 * (1 - self.c)), 16)
        parts, item = self.parts(plane, part), 2 * self.item(plane, part) + y
        return self.copy(
            self.grads.at[parts, pl.ds(row, TWO)],
            self.core_land.at[plane % 3, y, parts],
            self.sum_core_send.at[item],
            self.sum_core_recv.at[item],
            self.core_peer(),
        )

    def sum_all(self, part, step):
        index = 3 * part + step - 1
        return self.copy(
            self.land.at[0, pl.ds(part, 1), 0, self.spot_of(step)],
            self.all_land.at[step - 1, pl.ds(part, 1)],
            self.sum_flat_send.at[index],
            self.sum_flat_recv.at[index],
            self.chip_peer(step),
        )

    def sum_half(self, plane, step):
        index = 5 + 4 * plane + step - 1
        return self.copy(
            self.land.at[plane, :, 0, self.spot_of(3), pl.ds((step - 1) * HALF, HALF)],
            self.half_land.at[plane - 1, step - 1],
            self.sum_flat_send.at[index],
            self.sum_flat_recv.at[index],
            self.chip_peer(step),
        )

    def sum_next(self, plane, step):
        index = 5 + 4 * plane + step + 1
        return self.copy(
            self.land.at[plane, :, 0, self.spot_of(step)],
            self.next_land.at[plane - 1, step - 1],
            self.sum_flat_send.at[index],
            self.sum_flat_recv.at[index],
            self.chip_peer(step),
        )

    def sum_line(self, plane, part, slot):
        parts, item = self.parts(plane, part), self.item(plane, part)
        return self.copy(
            self.plane_sum.at[plane, parts],
            self.line_land.at[slot, parts],
            self.sum_line_send.at[item],
            self.sum_line_recv.at[3 * part + slot],
            self.device(plane, self.y, self.c, self.x),
        )

    def reduce_core(self, plane, part=0):
        for y in (0, 1):
            self.sum_core(plane, part, y).start()

    def add_core(self, plane, part):
        for y in (0, 1):
            self.sum_core(plane, part, y).wait_recv()
            for block in self.blocks(plane, part):
                for x in (0, 1):
                    row = pl.multiple_of(STEP * (8 * plane + 4 * y + 2 * self.c + x), 16)
                    own = self.grads[block, pl.ds(row, FRAME), :].astype(F32)
                    other = self.core_land[plane % 3, y, block, x * STEP : x * STEP + FRAME, :].astype(F32)
                    self.land[plane, block, 0, 2 * y + x] = (own + other).astype(BF)

    def reduce_all(self, part):
        self.add_core(0, part)
        for step in (3, 2, 1):
            self.sum_all(part, step).start()

    def reduce_halves(self, plane):
        self.add_core(plane, 0)
        for step in (1, 2):
            self.sum_half(plane, step).start()

    def reduce_next(self, plane):
        for step in (1, 2):
            self.sum_half(plane, step).wait_recv()
            rows = slice((step - 1) * HALF, step * HALF)
            spot = self.spot_of(3 - step)
            for block in range(PAIRS):
                own = self.land[plane, block, 0, spot, rows, :].astype(F32)
                both = own + self.half_land[plane - 1, step - 1, block].astype(F32)
                self.land[plane, block, 0, spot, rows, :] = both.astype(BF)
            self.sum_next(plane, 3 - step).start()

    def reduce_line(self, plane, part=0):
        if plane == 0:
            for step in (1, 2, 3):
                self.sum_all(part, step).wait_recv()
        else:
            for step in (1, 2):
                self.sum_next(plane, step).wait_recv()
        for block in self.blocks(plane, part):
            total = self.land[plane, block, 0, self.spot].astype(F32)
            if plane == 0:
                for step in (1, 2, 3):
                    total = total + self.all_land[step - 1, block].astype(F32)
            else:
                for step in (1, 2):
                    total = total + self.next_land[plane - 1, step - 1, block].astype(F32)
            self.plane_sum[plane, block] = total.astype(BF)

            @pl.when(self.z == plane)
            def _():
                self.total[block] = total

        @pl.when(self.z != plane)
        def _():
            self.sum_line(plane, part, (self.z - plane + 2 * PLANES - 1) % PLANES).start()

    def vector_core(self):
        peer = self.core_peer()
        return self.copy(self.grad_vecs, self.vec_core, self.vec_send.at[0], self.vec_recv.at[0], peer)

    def vector_flat(self, slot):
        peer = self.device(self.z, 1, 1, 1)
        return self.copy(self.vec_sum, self.vec_flat.at[slot], self.vec_send.at[1], self.vec_recv.at[1 + slot], peer)

    def vector_line(self, slot):
        peer = self.device(PLANES - 1, 1, 1, 1)
        return self.copy(self.vec_sum, self.vec_line.at[slot], self.vec_send.at[2], self.vec_recv.at[4 + slot], peer)

    def reduce_vectors_core(self):
        @pl.when(self.c == 0)
        def _():
            self.vector_core().start()

    def reduce_vectors_flat(self):
        @pl.when(self.c == 1)
        def _():
            self.vector_core().wait_recv()
            self.vec_sum[...] = self.grad_vecs[...] + self.vec_core[...]

            @pl.when(self.spot != 3)
            def _():
                self.vector_flat(2 - self.spot).start()

    def reduce_vectors_line(self):
        @pl.when(self.corner)
        def _():
            for slot in range(3):
                self.vector_flat(slot).wait_recv()
            self.vec_sum[...] = self.vec_sum[...] + self.vec_flat[0] + self.vec_flat[1] + self.vec_flat[2]

            @pl.when(self.z != PLANES - 1)
            def _():
                self.vector_line(self.z).start()

    def finish_vectors(self):
        @pl.when(self.corner & (self.z == PLANES - 1))
        def _():
            total = self.vec_sum[...]
            for slot in range(3):
                self.vector_line(slot).wait_recv()
                total = total + self.vec_line[slot]
            for block in range(PAIRS):
                self.total[block, STEP:, :] = total[:, block * 128 : block * 128 + 128]

        @pl.when(self.c == 0)
        def _():
            self.vector_core().wait_send()

        @pl.when((self.c == 1) & (self.spot != 3))
        def _():
            self.vector_flat(0).wait_send()

        @pl.when(self.corner & (self.z != PLANES - 1))
        def _():
            self.vector_line(0).wait_send()

    def finish_sum(self):
        for plane in range(PLANES):

            @pl.when(self.z == plane)
            def _():
                for part in range(PAIRS if plane == 0 else 1):
                    for slot in range(3):
                        self.sum_line(plane, part, slot).wait_recv()
                    for block in self.blocks(plane, part):
                        total = self.total[block]
                        for slot in range(3):
                            total = total + self.line_land[slot, block].astype(F32)
                        self.total[block] = total

    def drain_sum(self, plane, part=0):
        @pl.when(self.z != plane)
        def _():
            self.sum_line(plane, part, 0).wait_send()

        if plane == 0:
            for step in (1, 2, 3):
                self.sum_all(part, step).wait_send()
        else:
            for step in (1, 2):
                self.sum_half(plane, step).wait_send()
                self.sum_next(plane, step).wait_send()
        for y in (0, 1):
            self.sum_core(plane, part, y).wait_send()

    def unframe(self):
        rows = self.own_grad.shape[0]
        up, across = self.offsets()
        gap = iota((rows, FRAME), 0) + up - 3 * iota((rows, FRAME), 1)
        same = jnp.zeros((rows, 256), F32)
        carried = jnp.zeros((rows, 256), F32)
        for block in range(PAIRS):
            total = self.total[block]
            high = total.astype(BF)
            both = jnp.concatenate([high, (total - high.astype(F32)).astype(BF)], axis=1)
            same = same + dot(jnp.where(gap == block, 1.0, 0.0).astype(BF), both)
            carried = carried + dot(jnp.where(gap == block - 1, 1.0, 0.0).astype(BF), both)
        same = same[:, :128] + same[:, 128:]
        carried = carried[:, :128] + carried[:, 128:]
        mixed = jnp.where(iota((rows, 128), 1) >= across, same, carried)
        self.own_grad[...] = pltpu.roll(mixed, (128 - across) % 128, 1)


def exchange_refs():
    vmem, dma = pltpu.VMEM, pltpu.SemaphoreType.DMA
    return {
        "grads": vmem((PAIRS, ALL_ROWS, 128), BF),
        "grad_vecs": vmem((16, D), F32),
        "land": vmem((PLANES, PAIRS, 2, 4, FRAME, 128), BF),
        "core_land": vmem((3, 2, PAIRS, TWO, 128), BF),
        "all_land": vmem((3, PAIRS, FRAME, 128), BF),
        "half_land": vmem((PLANES - 1, 2, PAIRS, HALF, 128), BF),
        "next_land": vmem((PLANES - 1, 2, PAIRS, FRAME, 128), BF),
        "plane_sum": vmem((PLANES, PAIRS, FRAME, 128), BF),
        "line_land": vmem((3, PAIRS, FRAME, 128), BF),
        "total": vmem((PAIRS, FRAME, 128), F32),
        "vec_par": vmem((PAIRS, 16, 128), BF),
        "vec_core": vmem((16, D), F32),
        "vec_sum": vmem((16, D), F32),
        "vec_flat": vmem((3, 16, D), F32),
        "vec_line": vmem((3, 16, D), F32),
        "line_send": dma((PAIRS, 3)),
        "line_recv": dma((6,)),
        "flat_send": dma((21,)),
        "flat_recv": dma((21,)),
        "core_send": dma((6,)),
        "core_recv": dma((6,)),
        "sum_core_send": dma((12,)),
        "sum_core_recv": dma((12,)),
        "sum_flat_send": dma((21,)),
        "sum_flat_recv": dma((21,)),
        "sum_line_send": dma((6,)),
        "sum_line_recv": dma((9,)),
        "par_send": dma((10,)),
        "par_recv": dma((2,)),
        "vec_send": dma((3,)),
        "vec_recv": dma((7,)),
    }


def whole_kernel(names, *refs):
    refs = dict(zip(names, refs))
    refs["flat"] = refs["grads"]
    layer, swap = Layer(refs), Exchange(refs)
    layer.load()
    swap.greet()
    swap.frame_own()
    layer.start()
    swap.greeted()
    swap.send_vectors_line()
    for part in range(PAIRS):
        swap.send_line(0, part, (3, 2, 1))
    swap.send_line(3, 0, (3, 2, 1))
    swap.send_line(2, 0, (3, 2))
    swap.send_line(1, 0, (3,))
    swap.send_all(0)
    swap.send_vectors_plane()
    swap.send_all(1)
    swap.send_core(0, 0)
    swap.send_all(2)
    swap.send_line(1, 0, (2, 1))
    swap.send_line(2, 0, (1,))
    swap.finish_vectors_plane()
    layer.load_vectors()
    swap.finish_gather(0, 0)
    layer.query_key_value(0)
    layer.attend_first(0)
    swap.send_core(0, 1)
    swap.send_next(1)

    before = {
        1: [lambda: swap.finish_gather(0, 1), lambda: layer.query_key_value(1)],
        3: [lambda: swap.finish_gather(0, 2), lambda: layer.query_key_value(2)],
    }
    after = {
        0: [lambda: swap.send_core(0, 2)],
        1: [lambda: swap.send_next(2), lambda: swap.send_halves(1)],
        2: [lambda: swap.send_next(3)],
        3: [lambda: swap.send_core(1), lambda: swap.send_halves(2)],
        4: [lambda: swap.finish_gather(1), lambda: swap.send_halves(3)],
    }

    @pl.loop(0, HEADS - 1)
    def _(head):
        for table, step in ((before, None), (after, layer.attend_step)):
            if step is not None:
                step(head, head + 1)
            for index, actions in table.items():

                @pl.when(head == index)
                def _():
                    for action in actions:
                        action()

    layer.attend_step(HEADS - 1, None)
    swap.send_core(2)
    layer.after_attention()
    swap.finish_gather(2)
    swap.send_core(3)
    layer.up_weights()

    def before_down():
        swap.finish_gather(3)
        layer.down_weights()

    layer.feed_forward(before_down)
    layer.down_grad()
    for block in range(PAIRS):
        layer.grads[block, ROW_VEC:, :] = jnp.zeros((ALL_ROWS - ROW_VEC, 128), BF)
    swap.reduce_core(3)
    swap.drain_gather()
    layer.hidden_grad({2: lambda: swap.reduce_halves(3)})
    swap.reduce_next(3)
    layer.up_grad()
    swap.reduce_core(2)
    layer.out_grad()
    swap.reduce_core(1)
    swap.reduce_halves(2)
    swap.reduce_line(3)

    def first_middle():
        swap.reduce_halves(1)
        swap.reduce_next(2)

    layer.pair_backward(0, first_middle)
    swap.reduce_core(0, 0)
    swap.reduce_next(1)
    swap.reduce_line(2)

    def second_middle():
        swap.reduce_all(0)
        swap.reduce_line(1)

    layer.pair_backward(1, second_middle)
    swap.reduce_core(0, 1)
    swap.reduce_line(0, 0)
    layer.pair_backward(2, lambda: swap.reduce_all(1))
    swap.reduce_core(0, 2)
    layer.vector_grads()
    swap.reduce_vectors_core()
    swap.reduce_line(0, 1)

    def last_flat():
        swap.reduce_all(2)
        swap.reduce_vectors_flat()

    layer.input_grad_step({1: last_flat})
    swap.reduce_vectors_line()
    swap.reduce_line(0, 2)
    for plane in (1, 2, 3):
        swap.drain_sum(plane)
    for part in range(PAIRS):
        swap.drain_sum(0, part)
    layer.finish()
    swap.finish_sum()
    swap.finish_vectors()
    swap.unframe()


def whole_layer(tokens, cotangent, own_params, subnets, lengths):
    rows = tokens.shape[0]
    scratch = scratch_refs(rows) | exchange_refs()
    inputs = ["tokens", "cotangent", "own_params", "subnets", "lengths"]
    outputs = ["layer_out", "input_grad", "own_grad"]
    spaces = [pl.ANY] * 2 + [pltpu.VMEM] + [pltpu.SMEM] * 2
    return pl.pallas_call(
        functools.partial(whole_kernel, inputs + outputs + list(scratch)),
        out_shape=(
            jax.ShapeDtypeStruct((rows, D), BF),
            jax.ShapeDtypeStruct((rows, D), F32),
            jax.ShapeDtypeStruct(own_params.shape, F32),
        ),
        in_specs=[pl.BlockSpec(memory_space=space) for space in spaces],
        out_specs=[pl.BlockSpec(memory_space=space) for space in (pl.ANY, pl.ANY, pltpu.VMEM)],
        scratch_shapes=list(scratch.values()),
        compiler_params=pltpu.CompilerParams(
            vmem_limit_bytes=VMEM_LIMIT, collective_id=0, has_side_effects=True
        ),
    )(tokens, cotangent, own_params, subnets, lengths)


def local_kernel(names, *refs):
    refs = dict(zip(names, refs))
    refs["vec_par"] = refs["flat"].at[:, ROW_VEC:, :]
    layer = Layer(refs)
    layer.load()
    layer.start()
    layer.load_vectors()
    for pair in range(PAIRS):
        layer.query_key_value(pair)
    layer.attend_first(0)

    @pl.loop(0, HEADS - 1)
    def _(head):
        layer.attend_step(head, head + 1)

    layer.attend_step(HEADS - 1, None)
    layer.after_attention()
    layer.up_weights()
    layer.feed_forward(layer.down_weights)
    layer.down_grad()
    layer.hidden_grad({})
    layer.up_grad()
    layer.out_grad()
    for pair in range(PAIRS):
        layer.pair_backward(pair, lambda: None)
    layer.input_grad_step({})
    layer.vector_grads()
    for block in range(PAIRS):
        layer.grads[block, ROW_VEC:, :] = layer.grad_vecs[:, block * 128 : block * 128 + 128].astype(BF)
    layer.finish()


def local_layer(tokens, cotangent, flat, subnets, lengths):
    rows = tokens.shape[0]
    scratch = scratch_refs(rows) | {"grad_vecs": pltpu.VMEM((16, D), F32)}
    inputs = ["tokens", "cotangent", "flat", "subnets", "lengths"]
    outputs = ["layer_out", "input_grad", "grads"]
    spaces = [pl.ANY] * 2 + [pltpu.VMEM] + [pltpu.SMEM] * 2
    return pl.pallas_call(
        functools.partial(local_kernel, inputs + outputs + list(scratch)),
        out_shape=(
            jax.ShapeDtypeStruct((rows, D), BF),
            jax.ShapeDtypeStruct((rows, D), F32),
            jax.ShapeDtypeStruct((PAIRS, ALL_ROWS, 128), BF),
        ),
        in_specs=[pl.BlockSpec(memory_space=space) for space in spaces],
        out_specs=[pl.BlockSpec(memory_space=space) for space in (pl.ANY, pl.ANY, pltpu.VMEM)],
        scratch_shapes=list(scratch.values()),
        compiler_params=pltpu.CompilerParams(vmem_limit_bytes=VMEM_LIMIT),
    )(tokens, cotangent, flat, subnets, lengths)


def on_device(tokens, cotangent, params, subnets, lengths):
    flat = lax.all_gather(params, ("group", "item"), axis=0, tiled=True)
    flat = flat.reshape(-1, D)
    whole = flat.shape[0]
    flat = jnp.pad(flat, ((0, ALL_ROWS - whole), (0, 0)))
    flat = jnp.swapaxes(flat.reshape(ALL_ROWS, PAIRS, 128), 0, 1)
    layer_out, input_grad, grads = local_layer(tokens[0], cotangent[0], flat, subnets, lengths[0])
    grad = jnp.swapaxes(grads[:, :whole], 0, 1).astype(F32).reshape(-1)
    param_grad = lax.psum_scatter(grad, ("group", "item"), scatter_dimension=0, tiled=True)
    return layer_out[None], input_grad[None], param_grad


def on_known_device(tokens, cotangent, params, subnets, lengths):
    count = params.shape[0]
    rows = -(-count // 1024) * 8
    own = jnp.pad(params, (0, rows * 128 - count)).reshape(rows, 128)
    layer_out, input_grad, own_grad = whole_layer(tokens[0], cotangent[0], own, subnets, lengths[0])
    return layer_out[None], input_grad[None], own_grad.reshape(-1)[:count]


def solution(mesh):
    in_specs = (
        P("group", "item", None),
        P("group", "item", None),
        P(("group", "item")),
        P("group", None),
        P("group", "item", None),
    )
    out_specs = (P("group", "item", None), P("group", "item", None), P(("group", "item")))
    known = mesh.shape["group"] == 16 and mesh.shape["item"] == 2
    return jax.shard_map(
        on_known_device if known else on_device, mesh=mesh, in_specs=in_specs, out_specs=out_specs, check_vma=False
    )
```

```python
import functools

import jax
import jax.numpy as jnp
from jax import lax
from jax.experimental import pallas as pl
from jax.experimental.pallas import tpu as pltpu
from jax.sharding import PartitionSpec as P

HD = 64
HEADS = 6
D = 384
FF = 1536
LIVE = 960
PAIRS = HEADS // 2
CHUNKS = FF // D
BLOCK = 256
TILE = 192
BIG = 1e30
BF = jnp.bfloat16
F32 = jnp.float32
ROW_Q, ROW_K, ROW_V, ROW_O, ROW_UP, ROW_DOWN, ROW_VEC = 0, 384, 768, 1152, 1536, 3072, 4608
ALL_ROWS = 4624
STEP, FRAME, TWO, HALF = 144, 160, 304, 80
PLANES = 4
MESH = pl.DeviceIdType.MESH
VMEM_LIMIT = 62 * 2**20
EMIT = 4


def dot(left, right):
    return jnp.dot(left, right, preferred_element_type=F32)


def dot_nt(left, right):
    return lax.dot_general(left, right, (((1,), (1,)), ((), ())), preferred_element_type=F32)


def dot_tn(left, right):
    return lax.dot_general(left, right, (((0,), (0,)), ((), ())), preferred_element_type=F32)


def iota(shape, axis):
    return lax.broadcasted_iota(jnp.int32, shape, axis)


def below(shape, axis, bound):
    return jnp.where(iota(shape, axis) < bound, 1.0, 0.0).astype(F32)


def key_range(block):
    first = max(0, block * BLOCK - 479) // 32 * 32
    last = min(LIVE, -(-(block * BLOCK + BLOCK + 479) // 32) * 32)
    return first, last


def gelu_parts(z):
    cdf = 0.5 + 0.5 * lax.erf(z * 0.7071067811865476)
    bell = jnp.exp(-0.5 * (z * z)) * 0.3989422804014327
    return z * cdf, cdf + z * bell


def norm_forward(hidden, gain, shift, feature, inv_count):
    center = (hidden - jnp.sum(hidden * feature, axis=-1, keepdims=True) * inv_count) * feature
    inverse = lax.rsqrt(jnp.sum(center * center, axis=-1, keepdims=True) * inv_count + 1e-05)
    normed = center * inverse
    return normed * gain + shift, normed, inverse


def norm_backward(grad, normed, inverse, gain, feature, inv_count):
    scaled = grad * gain
    first = jnp.sum(scaled, axis=-1, keepdims=True) * inv_count
    second = jnp.sum(scaled * normed, axis=-1, keepdims=True) * inv_count
    return inverse * (scaled - first - normed * second) * feature


def col_sum(value):
    return jnp.sum(value, axis=0, keepdims=True)


class Layer:
    def __init__(self, refs):
        self.__dict__.update(refs)
        self.d_a, self.dot_t = self.xm, self.v_t
        for index, name in enumerate(("norm_one", "normed_one", "grad_second")):
            setattr(self, name, self.hold.at[:, index * D : index * D + D])
        self.lanes = self.expo.shape[2]
        width, heads, hidden = self.subnets[0, 0], self.subnets[0, 1], self.subnets[0, 2]
        self.width, self.attend, self.hidden = width, heads * HD, hidden
        self.inv_count = 1.0 / jnp.full((1, 1), width, jnp.int32).astype(F32)

    def row_mask(self, cols, bound, offset=0):
        return jnp.where(iota((1, cols), 1) + offset < bound, 1.0, 0.0).astype(F32)

    def col_mask(self, rows, bound, offset=0):
        return jnp.where(iota((rows, 1), 0) + offset < bound, 1.0, 0.0).astype(F32)

    def feature(self):
        return self.row_mask(D, self.width)

    def vector(self, index):
        mask = self.attend if index < 2 else self.width
        return self.vecs[4 + index : 5 + index, :] * self.row_mask(D, mask)

    def add_sum(self, index, value, first):
        part = value[:8, :]
        for start in range(8, value.shape[0], 8):
            part = part + value[start : start + 8, :]
        if first:
            self.sums[index] = part
        else:
            self.sums[index] += part


    def tokens_copy(self):
        return pltpu.make_async_copy(self.tokens.at[pl.ds(0, LIVE)], self.xm, self.io_sem.at[0])

    def cotangent_copy(self):
        return pltpu.make_async_copy(self.cotangent.at[pl.ds(0, LIVE)], self.cot, self.io_sem.at[1])

    def layer_out_copy(self):
        return pltpu.make_async_copy(self.cot, self.layer_out.at[pl.ds(0, LIVE)], self.io_sem.at[2])

    def layer_rest_copy(self):
        rest = self.layer_out.shape[0] - LIVE
        return pltpu.make_async_copy(self.none, self.layer_out.at[pl.ds(LIVE, rest)], self.io_sem.at[5])

    def input_grad_copy(self, start, size):
        rows = pl.ds(start, size)
        return pltpu.make_async_copy(self.normed_one.at[rows], self.input_grad.at[rows], self.io_sem.at[3])

    def input_rest_copy(self):
        rest = self.input_grad.shape[0] - LIVE
        return pltpu.make_async_copy(self.nothing, self.input_grad.at[pl.ds(LIVE, rest)], self.io_sem.at[4])

    def load(self):
        self.tokens_copy().start()
        self.cotangent_copy().start()

    def start(self):
        pad = self.lanes - LIVE
        self.nothing[...] = jnp.zeros(self.nothing.shape, F32)
        self.input_rest_copy().start()
        self.none[...] = jnp.zeros(self.none.shape, BF)
        self.layer_rest_copy().start()
        self.dot_t[:, :, LIVE:] = jnp.zeros((HEADS, HD, pad), BF)
        self.q_t[:, :, LIVE:] = jnp.zeros((HEADS, HD, pad), BF)
        self.delta[:, :, LIVE:] = jnp.zeros((HEADS, 1, pad), F32)
        self.do_s[LIVE:, :] = jnp.zeros((pad, D), BF)
        self.q_rows[LIVE:, :] = jnp.zeros((pad, D), BF)
        ends = []
        total = 0
        for index in range(4):
            total = total + self.lengths[0, index]
            ends.append(total)
        lane = iota((HD, self.lanes), 1)
        seg = sum((lane >= end).astype(jnp.int32) for end in ends)
        part = iota((HD, self.lanes), 0)
        self.far[...] = jnp.where((part < 4) & (part != seg), -BIG, 0.0).astype(BF)
        row = iota((LIVE, 128), 0)
        seg = sum((row >= end).astype(jnp.int32) for end in ends[:3])
        self.hot[...] = jnp.where(iota((LIVE, 128), 1) - HD == seg, 1.0, 0.0).astype(BF)
        fe = self.feature().astype(BF)
        self.tokens_copy().wait()
        for rows in row_tiles():
            self.xm[rows, :] = self.xm[rows, :] * fe
        for part in range(PAIRS):
            lanes = slice(part * 128, part * 128 + 128)
            self.xt[lanes, :] = self.xm[:, lanes].T

    def load_vectors(self):
        for part in range(PAIRS):
            lanes = slice(part * 128, part * 128 + 128)
            self.vecs[:, lanes] = self.vec_par[part].astype(F32)


    def query_key_value(self, pair):
        lanes = slice(pair * 128, pair * 128 + 128)
        mask = self.col_mask(D, self.width) * self.row_mask(128, self.attend, pair * 128)
        for index, row in enumerate((ROW_Q, ROW_K, ROW_V)):
            weight = (self.flat[pair, row : row + D, :].astype(F32) * mask).astype(BF)
            self.w_qkv[:, pair * D + index * 128 : pair * D + index * 128 + 128] = weight
        bias_q, bias_v = self.vector(0)[:, lanes], self.vector(1)[:, lanes]
        weight = self.w_qkv[:, pair * D : pair * D + D]
        for start in range(0, LIVE, BLOCK):
            rows = slice(start, min(start + BLOCK, LIVE))
            size = rows.stop - rows.start
            even = iota((size, 128), 1) < HD
            out = dot(self.xm[rows, :], weight)
            q = (out[:, :128] + bias_q).astype(BF)
            self.q_rows[rows, lanes] = q
            k32 = out[:, 128:256]
            k = k32.astype(BF)
            hot = self.hot[rows, :]
            self.k_ext[2 * pair, rows, :] = jnp.where(even, k32, hot.astype(F32)).astype(BF)
            self.k_ext[2 * pair + 1, rows, :] = jnp.where(even, pltpu.roll(k32, HD, 1), hot.astype(F32)).astype(BF)
            v = (out[:, 256:] + bias_v).astype(BF)
            self.v_rows[rows, lanes] = v
            turned = (q * jnp.asarray(0.125, BF)).T
            self.q_t[2 * pair, :, rows] = turned[:HD, :]
            self.q_t[2 * pair + 1, :, rows] = turned[HD:, :]
            turned = k.T
            self.k_t[2 * pair, :, rows] = turned[:HD, :]
            self.k_t[2 * pair + 1, :, rows] = turned[HD:, :]
            turned = v.T
            self.v_t[2 * pair, :, rows] = turned[:HD, :]
            self.v_t[2 * pair + 1, :, rows] = turned[HD:, :]

    def score(self, head, block):
        cols = slice(block * BLOCK, block * BLOCK + BLOCK)
        first, last = key_range(block)
        right = jnp.concatenate([self.q_t[head, :, cols], self.far[:, cols]], axis=0)
        self.hold[first:last, cols] = dot(self.k_ext[head, first:last, :], right)

    def soft(self, head, block):
        cols = slice(block * BLOCK, block * BLOCK + BLOCK)
        first, last = key_range(block)
        scores = self.hold[first:last, cols]
        expo = jnp.exp(scores - jnp.max(scores, axis=0, keepdims=True))
        inv = 1.0 / jnp.sum(expo, axis=0, keepdims=True)
        expo = expo.astype(BF)
        self.expo[head, first:last, cols] = expo
        self.inv[head, :, cols] = inv
        return expo, inv

    def attend_first(self, head):
        for block in range(self.lanes // BLOCK):
            self.score(head, block)

    def attend_step(self, head, after):
        for block in range(self.lanes // BLOCK):
            cols = slice(block * BLOCK, block * BLOCK + BLOCK)
            first, last = key_range(block)
            expo, inv = self.soft(head, block)
            if after is not None:
                self.score(after, block)
            mixed = dot(self.v_t[head, :, first:last], expo) * inv
            self.o_t[head, :, cols] = mixed.astype(BF)

    def after_attention(self):
        mask = self.col_mask(D, self.attend) * self.feature()
        for part in range(PAIRS):
            lanes = slice(part * 128, part * 128 + 128)
            rows = self.flat[part, ROW_O : ROW_O + D, :].astype(F32)
            self.w_out[:, lanes] = (rows * mask[:, lanes]).astype(BF)
        fe, bias, gain, shift = self.feature(), self.vector(2), self.vector(3), self.vector(4)
        for start in range(0, LIVE, BLOCK):
            size = min(BLOCK, LIVE - start)
            rows = slice(start, start + size)
            mixed = self.o_t[:, :, start : start + BLOCK].reshape(D, BLOCK)
            attended = dot_tn(mixed, self.w_out[...])[:size, :]
            hidden = self.xm[rows, :].astype(F32) + attended + bias
            norm, normed, inverse = norm_forward(hidden, gain, shift, fe, self.inv_count)
            self.norm_one[rows, :] = norm
            self.normed_one[rows, :] = normed
            self.inverse_one[rows, :] = jnp.broadcast_to(inverse, (size, 128))
            self.norm_low[rows, :] = norm.astype(BF)

    def up_weights(self):
        for part in range(PAIRS):
            self.wide[part] = self.flat[part, ROW_UP : ROW_UP + FF, :].astype(F32)
        for chunk in range(CHUNKS):
            mask = self.col_mask(D, self.width) * self.row_mask(D, self.hidden, chunk * D)
            for part in range(PAIRS):
                lanes = slice(part * 128, part * 128 + 128)
                piece = self.wide[part, pl.ds(chunk, D, stride=CHUNKS), :]
                self.w_up[:, chunk * D + part * 128 : chunk * D + part * 128 + 128] = (
                    piece * mask[:, lanes]
                ).astype(BF)

    def down_weights(self):
        mask = self.feature()
        for chunk in range(CHUNKS):
            rows = slice(chunk * D, chunk * D + D)
            hidden = self.col_mask(D, self.hidden, chunk * D)
            for part in range(PAIRS):
                lanes = slice(part * 128, part * 128 + 128)
                piece = self.flat[part, ROW_DOWN + chunk * D : ROW_DOWN + chunk * D + D, :].astype(F32)
                self.w_down[rows, lanes] = (piece * (hidden * mask[:, lanes])).astype(BF)

    def up_tile(self, rows):
        low = self.norm_low[rows, :]
        for chunk in range(CHUNKS):
            cols = slice(chunk * D, chunk * D + D)
            bias = self.vecs[chunk : chunk + 1, :] * self.row_mask(D, self.hidden, chunk * D)
            act, slope = gelu_parts(dot(low, self.w_up[:, cols]) + bias)
            self.act[rows, cols] = act.astype(BF)
            self.slope[rows, cols] = slope.astype(BF)

    def down_tile(self, rows):
        fe = self.feature()
        bias, gain, shift = self.vector(5), self.vector(6), self.vector(7)
        second = self.norm_one[rows, :] + dot(self.act[rows, :FF], self.w_down[...]) + bias
        result, normed, inverse = norm_forward(second, gain, shift, fe, self.inv_count)
        grad = self.cot[rows, :].astype(F32)
        self.cot[rows, :] = result.astype(BF)
        grad_second = norm_backward(grad, normed, inverse, gain, fe, self.inv_count)
        self.grad_second[rows, :] = grad_second
        low = grad_second.astype(BF)
        self.d_f[rows, :] = low
        first = rows.start == 0
        self.add_sum(10, grad * normed, first)
        self.add_sum(11, grad, first)
        self.add_sum(9, low.astype(F32), first)

    def feed_forward(self, before_down):
        tiles = row_tiles()
        self.up_tile(tiles[0])
        before_down()
        self.cotangent_copy().wait()
        for rows, after in zip(tiles, tiles[1:] + [None]):
            if after is not None:
                self.up_tile(after)
            self.down_tile(rows)
        self.layer_out_copy().start()


    def down_grad(self, chunks):
        fe = self.feature()
        for chunk in chunks:
            cols = slice(chunk * D, chunk * D + D)
            mask = self.col_mask(D, self.hidden, chunk * D) * fe
            grad = (dot_tn(self.act[:, cols], self.d_f[...]) * mask).astype(BF)
            for part in range(PAIRS):
                lanes = slice(part * 128, part * 128 + 128)
                self.grads[part, ROW_DOWN + chunk * D : ROW_DOWN + chunk * D + D, :] = grad[:, lanes]

    def hidden_tile(self, rows):
        d_f = self.d_f[rows, :]
        for chunk in range(CHUNKS):
            cols = slice(chunk * D, chunk * D + D)
            grad = dot_nt(d_f, self.w_down[cols, :])
            dz = (grad * self.slope[rows, cols].astype(F32)).astype(BF)
            self.slope[rows, cols] = dz
            self.add_sum(chunk, dz.astype(F32), rows.start == 0)

    def first_norm_tile(self, rows):
        gain, fe = self.vector(3), self.feature()
        normed = self.normed_one[rows, :]
        grad = self.grad_second[rows, :] + dot_nt(self.slope[rows, :], self.w_up[...])
        grad_first = norm_backward(grad, normed, self.inverse_one[rows, :1], gain, fe, self.inv_count)
        self.norm_one[rows, :] = grad_first
        low = grad_first.astype(BF)
        self.d_a[rows, :] = low
        first = rows.start == 0
        self.add_sum(7, grad * normed, first)
        self.add_sum(8, grad, first)
        self.add_sum(6, low.astype(F32), first)

    def hidden_grad(self):
        for rows in row_tiles():
            self.hidden_tile(rows)

    def first_norm_grad(self, tiles):
        for index in tiles:
            self.first_norm_tile(row_tiles()[index])

    def up_grad(self, start):
        half = D // 2
        low = self.norm_low[:, start : start + half]
        for chunk in range(CHUNKS):
            cols = slice(chunk * D, chunk * D + D)
            mask = self.col_mask(half, self.width, start) * self.row_mask(D, self.hidden, chunk * D)
            grad = dot_tn(low, self.slope[:, cols]) * mask
            for part in range(PAIRS):
                lanes = slice(part * 128, part * 128 + 128)
                self.wide[part, pl.ds(start * CHUNKS + chunk, half, stride=CHUNKS), :] = grad[:, lanes]
        rows = slice(start * CHUNKS, (start + half) * CHUNKS)
        for part in range(PAIRS):
            self.grads[part, ROW_UP + rows.start : ROW_UP + rows.stop, :] = self.wide[part, rows, :].astype(BF)

    def out_grad(self):
        fe = self.feature()
        d_a = self.d_a[...]
        half = D // 2
        for start in (0, half):
            rows = slice(start, start + half)
            heads = range(start // HD, (start + half) // HD)
            mask = self.col_mask(half, self.attend, start) * fe
            o_t = self.o_t[heads.start : heads.stop, :, :LIVE].reshape(half, LIVE)
            grad = (dot(o_t, d_a) * mask).astype(BF)
            for part in range(PAIRS):
                lanes = slice(part * 128, part * 128 + 128)
                self.grads[part, ROW_O + start : ROW_O + start + half, :] = grad[:, lanes]
            mixed = dot_nt(self.w_out[rows, :], d_a)
            for head in heads:
                own = mixed[head * HD - start : head * HD - start + HD, :] * self.inv[head, :, :LIVE]
                self.delta[head, :, :LIVE] = col_sum(own * self.o_t[head, :, :LIVE].astype(F32))
                self.dot_t[head, :, :LIVE] = own.astype(BF)
        for pair in range(PAIRS):
            both = self.dot_t[2 * pair : 2 * pair + 2, :, :LIVE].reshape(128, LIVE)
            self.do_s[:LIVE, pair * 128 : pair * 128 + 128] = both.T

    def score_place(self, odd, block):
        if not odd:
            return self.act, block * BLOCK
        return ((self.act, 4 * BLOCK), (self.act, 5 * BLOCK), (self.slope, PAIRS * D), (self.d_f, 0))[block]

    def prob_grad(self, pair, odd, block):
        cols = slice(block * BLOCK, block * BLOCK + BLOCK)
        first, last = key_range(block)
        right = self.dot_t[2 * pair + odd, :, cols]
        none = jnp.zeros_like(right)
        right = jnp.concatenate([none, right] if odd else [right, none], axis=0)
        return dot(self.v_rows[first:last, pair * 128 : pair * 128 + 128], right)

    def score_grad(self, pair, odd, block, grad):
        head = 2 * pair + odd
        cols = slice(block * BLOCK, block * BLOCK + BLOCK)
        first, last = key_range(block)
        grad = self.expo[head, first:last, cols].astype(F32) * (grad - self.delta[head, :, cols])
        grad = grad.astype(BF)
        place, start = self.score_place(odd, block)
        place[first:last, start : start + BLOCK] = grad
        return grad

    def query_grad(self, pair, odd, block, grad):
        head = 2 * pair + odd
        cols = slice(block * BLOCK, block * BLOCK + BLOCK)
        first, last = key_range(block)
        dq = dot(self.k_t[head, :, first:last], grad) * 0.125
        self.dq_t[odd * HD : odd * HD + HD, cols] = dq.astype(BF)

    def pair_backward(self, pair, hooks):
        lanes = slice(pair * 128, pair * 128 + 128)
        blocks = self.lanes // BLOCK
        ranges = [key_range(block) for block in range(blocks)]
        edges = sorted({edge for both in ranges for edge in both})
        cuts = []
        for low, high in zip(edges[:-1], edges[1:]):
            used = [b for b in range(blocks) if ranges[b][0] <= low and high <= ranges[b][1]]
            cuts.append((slice(low, high), slice(used[0] * BLOCK, used[-1] * BLOCK + BLOCK)))
        own = [jnp.where((iota((1, 128), 1) >= HD) == bool(odd), 1.0, 0.0).astype(BF) for odd in (0, 1)]
        d_out = [self.do_s[:, lanes] * own[odd] for odd in (0, 1)]
        items = [(odd, block) for odd in (0, 1) for block in range(blocks)]
        grad = self.prob_grad(pair, *items[0])
        for index, (odd, block) in enumerate(items):
            if index % 2 == 0 and index // 2 < len(cuts):
                rows, span = cuts[index // 2]
                dv = sum(dot(self.expo[2 * pair + odd_, rows, span], d_out[odd_][span]) for odd_ in (0, 1))
                self.slope[rows, pair * D + 256 : pair * D + 384] = dv.astype(BF)
            after = self.prob_grad(pair, *items[index + 1]) if index + 1 < len(items) else None
            low = self.score_grad(pair, odd, block, grad)
            grad = after
            self.query_grad(pair, odd, block, low)
            if index in hooks:
                hooks[index]()
        queries = [self.q_rows[:, lanes] * own[odd] for odd in (0, 1)]
        for rows, span in cuts:
            dk = 0.0
            for odd in (0, 1):
                places = [self.score_place(odd, block) for block in range(span.start // BLOCK, span.stop // BLOCK)]
                first = 0
                for last in range(1, len(places) + 1):
                    if last == len(places) or places[last][0] is not places[first][0]:
                        place, start = places[first]
                        begin, size = span.start + first * BLOCK, (last - first) * BLOCK
                        dk = dk + dot(place[rows, start : start + size], queries[odd][begin : begin + size])
                        first = last
            self.slope[rows, pair * D + 128 : pair * D + 256] = (dk * 0.125).astype(BF)
        self.slope[:, pair * D : pair * D + 128] = self.dq_t[:, :LIVE].T
        mask = self.col_mask(D, self.width) * self.row_mask(128, self.attend, pair * 128)
        all_three = self.slope[:, pair * D : pair * D + D]
        grad = dot(self.xt[...], all_three)
        for index, row in enumerate((ROW_Q, ROW_K, ROW_V)):
            self.grads[pair, row : row + D, :] = (grad[:, index * 128 : index * 128 + 128] * mask).astype(BF)
        totals = dot(jnp.ones((8, LIVE), BF), all_three)
        self.sums[4, :, lanes] = totals[:, :128] * 0.125
        self.sums[5, :, lanes] = totals[:, 256:] * 0.125

    def input_grad_step(self, hooks):
        fe = self.feature()
        for index, rows in enumerate(row_tiles()):
            total = self.norm_one[rows, :] + dot_nt(self.slope[rows, : PAIRS * D], self.w_qkv[...])
            self.normed_one[rows, :] = total * fe
            self.input_grad_copy(rows.start, rows.stop - rows.start).start()
            if index in hooks:
                hooks[index]()

    def finish(self):
        self.input_grad_copy(0, LIVE).wait()
        self.input_rest_copy().wait()
        self.layer_out_copy().wait()
        self.layer_rest_copy().wait()

    def vector_grads(self):
        for index in range(12):
            total = jnp.sum(self.sums[index], axis=0, keepdims=True)
            if index < CHUNKS:
                mask = self.row_mask(D, self.hidden, index * D)
            else:
                mask = self.row_mask(D, self.attend if index < 6 else self.width)
            self.grad_vecs[index : index + 1, :] = total * mask
        self.grad_vecs[12:, :] = jnp.zeros((4, D), F32)


def row_tiles():
    return [slice(start, min(start + TILE, LIVE)) for start in range(0, LIVE, TILE)]


def scratch_refs(rows):
    vmem = pltpu.VMEM
    lanes = -(-LIVE // BLOCK) * BLOCK
    return {
        "xm": vmem((LIVE, D), BF),
        "cot": vmem((LIVE, D), BF),
        "none": vmem((rows - LIVE, D), BF),
        "nothing": vmem((rows - LIVE, D), F32),
        "hold": vmem((LIVE, 3 * D), F32),
        "xt": vmem((D, LIVE), BF),
        "hot": vmem((LIVE, 128), BF),
        "far": vmem((HD, lanes), BF),
        "vecs": vmem((16, D), F32),
        "sums": vmem((12, 8, D), F32),
        "w_qkv": vmem((D, PAIRS * D), BF),
        "w_out": vmem((D, D), BF),
        "w_up": vmem((D, FF), BF),
        "w_down": vmem((FF, D), BF),
        "wide": vmem((PAIRS, FF, 128), F32),
        "q_rows": vmem((lanes, D), BF),
        "q_t": vmem((HEADS, HD, lanes), BF),
        "k_t": vmem((HEADS, HD, LIVE), BF),
        "k_ext": vmem((HEADS, LIVE, 128), BF),
        "v_rows": vmem((LIVE, D), BF),
        "v_t": vmem((HEADS, HD, lanes), BF),
        "expo": vmem((HEADS, LIVE, lanes), BF),
        "inv": vmem((HEADS, 1, lanes), F32),
        "o_t": vmem((HEADS, HD, lanes), BF),
        "inverse_one": vmem((LIVE, 128), F32),
        "norm_low": vmem((LIVE, D), BF),
        "act": vmem((LIVE, FF), BF),
        "slope": vmem((LIVE, FF), BF),
        "d_f": vmem((LIVE, D), BF),
        "do_s": vmem((lanes, D), BF),
        "delta": vmem((HEADS, 1, lanes), F32),
        "dq_t": vmem((128, lanes), BF),
        "io_sem": pltpu.SemaphoreType.DMA((6,)),
    }


class Exchange:
    def __init__(self, refs):
        self.__dict__.update(refs)
        group, self.x = lax.axis_index("group"), lax.axis_index("item")
        self.z, self.y, self.c = group // 4, (group // 2) % 2, group % 2
        self.spot = 2 * self.y + self.x
        self.shard = 2 * group + self.x
        self.corner = (self.c == 1) & (self.spot == 3)

    def device(self, z, y, c, x):
        return (z * 4 + y * 2 + c, x)

    def line(self, step):
        return self.device((self.z + step) % PLANES, self.y, self.c, self.x)

    def plane_peer(self, step):
        y, x = (self.y + step // 4) % 2, (self.x + step % 2) % 2
        return self.device(self.z, y, (self.c + step // 2 % 2) % 2, x)

    def chip_peer(self, step):
        y, x = (self.y + step // 2) % 2, (self.x + step % 2) % 2
        return self.device(self.z, y, self.c, x)

    def spot_of(self, step):
        return 2 * ((self.y + step // 2) % 2) + (self.x + step % 2) % 2

    def core_peer(self):
        return self.device(self.z, self.y, 1 - self.c, self.x)

    def greet(self):
        barrier = pltpu.get_barrier_semaphore()
        peers = [self.line(step) for step in (1, 2, 3)] + [self.plane_peer(step) for step in range(1, 8)]
        for peer in peers:
            pl.semaphore_signal(barrier, inc=1, device_id=peer, device_id_type=MESH)

    def greeted(self):
        pl.semaphore_wait(pltpu.get_barrier_semaphore(), 10)

    def copy(self, source, target, send, recv, peer):
        return pltpu.make_async_remote_copy(
            src_ref=source, dst_ref=target, send_sem=send, recv_sem=recv, device_id=peer, device_id_type=MESH
        )


    def offsets(self):
        shift = STEP * self.shard
        return shift // 128, shift % 128

    def frame_own(self):
        rows = self.own_params.shape[0]
        up, across = self.offsets()
        turned = pltpu.roll(self.own_params[...].astype(F32), across, 1)
        late = iota((rows, 128), 1) >= across
        same = jnp.where(late, turned, 0.0).astype(BF)
        carried = jnp.where(late, 0.0, turned).astype(BF)
        gap = 3 * iota((FRAME, rows), 0) - up - iota((FRAME, rows), 1)
        for part in range(PAIRS):
            here = jnp.where(gap == -part, 1.0, 0.0).astype(BF)
            after = jnp.where(gap == 1 - part, 1.0, 0.0).astype(BF)
            frame = dot(here, same) + dot(after, carried)
            self.land[self.z, part, self.c, self.spot] = frame.astype(BF)

    def vectors_line(self, step):
        sems = self.par_send.at[step - 1], self.par_recv.at[0]
        return self.copy(self.vec_par, self.vec_par, *sems, self.line(step))

    def vectors_plane(self, step):
        sems = self.par_send.at[step + 2], self.par_recv.at[1]
        return self.copy(self.vec_par, self.vec_par, *sems, self.plane_peer(step))

    def send_vectors_line(self):
        @pl.when(self.corner & (self.z == PLANES - 1))
        def _():
            self.vec_par[...] = self.land[PLANES - 1, :, 1, 3, STEP:, :]
            for step in (1, 2, 3):
                self.vectors_line(step).start()

    def send_vectors_plane(self):
        @pl.when(self.corner & (self.z != PLANES - 1))
        def _():
            self.vectors_line(1).wait_recv()

        @pl.when(self.corner)
        def _():
            for step in range(1, 8):
                self.vectors_plane(step).start()

    def finish_vectors_plane(self):
        @pl.when(jnp.logical_not(self.corner))
        def _():
            self.vectors_plane(1).wait_recv()

    def parts(self, plane, part):
        return pl.ds(part, 1) if isinstance(plane, int) and plane == 0 else slice(None)

    def blocks(self, plane, part):
        return [part] if plane == 0 else range(PAIRS)

    def item(self, plane, part):
        return part if isinstance(plane, int) and plane == 0 else 2 + plane

    def gather_line(self, plane, part, step):
        piece = self.land.at[plane, self.parts(plane, part), self.c, self.spot]
        sems = self.line_send.at[part, step - 1], self.line_recv.at[self.item(plane, part)]
        return self.copy(piece, piece, *sems, self.line(step))

    def send_line(self, plane, part, steps):
        @pl.when(self.z == plane)
        def _():
            for step in steps:
                self.gather_line(plane, part, step).start()

    def gather_all(self, part, step, spot):
        piece = self.land.at[0, pl.ds(part, 1), self.c, spot]
        sems = self.flat_send.at[3 * part + step - 1], self.flat_recv.at[3 * part + step - 1]
        return self.copy(piece, piece, *sems, self.chip_peer(step))

    def gather_next(self, plane, step, spot):
        piece = self.land.at[plane, :, self.c, spot]
        index = 5 + 4 * plane + step - 1
        return self.copy(piece, piece, self.flat_send.at[index], self.flat_recv.at[index], self.chip_peer(step))

    def gather_half(self, plane, step, spot):
        rows = pl.ds((2 - step) * HALF, HALF)
        piece = self.land.at[plane, :, self.c, spot, rows]
        index = 5 + 4 * plane + step + 1
        return self.copy(piece, piece, self.flat_send.at[index], self.flat_recv.at[index], self.chip_peer(step))

    def wait_line(self, plane, part):
        @pl.when(self.z != plane)
        def _():
            self.gather_line(plane, part, 1).wait_recv()

    def send_all(self, part):
        self.wait_line(0, part)
        for step in (3, 2, 1):
            self.gather_all(part, step, self.spot).start()

    def plane_order(self):
        second = jnp.where(self.z == 0, 3, jnp.where(self.z == 1, 2, 1))
        third = jnp.where(self.z % 3 == 0, 2, 3)
        return jnp.maximum(self.z, 1), second, third

    def own_first(self, action):
        @pl.when(self.z != 0)
        def _():
            action()

    def others_first(self, *actions):
        @pl.when(self.z == 0)
        def _():
            for action in actions:
                action()

    def receive_line(self, plane):
        self.copy_line(plane).wait_recv()

    def copy_line(self, plane):
        piece = self.land.at[plane, :, self.c, self.spot]
        return self.copy(piece, piece, self.line_send.at[1, 0], self.line_recv.at[2 + plane], self.line(1))

    def send_next(self, plane):
        for step in (2, 1):
            self.gather_next(plane, step, self.spot).start()

    def send_halves(self, plane):
        self.gather_next(plane, 1, self.spot_of(1)).wait_recv()
        self.gather_half(plane, 2, self.spot_of(1)).start()
        self.gather_next(plane, 2, self.spot_of(2)).wait_recv()
        self.gather_half(plane, 1, self.spot_of(2)).start()

    def gather_core(self, plane, part, core):
        piece = self.land.at[plane, self.parts(plane, part), core]
        item = self.item(plane, part)
        return self.copy(piece, piece, self.core_send.at[item], self.core_recv.at[item], self.core_peer())

    def send_core(self, plane, part=0):
        if isinstance(plane, int) and plane == 0:
            for step in (3, 2, 1):
                self.gather_all(part, step, self.spot_of(step)).wait_recv()
        else:
            for step in (2, 1):
                self.gather_half(plane, step, self.spot_of(3)).wait_recv()
        self.gather_core(plane, part, self.c).start()

    def finish_gather(self, plane, part=0):
        self.gather_core(plane, part, 1 - self.c).wait_recv()
        for place in range(8):
            y, c, x = place // 4, (place // 2) % 2, place % 2
            chunk = 8 * plane + place
            for block in self.blocks(plane, part):
                frame = self.land[plane, block, c, 2 * y + x]
                self.flat[block, chunk * STEP : chunk * STEP + STEP, :] = frame[:STEP, :]
                if chunk:
                    before = (chunk - 1) % 8
                    spot = 2 * (before // 4) + before % 2
                    tail = self.land[(chunk - 1) // 8, block, (before // 2) % 2, spot, STEP:, :]
                    both = tail + frame[: FRAME - STEP, :]
                    self.flat[block, chunk * STEP : chunk * STEP + FRAME - STEP, :] = both

    def drain_gather(self):
        @pl.when(self.corner & (self.z == PLANES - 1))
        def _():
            for step in (1, 2, 3):
                self.vectors_line(step).wait_send()

        @pl.when(self.corner)
        def _():
            for step in range(1, 8):
                self.vectors_plane(step).wait_send()

        for plane in range(PLANES):
            for part in range(PAIRS if plane == 0 else 1):

                @pl.when(self.z == plane)
                def _():
                    for step in (1, 2, 3):
                        self.gather_line(plane, part, step).wait_send()

                if plane == 0:
                    for step in (1, 2, 3):
                        self.gather_all(part, step, self.spot).wait_send()
                else:
                    for step in (1, 2):
                        self.gather_next(plane, step, self.spot).wait_send()
                        self.gather_half(plane, step, self.spot).wait_send()
                self.gather_core(plane, part, self.c).wait_send()


    def sum_core(self, plane, part, y):
        row = pl.multiple_of(STEP * (8 * plane + 4 * y + 2 * (1 - self.c)), 16)
        parts, item = self.parts(plane, part), 2 * self.item(plane, part) + y
        return self.copy(
            self.grads.at[parts, pl.ds(row, TWO)],
            self.core_land.at[plane % 3, y, parts],
            self.sum_core_send.at[item],
            self.sum_core_recv.at[item],
            self.core_peer(),
        )

    def sum_all(self, part, step):
        index = 3 * part + step - 1
        return self.copy(
            self.land.at[0, pl.ds(part, 1), 0, self.spot_of(step)],
            self.all_land.at[step - 1, pl.ds(part, 1)],
            self.sum_flat_send.at[index],
            self.sum_flat_recv.at[index],
            self.chip_peer(step),
        )

    def sum_half(self, plane, step):
        index = 5 + 4 * plane + step - 1
        return self.copy(
            self.land.at[plane, :, 0, self.spot_of(3), pl.ds((step - 1) * HALF, HALF)],
            self.half_land.at[plane - 1, step - 1],
            self.sum_flat_send.at[index],
            self.sum_flat_recv.at[index],
            self.chip_peer(step),
        )

    def sum_next(self, plane, step):
        index = 5 + 4 * plane + step + 1
        return self.copy(
            self.land.at[plane, :, 0, self.spot_of(step)],
            self.next_land.at[plane - 1, step - 1],
            self.sum_flat_send.at[index],
            self.sum_flat_recv.at[index],
            self.chip_peer(step),
        )

    def sum_line(self, plane, part, slot):
        parts, item = self.parts(plane, part), self.item(plane, part)
        return self.copy(
            self.plane_sum.at[plane, parts],
            self.line_land.at[slot, parts],
            self.sum_line_send.at[item],
            self.sum_line_recv.at[3 * part + slot],
            self.device(plane, self.y, self.c, self.x),
        )

    def reduce_core(self, plane, part=0):
        for y in (0, 1):
            self.sum_core(plane, part, y).start()

    def add_core(self, plane, part):
        for y in (0, 1):
            self.sum_core(plane, part, y).wait_recv()
            for block in self.blocks(plane, part):
                for x in (0, 1):
                    row = pl.multiple_of(STEP * (8 * plane + 4 * y + 2 * self.c + x), 16)
                    own = self.grads[block, pl.ds(row, FRAME), :]
                    other = self.core_land[plane % 3, y, block, x * STEP : x * STEP + FRAME, :]
                    self.land[plane, block, 0, 2 * y + x] = own + other

    def reduce_all(self, part):
        self.add_core(0, part)
        for step in (3, 2, 1):
            self.sum_all(part, step).start()

    def reduce_halves(self, plane):
        self.add_core(plane, 0)
        for step in (1, 2):
            self.sum_half(plane, step).start()

    def reduce_next(self, plane):
        for step in (1, 2):
            self.sum_half(plane, step).wait_recv()
            rows = slice((step - 1) * HALF, step * HALF)
            spot = self.spot_of(3 - step)
            for block in range(PAIRS):
                own = self.land[plane, block, 0, spot, rows, :]
                self.land[plane, block, 0, spot, rows, :] = own + self.half_land[plane - 1, step - 1, block]
            self.sum_next(plane, 3 - step).start()

    def reduce_line(self, plane, part=0):
        if plane == 0:
            for step in (1, 2, 3):
                self.sum_all(part, step).wait_recv()
        else:
            for step in (1, 2):
                self.sum_next(plane, step).wait_recv()
        for block in self.blocks(plane, part):
            total = self.land[plane, block, 0, self.spot].astype(F32)
            if plane == 0:
                for step in (1, 2, 3):
                    total = total + self.all_land[step - 1, block].astype(F32)
            else:
                for step in (1, 2):
                    total = total + self.next_land[plane - 1, step - 1, block].astype(F32)
            self.plane_sum[plane, block] = total.astype(BF)

            @pl.when(self.z == plane)
            def _():
                self.total[block] = total

        @pl.when(self.z != plane)
        def _():
            self.sum_line(plane, part, (self.z - plane + 2 * PLANES - 1) % PLANES).start()

    def vector_core(self):
        peer = self.core_peer()
        return self.copy(self.grad_vecs, self.vec_core, self.vec_send.at[0], self.vec_recv.at[0], peer)

    def vector_flat(self, slot):
        peer = self.device(self.z, 1, 1, 1)
        return self.copy(self.vec_sum, self.vec_flat.at[slot], self.vec_send.at[1], self.vec_recv.at[1 + slot], peer)

    def vector_line(self, slot):
        peer = self.device(PLANES - 1, 1, 1, 1)
        return self.copy(self.vec_sum, self.vec_line.at[slot], self.vec_send.at[2], self.vec_recv.at[4 + slot], peer)

    def reduce_vectors_core(self):
        @pl.when(self.c == 0)
        def _():
            self.vector_core().start()

    def reduce_vectors_flat(self):
        @pl.when(self.c == 1)
        def _():
            self.vector_core().wait_recv()
            self.vec_sum[...] = self.grad_vecs[...] + self.vec_core[...]

            @pl.when(self.spot != 3)
            def _():
                self.vector_flat(2 - self.spot).start()

    def reduce_vectors_line(self):
        @pl.when(self.corner)
        def _():
            for slot in range(3):
                self.vector_flat(slot).wait_recv()
            self.vec_sum[...] = self.vec_sum[...] + self.vec_flat[0] + self.vec_flat[1] + self.vec_flat[2]

            @pl.when(self.z != PLANES - 1)
            def _():
                self.vector_line(self.z).start()

    def finish_vectors(self):
        @pl.when(self.corner & (self.z == PLANES - 1))
        def _():
            total = self.vec_sum[...]
            for slot in range(3):
                self.vector_line(slot).wait_recv()
                total = total + self.vec_line[slot]
            for block in range(PAIRS):
                self.total[block, STEP:, :] = total[:, block * 128 : block * 128 + 128]

        @pl.when(self.c == 0)
        def _():
            self.vector_core().wait_send()

        @pl.when((self.c == 1) & (self.spot != 3))
        def _():
            self.vector_flat(0).wait_send()

        @pl.when(self.corner & (self.z != PLANES - 1))
        def _():
            self.vector_line(0).wait_send()

    def finish_line(self, plane, part=0):
        @pl.when(self.z == plane)
        def _():
            for slot in range(3):
                self.sum_line(plane, part, slot).wait_recv()
            for block in self.blocks(plane, part):
                total = self.total[block]
                for slot in range(3):
                    total = total + self.line_land[slot, block].astype(F32)
                self.total[block] = total

    def drain_sum(self, plane, part=0):
        @pl.when(self.z != plane)
        def _():
            self.sum_line(plane, part, 0).wait_send()

        if plane == 0:
            for step in (1, 2, 3):
                self.sum_all(part, step).wait_send()
        else:
            for step in (1, 2):
                self.sum_half(plane, step).wait_send()
                self.sum_next(plane, step).wait_send()
        for y in (0, 1):
            self.sum_core(plane, part, y).wait_send()

    def unframe(self, parts, last):
        rows = self.own_grad.shape[0]
        up, across = self.offsets()
        gap = iota((rows, FRAME), 0) + up - 3 * iota((rows, FRAME), 1)
        here = self.shard_sum[0] if last else jnp.zeros((rows, 128), F32)
        carried = self.shard_sum[1] if last else jnp.zeros((rows, 128), F32)
        for block in parts:
            total = self.total[block]
            high = total.astype(BF)
            both = jnp.concatenate([high, (total - high.astype(F32)).astype(BF)], axis=1)
            moved = dot(jnp.where(gap == block, 1.0, 0.0).astype(BF), both)
            here = here + (moved[:, :128] + moved[:, 128:])
            moved = dot(jnp.where(gap == block - 1, 1.0, 0.0).astype(BF), both)
            carried = carried + (moved[:, :128] + moved[:, 128:])
        if last:
            mixed = jnp.where(iota((rows, 128), 1) >= across, here, carried)
            self.own_grad[...] = pltpu.roll(mixed, (128 - across) % 128, 1)
        else:
            self.shard_sum[0] = here
            self.shard_sum[1] = carried


def exchange_refs(shard_rows):
    vmem, dma = pltpu.VMEM, pltpu.SemaphoreType.DMA
    return {
        "grads": vmem((PAIRS, ALL_ROWS, 128), BF),
        "grad_vecs": vmem((16, D), F32),
        "land": vmem((PLANES, PAIRS, 2, 4, FRAME, 128), BF),
        "core_land": vmem((3, 2, PAIRS, TWO, 128), BF),
        "all_land": vmem((3, PAIRS, FRAME, 128), BF),
        "half_land": vmem((PLANES - 1, 2, PAIRS, HALF, 128), BF),
        "next_land": vmem((PLANES - 1, 2, PAIRS, FRAME, 128), BF),
        "plane_sum": vmem((PLANES, PAIRS, FRAME, 128), BF),
        "line_land": vmem((3, PAIRS, FRAME, 128), BF),
        "total": vmem((PAIRS, FRAME, 128), F32),
        "shard_sum": vmem((2, shard_rows, 128), F32),
        "vec_par": vmem((PAIRS, 16, 128), BF),
        "vec_core": vmem((16, D), F32),
        "vec_sum": vmem((16, D), F32),
        "vec_flat": vmem((3, 16, D), F32),
        "vec_line": vmem((3, 16, D), F32),
        "line_send": dma((PAIRS, 3)),
        "line_recv": dma((6,)),
        "flat_send": dma((21,)),
        "flat_recv": dma((21,)),
        "core_send": dma((6,)),
        "core_recv": dma((6,)),
        "sum_core_send": dma((12,)),
        "sum_core_recv": dma((12,)),
        "sum_flat_send": dma((21,)),
        "sum_flat_recv": dma((21,)),
        "sum_line_send": dma((6,)),
        "sum_line_recv": dma((9,)),
        "par_send": dma((10,)),
        "par_recv": dma((2,)),
        "vec_send": dma((3,)),
        "vec_recv": dma((7,)),
    }


def whole_kernel(names, *refs):
    refs = dict(zip(names, refs))
    refs["flat"] = refs["grads"]
    layer, swap = Layer(refs), Exchange(refs)
    layer.load()
    swap.greet()
    swap.frame_own()
    layer.start()
    swap.greeted()
    swap.send_vectors_line()
    for part in range(PAIRS):
        swap.send_line(0, part, (3, 2, 1))
    swap.send_line(3, 0, (1, 2, 3))
    swap.send_line(2, 0, (3, 2, 1))
    swap.send_line(1, 0, (3,))
    own, second, third = swap.plane_order()
    swap.own_first(lambda: swap.send_next(own))
    swap.send_all(0)
    swap.send_line(1, 0, (2, 1))
    swap.send_vectors_plane()
    swap.send_all(1)
    swap.send_core(0, 0)
    swap.own_first(lambda: swap.send_halves(own))
    swap.send_all(2)
    swap.others_first(lambda: swap.receive_line(own), lambda: swap.send_next(own))
    swap.finish_vectors_plane()
    layer.load_vectors()
    swap.finish_gather(0, 0)
    layer.query_key_value(0)
    layer.attend_first(0)
    swap.send_core(0, 1)

    before = {
        1: [lambda: swap.finish_gather(0, 1), lambda: layer.query_key_value(1)],
        3: [lambda: swap.finish_gather(0, 2), lambda: layer.query_key_value(2)],
    }
    after = {
        0: [lambda: swap.receive_line(second), lambda: swap.send_next(second)],
        1: [
            lambda: swap.others_first(lambda: swap.send_halves(own)),
            lambda: swap.receive_line(third),
            lambda: swap.send_next(third),
            lambda: swap.send_core(0, 2),
        ],
        2: [lambda: swap.send_halves(second), lambda: swap.send_core(own)],
        3: [lambda: swap.send_halves(third)],
        4: [lambda: swap.send_core(second)],
    }

    @pl.loop(0, HEADS - 1)
    def _(head):
        for table, step in ((before, None), (after, layer.attend_step)):
            if step is not None:
                step(head, head + 1)
            for index, actions in table.items():

                @pl.when(head == index)
                def _():
                    for action in actions:
                        action()

    layer.attend_step(HEADS - 1, None)
    swap.send_core(third)
    swap.finish_gather(1)
    layer.after_attention()
    swap.finish_gather(2)
    layer.up_weights()

    def before_down():
        swap.finish_gather(3)
        layer.down_weights()

    layer.feed_forward(before_down)
    for block in range(PAIRS):
        layer.grads[block, ROW_VEC:, :] = jnp.zeros((ALL_ROWS - ROW_VEC, 128), BF)
    layer.down_grad((1, 2, 3))
    swap.reduce_core(3)
    layer.down_grad((0,))
    swap.drain_gather()
    layer.hidden_grad()
    swap.reduce_halves(3)
    layer.up_grad(D // 2)
    swap.reduce_core(2)
    layer.first_norm_grad((0, 1))
    layer.up_grad(0)
    swap.reduce_next(3)
    swap.reduce_halves(2)
    layer.first_norm_grad((2, 3, 4))
    layer.out_grad()
    swap.reduce_core(1)

    def first_late():
        swap.reduce_halves(1)
        swap.reduce_next(2)
        swap.reduce_line(3)

    layer.pair_backward(0, {7: first_late})
    swap.reduce_core(0, 0)
    def second_late():
        swap.reduce_all(0)
        swap.reduce_line(2)

    layer.pair_backward(1, {3: lambda: swap.reduce_next(1), 7: second_late})
    swap.reduce_core(0, 1)
    swap.reduce_line(1)

    def third_late():
        swap.reduce_all(1)
        swap.reduce_line(0, 0)

    layer.pair_backward(2, {7: third_late})
    swap.reduce_core(0, 2)
    layer.vector_grads()
    swap.reduce_vectors_core()

    def last_flat():
        swap.reduce_all(2)
        swap.reduce_vectors_flat()
        swap.reduce_line(0, 1)

    layer.input_grad_step({1: last_flat})
    swap.reduce_line(0, 2)
    swap.reduce_vectors_line()
    for plane in (1, 2, 3):
        swap.drain_sum(plane)
        swap.finish_line(plane)
    for part in (0, 1):
        swap.drain_sum(0, part)
        swap.finish_line(0, part)
    swap.finish_vectors()
    swap.unframe((0, 1), False)
    layer.finish()
    swap.drain_sum(0, 2)
    swap.finish_line(0, 2)
    swap.unframe((2,), True)


def whole_layer(tokens, cotangent, own_params, subnets, lengths):
    rows = tokens.shape[0]
    scratch = scratch_refs(rows) | exchange_refs(own_params.shape[0])
    inputs = ["tokens", "cotangent", "own_params", "subnets", "lengths"]
    outputs = ["layer_out", "input_grad", "own_grad"]
    spaces = [pl.ANY] * 2 + [pltpu.VMEM] + [pltpu.SMEM] * 2
    return pl.pallas_call(
        functools.partial(whole_kernel, inputs + outputs + list(scratch)),
        out_shape=(
            jax.ShapeDtypeStruct((rows, D), BF),
            jax.ShapeDtypeStruct((rows, D), F32),
            jax.ShapeDtypeStruct(own_params.shape, F32),
        ),
        in_specs=[pl.BlockSpec(memory_space=space) for space in spaces],
        out_specs=[pl.BlockSpec(memory_space=space) for space in (pl.ANY, pl.ANY, pltpu.VMEM)],
        scratch_shapes=list(scratch.values()),
        compiler_params=pltpu.CompilerParams(
            vmem_limit_bytes=VMEM_LIMIT, collective_id=0, has_side_effects=True
        ),
    )(tokens, cotangent, own_params, subnets, lengths)


def emit_kernel(out_from, grad_from, out_to, grad_to, out_hold, grad_hold, sems):
    pieces = []
    for index, (source, hold, target) in enumerate(((out_from, out_hold, out_to), (grad_from, grad_hold, grad_to))):
        step = source.shape[0] // EMIT
        for part in range(EMIT):
            rows, number = pl.ds(part * step, step), index * EMIT + part
            load = pltpu.make_async_copy(source.at[rows], hold.at[rows], sems.at[0, number])
            store = pltpu.make_async_copy(hold.at[rows], target.at[rows], sems.at[1, number])
            pieces.append((load, store))
    for load, _ in pieces:
        load.start()
    for load, store in pieces:
        load.wait()
        store.start()
    for _, store in pieces:
        store.wait()


def emit(*arrays):
    shapes = [jax.ShapeDtypeStruct(array.shape, array.dtype) for array in arrays]
    holds = [pltpu.VMEM(array.shape, array.dtype) for array in arrays]
    anywhere = pl.BlockSpec(memory_space=pl.ANY)
    return pl.pallas_call(
        emit_kernel,
        out_shape=shapes,
        in_specs=[anywhere] * 2,
        out_specs=[anywhere] * 2,
        scratch_shapes=holds + [pltpu.SemaphoreType.DMA((2, 2 * EMIT))],
    )(*arrays)


def local_kernel(names, *refs):
    refs = dict(zip(names, refs))
    refs["vec_par"] = refs["flat"].at[:, ROW_VEC:, :]
    layer = Layer(refs)
    layer.load()
    layer.start()
    layer.load_vectors()
    for pair in range(PAIRS):
        layer.query_key_value(pair)
    layer.attend_first(0)

    @pl.loop(0, HEADS - 1)
    def _(head):
        layer.attend_step(head, head + 1)

    layer.attend_step(HEADS - 1, None)
    layer.after_attention()
    layer.up_weights()
    layer.feed_forward(layer.down_weights)
    layer.down_grad(range(CHUNKS))
    layer.hidden_grad()
    layer.up_grad(0)
    layer.up_grad(D // 2)
    layer.first_norm_grad(range(LIVE // TILE))
    layer.out_grad()
    for pair in range(PAIRS):
        layer.pair_backward(pair, {})
    layer.input_grad_step({})
    layer.vector_grads()
    for block in range(PAIRS):
        layer.grads[block, ROW_VEC:, :] = layer.grad_vecs[:, block * 128 : block * 128 + 128].astype(BF)
    layer.finish()


def local_layer(tokens, cotangent, flat, subnets, lengths):
    rows = tokens.shape[0]
    scratch = scratch_refs(rows) | {"grad_vecs": pltpu.VMEM((16, D), F32)}
    inputs = ["tokens", "cotangent", "flat", "subnets", "lengths"]
    outputs = ["layer_out", "input_grad", "grads"]
    spaces = [pl.ANY] * 2 + [pltpu.VMEM] + [pltpu.SMEM] * 2
    return pl.pallas_call(
        functools.partial(local_kernel, inputs + outputs + list(scratch)),
        out_shape=(
            jax.ShapeDtypeStruct((rows, D), BF),
            jax.ShapeDtypeStruct((rows, D), F32),
            jax.ShapeDtypeStruct((PAIRS, ALL_ROWS, 128), BF),
        ),
        in_specs=[pl.BlockSpec(memory_space=space) for space in spaces],
        out_specs=[pl.BlockSpec(memory_space=space) for space in (pl.ANY, pl.ANY, pltpu.VMEM)],
        scratch_shapes=list(scratch.values()),
        compiler_params=pltpu.CompilerParams(vmem_limit_bytes=VMEM_LIMIT),
    )(tokens, cotangent, flat, subnets, lengths)


def on_device(tokens, cotangent, params, subnets, lengths):
    flat = lax.all_gather(params, ("group", "item"), axis=0, tiled=True)
    flat = flat.reshape(-1, D)
    whole = flat.shape[0]
    flat = jnp.pad(flat, ((0, ALL_ROWS - whole), (0, 0)))
    flat = jnp.swapaxes(flat.reshape(ALL_ROWS, PAIRS, 128), 0, 1)
    layer_out, input_grad, grads = local_layer(tokens[0], cotangent[0], flat, subnets, lengths[0])
    grad = jnp.swapaxes(grads[:, :whole], 0, 1).astype(F32).reshape(-1)
    param_grad = lax.psum_scatter(grad, ("group", "item"), scatter_dimension=0, tiled=True)
    return layer_out[None], input_grad[None], param_grad


def on_known_device(tokens, cotangent, params, subnets, lengths):
    count = params.shape[0]
    rows = -(-count // 1024) * 8
    own = jnp.pad(params, (0, rows * 128 - count)).reshape(rows, 128)
    layer_out, input_grad, own_grad = whole_layer(tokens[0], cotangent[0], own, subnets, lengths[0])
    layer_out, input_grad = emit(layer_out, input_grad)
    return layer_out[None], input_grad[None], own_grad.reshape(-1)[:count]


def solution(mesh):
    in_specs = (
        P("group", "item", None),
        P("group", "item", None),
        P(("group", "item")),
        P("group", None),
        P("group", "item", None),
    )
    out_specs = (P("group", "item", None), P("group", "item", None), P(("group", "item")))
    known = mesh.shape["group"] == 16 and mesh.shape["item"] == 2
    return jax.shard_map(
        on_known_device if known else on_device, mesh=mesh, in_specs=in_specs, out_specs=out_specs, check_vma=False
    )
```

```python
import functools

import jax
import jax.numpy as jnp
from jax import lax
from jax.experimental import pallas as pl
from jax.experimental.pallas import tpu as pltpu
from jax.sharding import PartitionSpec as P

HD = 64
HEADS = 6
D = 384
FF = 1536
LIVE = 960
PAIRS = HEADS // 2
CHUNKS = FF // D
BLOCK = 256
TILE = 320
WIDE = 512
BIG = 1e30
BF = jnp.bfloat16
F32 = jnp.float32
ROW_Q, ROW_K, ROW_V, ROW_O, ROW_UP, ROW_DOWN, ROW_VEC = 0, 384, 768, 1152, 1536, 3072, 4608
ALL_ROWS = 4624
STEP, FRAME, TWO, HALF = 144, 160, 304, 80
PLANES = 4
MESH = pl.DeviceIdType.MESH
VMEM_LIMIT = 61 * 2**20


def dot(left, right):
    return jnp.dot(left, right, preferred_element_type=F32)


def dot_nt(left, right):
    return lax.dot_general(left, right, (((1,), (1,)), ((), ())), preferred_element_type=F32)


def dot_tn(left, right):
    return lax.dot_general(left, right, (((0,), (0,)), ((), ())), preferred_element_type=F32)


def iota(shape, axis):
    return lax.broadcasted_iota(jnp.int32, shape, axis)


def below(shape, axis, bound):
    return jnp.where(iota(shape, axis) < bound, 1.0, 0.0).astype(F32)


def key_range(block):
    first = max(0, block * BLOCK - 479) // 96 * 96
    last = min(LIVE, -(-(block * BLOCK + BLOCK + 479) // 32) * 32)
    return first, last


def gelu_parts(z):
    cdf = 0.5 + 0.5 * lax.erf(z * 0.7071067811865476)
    bell = jnp.exp(-0.5 * (z * z)) * 0.3989422804014327
    return z * cdf, cdf + z * bell


def norm_forward(hidden, gain, shift, feature, inv_count):
    center = (hidden - jnp.sum(hidden * feature, axis=-1, keepdims=True) * inv_count) * feature
    inverse = lax.rsqrt(jnp.sum(center * center, axis=-1, keepdims=True) * inv_count + 1e-05)
    normed = center * inverse
    return normed * gain + shift, normed, inverse


def norm_backward(grad, normed, inverse, gain, feature, inv_count):
    scaled = grad * gain
    first = jnp.sum(scaled, axis=-1, keepdims=True) * inv_count
    second = jnp.sum(scaled * normed, axis=-1, keepdims=True) * inv_count
    return inverse * (scaled - first - normed * second) * feature


def col_sum(value):
    return jnp.sum(value, axis=0, keepdims=True)


class Layer:
    def __init__(self, refs):
        self.__dict__.update(refs)
        self.cot = self.layer_out
        self.d_a, self.dot_t = self.xm, self.v_t
        for index, name in enumerate(("norm_one", "normed_one", "grad_second")):
            setattr(self, name, self.hold.at[:, index * D : index * D + D])
        self.lanes = self.expo.shape[2]
        width, heads, hidden = self.subnets[0, 0], self.subnets[0, 1], self.subnets[0, 2]
        self.width, self.attend, self.hidden = width, heads * HD, hidden
        self.inv_count = 1.0 / jnp.full((1, 1), width, jnp.int32).astype(F32)

    def row_mask(self, cols, bound, offset=0):
        return jnp.where(iota((1, cols), 1) + offset < bound, 1.0, 0.0).astype(F32)

    def col_mask(self, rows, bound, offset=0):
        return jnp.where(iota((rows, 1), 0) + offset < bound, 1.0, 0.0).astype(F32)

    def feature(self):
        return self.row_mask(D, self.width)

    def vector(self, index):
        mask = self.attend if index < 2 else self.width
        return self.vecs[4 + index : 5 + index, :] * self.row_mask(D, mask)

    def add_sum(self, index, value, first):
        part = value[:8, :]
        for start in range(8, value.shape[0], 8):
            part = part + value[start : start + 8, :]
        if first:
            self.sums[index] = part
        else:
            self.sums[index] += part


    def tokens_copy(self):
        return pltpu.make_async_copy(self.tokens.at[pl.ds(0, LIVE)], self.xm, self.io_sem.at[0])

    def cotangent_copy(self):
        return pltpu.make_async_copy(self.cotangent.at[pl.ds(0, LIVE)], self.cot.at[pl.ds(0, LIVE)], self.io_sem.at[1])

    def load(self):
        self.tokens_copy().start()
        self.cotangent_copy().start()

    def start(self):
        pad = self.lanes - LIVE
        self.input_grad[LIVE:, :] = jnp.zeros((self.input_grad.shape[0] - LIVE, D), F32)
        self.cot[LIVE:, :] = jnp.zeros((self.cot.shape[0] - LIVE, D), BF)
        self.dot_t[:, :, LIVE:] = jnp.zeros((HEADS, HD, pad), BF)
        self.q_t[:, :, LIVE:] = jnp.zeros((HEADS, HD, pad), BF)
        self.delta[:, :, LIVE:] = jnp.zeros((HEADS, 1, pad), F32)
        self.do_s[LIVE:, :] = jnp.zeros((pad, D), BF)
        self.q_rows[LIVE:, :] = jnp.zeros((pad, D), BF)
        ends = []
        total = 0
        for index in range(4):
            total = total + self.lengths[0, index]
            ends.append(total)
        lane = iota((HD, self.lanes), 1)
        seg = sum((lane >= end).astype(jnp.int32) for end in ends)
        part = iota((HD, self.lanes), 0)
        self.far[...] = jnp.where((part < 4) & (part != seg), -BIG, 0.0).astype(BF)
        row = iota((LIVE, 128), 0)
        seg = sum((row >= end).astype(jnp.int32) for end in ends[:3])
        self.hot[...] = jnp.where(iota((LIVE, 128), 1) - HD == seg, 1.0, 0.0).astype(BF)
        fe = self.feature().astype(BF)
        self.tokens_copy().wait()
        for rows in row_tiles():
            self.xm[rows, :] = self.xm[rows, :] * fe
        for part in range(PAIRS):
            lanes = slice(part * 128, part * 128 + 128)
            self.xt[lanes, :] = self.xm[:, lanes].T

    def load_vectors(self):
        for part in range(PAIRS):
            lanes = slice(part * 128, part * 128 + 128)
            self.vecs[:, lanes] = self.vec_par[part].astype(F32)
        for chunk in range(CHUNKS):
            cols = slice(chunk * D, chunk * D + D)
            self.bias[:, cols] = self.vecs[chunk : chunk + 1, :] * self.row_mask(D, self.hidden, chunk * D)


    def query_key_value(self, pair):
        lanes = slice(pair * 128, pair * 128 + 128)
        mask = self.col_mask(D, self.width) * self.row_mask(128, self.attend, pair * 128)
        for index, row in enumerate((ROW_Q, ROW_K, ROW_V)):
            weight = (self.flat[pair, row : row + D, :].astype(F32) * mask).astype(BF)
            self.w_qkv[:, pair * D + index * 128 : pair * D + index * 128 + 128] = weight
        bias_q, bias_v = self.vector(0)[:, lanes], self.vector(1)[:, lanes]
        weight = self.w_qkv[:, pair * D : pair * D + D]
        for start in range(0, LIVE, BLOCK):
            rows = slice(start, min(start + BLOCK, LIVE))
            size = rows.stop - rows.start
            even = iota((size, 128), 1) < HD
            out = dot(self.xm[rows, :], weight)
            q = (out[:, :128] + bias_q).astype(BF)
            self.q_rows[rows, lanes] = q
            k32 = out[:, 128:256]
            k = k32.astype(BF)
            hot = self.hot[rows, :]
            for head, moved in ((2 * pair, k32), (2 * pair + 1, pltpu.roll(k32, HD, 1))):
                place, cols = self.keys_place(head)
                place[rows, cols] = jnp.where(even, moved, hot.astype(F32)).astype(BF)
            v = (out[:, 256:] + bias_v).astype(BF)
            self.v_rows[rows, lanes] = v
            turned = (q * jnp.asarray(0.125, BF)).T
            self.q_t[2 * pair, :, rows] = turned[:HD, :]
            self.q_t[2 * pair + 1, :, rows] = turned[HD:, :]
            turned = k.T
            self.k_t[2 * pair, :, rows] = turned[:HD, :]
            self.k_t[2 * pair + 1, :, rows] = turned[HD:, :]
            turned = v.T
            self.v_t[2 * pair, :, rows] = turned[:HD, :]
            self.v_t[2 * pair + 1, :, rows] = turned[HD:, :]

    def keys_place(self, head):
        first = head % PAIRS * 128
        return (self.d_f if head < PAIRS else self.norm_low), slice(first, first + 128)

    def score(self, head, block):
        cols = slice(block * BLOCK, block * BLOCK + BLOCK)
        first, last = key_range(block)
        right = jnp.concatenate([self.q_t[head, :, cols], self.far[:, cols]], axis=0)
        place, lanes = self.keys_place(head)
        self.hold[first:last, cols] = dot(place[first:last, lanes], right)

    def soft(self, head, block):
        cols = slice(block * BLOCK, block * BLOCK + BLOCK)
        first, last = key_range(block)
        scores = self.hold[first:last, cols]
        expo = jnp.exp(scores - jnp.max(scores, axis=0, keepdims=True))
        inv = 1.0 / jnp.sum(expo, axis=0, keepdims=True)
        expo = expo.astype(BF)
        self.expo[head, first:last, cols] = expo
        self.inv[head, :, cols] = inv
        return expo, inv

    def attend_first(self, head):
        for block in range(self.lanes // BLOCK):
            self.score(head, block)

    def attend_step(self, head, after):
        for block in range(self.lanes // BLOCK):
            cols = slice(block * BLOCK, block * BLOCK + BLOCK)
            first, last = key_range(block)
            expo, inv = self.soft(head, block)
            if after is not None:
                self.score(after, block)
            mixed = dot(self.v_t[head, :, first:last], expo) * inv
            self.o_t[head, :, cols] = mixed.astype(BF)

    def after_attention(self):
        mask = self.col_mask(D, self.attend) * self.feature()
        for part in range(PAIRS):
            lanes = slice(part * 128, part * 128 + 128)
            rows = self.flat[part, ROW_O : ROW_O + D, :].astype(F32)
            self.w_out[:, lanes] = (rows * mask[:, lanes]).astype(BF)
        fe, bias, gain, shift = self.feature(), self.vector(2), self.vector(3), self.vector(4)
        for start in range(0, LIVE, BLOCK):
            size = min(BLOCK, LIVE - start)
            rows = slice(start, start + size)
            mixed = self.o_t[:, :, start : start + BLOCK].reshape(D, BLOCK)
            attended = dot_tn(mixed, self.w_out[...])[:size, :]
            hidden = self.xm[rows, :].astype(F32) + attended + bias
            norm, normed, inverse = norm_forward(hidden, gain, shift, fe, self.inv_count)
            self.norm_one[rows, :] = norm
            self.normed_one[rows, :] = normed
            self.inverse_one[rows, :] = jnp.broadcast_to(inverse, (size, 128))
            self.norm_low[rows, :] = norm.astype(BF)

    def up_weights(self):
        for part in range(PAIRS):
            self.wide[part] = self.flat[part, ROW_UP : ROW_UP + FF, :].astype(F32)
        for chunk in range(CHUNKS):
            mask = self.col_mask(D, self.width) * self.row_mask(D, self.hidden, chunk * D)
            for part in range(PAIRS):
                lanes = slice(part * 128, part * 128 + 128)
                piece = self.wide[part, pl.ds(chunk, D, stride=CHUNKS), :]
                self.w_up[:, chunk * D + part * 128 : chunk * D + part * 128 + 128] = (
                    piece * mask[:, lanes]
                ).astype(BF)

    def down_weights(self):
        mask = self.feature()
        for chunk in range(CHUNKS):
            rows = slice(chunk * D, chunk * D + D)
            hidden = self.col_mask(D, self.hidden, chunk * D)
            for part in range(PAIRS):
                lanes = slice(part * 128, part * 128 + 128)
                piece = self.flat[part, ROW_DOWN + chunk * D : ROW_DOWN + chunk * D + D, :].astype(F32)
                self.w_down[rows, lanes] = (piece * (hidden * mask[:, lanes])).astype(BF)

    def up_tile(self, rows):
        low = self.norm_low[rows, :]
        for start in range(0, FF, BLOCK):
            cols = slice(start, start + BLOCK)
            act, slope = gelu_parts(dot(low, self.w_up[:, cols]) + self.bias[:, cols])
            self.act[rows, cols] = act.astype(BF)
            self.slope[rows, cols] = slope.astype(BF)

    def down_tile(self, rows):
        fe = self.feature()
        bias, gain, shift = self.vector(5), self.vector(6), self.vector(7)
        second = self.norm_one[rows, :] + dot(self.act[rows, :FF], self.w_down[...]) + bias
        result, normed, inverse = norm_forward(second, gain, shift, fe, self.inv_count)
        grad = self.cot[rows, :].astype(F32)
        self.cot[rows, :] = result.astype(BF)
        grad_second = norm_backward(grad, normed, inverse, gain, fe, self.inv_count)
        self.grad_second[rows, :] = grad_second
        low = grad_second.astype(BF)
        self.d_f[rows, :] = low
        first = rows.start == 0
        self.add_sum(10, grad * normed, first)
        self.add_sum(11, grad, first)
        self.add_sum(9, low.astype(F32), first)

    def feed_forward(self, before_down):
        for rows in row_tiles():
            self.up_tile(rows)
        before_down()
        self.cotangent_copy().wait()
        for rows in row_tiles():
            self.down_tile(rows)


    def down_grad(self, start, stop):
        fe = self.feature()
        for first in range(start, stop, WIDE):
            size = min(WIDE, stop - first)
            grad = dot_tn(self.d_f[...], self.act[:, first : first + size]).astype(BF).T
            grad = grad * (self.col_mask(size, self.hidden, first) * fe).astype(BF)
            for part in range(PAIRS):
                lanes = slice(part * 128, part * 128 + 128)
                self.grads[part, ROW_DOWN + first : ROW_DOWN + first + size, :] = grad[:, lanes]

    def hidden_tile(self, rows):
        d_f = self.d_f[rows, :]
        for start in range(0, FF, BLOCK):
            cols = slice(start, start + BLOCK)
            grad = dot_nt(d_f, self.w_down[cols, :])
            dz = (grad * self.slope[rows, cols].astype(F32)).astype(BF)
            self.slope[rows, cols] = dz
            part = dz[:8, :].astype(F32)
            for row in range(8, rows.stop - rows.start, 8):
                part = part + dz[row : row + 8, :].astype(F32)
            if rows.start == 0:
                self.hidden_sums[:, cols] = part
            else:
                self.hidden_sums[:, cols] += part

    def first_norm_tile(self, rows):
        gain, fe = self.vector(3), self.feature()
        normed = self.normed_one[rows, :]
        grad = self.grad_second[rows, :] + dot_nt(self.slope[rows, :], self.w_up[...])
        grad_first = norm_backward(grad, normed, self.inverse_one[rows, :1], gain, fe, self.inv_count)
        self.norm_one[rows, :] = grad_first
        low = grad_first.astype(BF)
        self.d_a[rows, :] = low
        first = rows.start == 0
        self.add_sum(7, grad * normed, first)
        self.add_sum(8, grad, first)
        self.add_sum(6, low.astype(F32), first)

    def hidden_grad(self):
        for rows in row_tiles():
            self.hidden_tile(rows)

    def first_norm_grad(self, tiles):
        for index in tiles:
            self.first_norm_tile(row_tiles()[index])

    def up_grad(self, start):
        half = D // 2
        low = self.norm_low[:, start : start + half]
        for first in range(0, FF, WIDE):
            mask = self.col_mask(half, self.width, start) * self.row_mask(WIDE, self.hidden, first)
            grad = dot_tn(low, self.slope[:, first : first + WIDE]) * mask
            for lane in range(0, WIDE, 128):
                chunk, part = (first + lane) // D, (first + lane) % D // 128
                rows = pl.ds(start * CHUNKS + chunk, half, stride=CHUNKS)
                self.wide[part, rows, :] = grad[:, lane : lane + 128]
        rows = slice(start * CHUNKS, (start + half) * CHUNKS)
        for part in range(PAIRS):
            self.grads[part, ROW_UP + rows.start : ROW_UP + rows.stop, :] = self.wide[part, rows, :].astype(BF)

    def out_grad(self):
        fe = self.feature()
        d_a = self.d_a[...]
        half = D // 2
        for start in (0, half):
            rows = slice(start, start + half)
            heads = range(start // HD, (start + half) // HD)
            mask = self.col_mask(half, self.attend, start) * fe
            o_t = self.o_t[heads.start : heads.stop, :, :LIVE].reshape(half, LIVE)
            grad = (dot(o_t, d_a) * mask).astype(BF)
            for part in range(PAIRS):
                lanes = slice(part * 128, part * 128 + 128)
                self.grads[part, ROW_O + start : ROW_O + start + half, :] = grad[:, lanes]
            mixed = dot_nt(self.w_out[rows, :], d_a)
            for head in heads:
                own = mixed[head * HD - start : head * HD - start + HD, :] * self.inv[head, :, :LIVE]
                self.delta[head, :, :LIVE] = col_sum(own * self.o_t[head, :, :LIVE].astype(F32))
                self.dot_t[head, :, :LIVE] = own.astype(BF)
        for pair in range(PAIRS):
            both = self.dot_t[2 * pair : 2 * pair + 2, :, :LIVE].reshape(128, LIVE)
            self.do_s[:LIVE, pair * 128 : pair * 128 + 128] = both.T

    def score_place(self, odd, block):
        if not odd:
            return self.act, block * BLOCK
        return ((self.act, 4 * BLOCK), (self.act, 5 * BLOCK), (self.slope, PAIRS * D), (self.d_f, 0))[block]

    def prob_grad(self, pair, odd, block):
        cols = slice(block * BLOCK, block * BLOCK + BLOCK)
        first, last = key_range(block)
        right = self.dot_t[2 * pair + odd, :, cols]
        none = jnp.zeros_like(right)
        right = jnp.concatenate([none, right] if odd else [right, none], axis=0)
        return dot(self.v_rows[first:last, pair * 128 : pair * 128 + 128], right)

    def score_grad(self, pair, odd, block, grad):
        head = 2 * pair + odd
        cols = slice(block * BLOCK, block * BLOCK + BLOCK)
        first, last = key_range(block)
        grad = self.expo[head, first:last, cols].astype(F32) * (grad - self.delta[head, :, cols])
        grad = grad.astype(BF)
        place, start = self.score_place(odd, block)
        place[first:last, start : start + BLOCK] = grad
        return grad

    def query_grad(self, pair, odd, block, grad):
        head = 2 * pair + odd
        cols = slice(block * BLOCK, block * BLOCK + BLOCK)
        first, last = key_range(block)
        dq = dot(self.k_t[head, :, first:last], grad) * 0.125
        self.dq_t[odd * HD : odd * HD + HD, cols] = dq.astype(BF)

    def pair_backward(self, pair, hooks):
        lanes = slice(pair * 128, pair * 128 + 128)
        blocks = self.lanes // BLOCK
        ranges = [key_range(block) for block in range(blocks)]
        edges = sorted({edge for both in ranges for edge in both})
        cuts = []
        for low, high in zip(edges[:-1], edges[1:]):
            used = [b for b in range(blocks) if ranges[b][0] <= low and high <= ranges[b][1]]
            cuts.append((slice(low, high), slice(used[0] * BLOCK, used[-1] * BLOCK + BLOCK)))
        own = [jnp.where((iota((1, 128), 1) >= HD) == bool(odd), 1.0, 0.0).astype(BF) for odd in (0, 1)]
        d_out = [self.do_s[:, lanes] * own[odd] for odd in (0, 1)]
        items = [(odd, block) for odd in (0, 1) for block in range(blocks)]
        grad = self.prob_grad(pair, *items[0])
        for index, (odd, block) in enumerate(items):
            if index % 2 == 0 and index // 2 < len(cuts):
                rows, span = cuts[index // 2]
                dv = sum(dot(self.expo[2 * pair + odd_, rows, span], d_out[odd_][span]) for odd_ in (0, 1))
                self.slope[rows, pair * D + 256 : pair * D + 384] = dv.astype(BF)
            after = self.prob_grad(pair, *items[index + 1]) if index + 1 < len(items) else None
            low = self.score_grad(pair, odd, block, grad)
            grad = after
            self.query_grad(pair, odd, block, low)
            if index in hooks:
                hooks[index]()
        queries = [self.q_rows[:, lanes] * own[odd] for odd in (0, 1)]
        for rows, span in cuts:
            dk = 0.0
            for odd in (0, 1):
                places = [self.score_place(odd, block) for block in range(span.start // BLOCK, span.stop // BLOCK)]
                first = 0
                for last in range(1, len(places) + 1):
                    if last == len(places) or places[last][0] is not places[first][0]:
                        place, start = places[first]
                        begin, size = span.start + first * BLOCK, (last - first) * BLOCK
                        dk = dk + dot(place[rows, start : start + size], queries[odd][begin : begin + size])
                        first = last
            self.slope[rows, pair * D + 128 : pair * D + 256] = (dk * 0.125).astype(BF)
        self.slope[:, pair * D : pair * D + 128] = self.dq_t[:, :LIVE].T
        mask = self.col_mask(D, self.width) * self.row_mask(128, self.attend, pair * 128)
        all_three = self.slope[:, pair * D : pair * D + D]
        grad = dot(self.xt[...], all_three)
        for index, row in enumerate((ROW_Q, ROW_K, ROW_V)):
            self.grads[pair, row : row + D, :] = (grad[:, index * 128 : index * 128 + 128] * mask).astype(BF)
        totals = dot(jnp.ones((8, LIVE), BF), all_three)
        self.sums[4, :, lanes] = totals[:, :128] * 0.125
        self.sums[5, :, lanes] = totals[:, 256:] * 0.125

    def input_grad_step(self, hooks):
        fe = self.feature()
        for index, rows in enumerate(row_tiles()):
            total = self.norm_one[rows, :] + dot_nt(self.slope[rows, : PAIRS * D], self.w_qkv[...])
            self.input_grad[rows, :] = total * fe
            if index in hooks:
                hooks[index]()

    def vector_grads(self):
        for index in range(12):
            if index < CHUNKS:
                total = jnp.sum(self.hidden_sums[:, index * D : index * D + D], axis=0, keepdims=True)
                mask = self.row_mask(D, self.hidden, index * D)
            else:
                total = jnp.sum(self.sums[index], axis=0, keepdims=True)
                mask = self.row_mask(D, self.attend if index < 6 else self.width)
            self.grad_vecs[index : index + 1, :] = total * mask
        self.grad_vecs[12:, :] = jnp.zeros((4, D), F32)


def row_tiles():
    return [slice(start, min(start + TILE, LIVE)) for start in range(0, LIVE, TILE)]


def scratch_refs():
    vmem = pltpu.VMEM
    lanes = -(-LIVE // BLOCK) * BLOCK
    return {
        "xm": vmem((LIVE, D), BF),
        "hold": vmem((LIVE, 3 * D), F32),
        "xt": vmem((D, LIVE), BF),
        "hot": vmem((LIVE, 128), BF),
        "far": vmem((HD, lanes), BF),
        "vecs": vmem((16, D), F32),
        "bias": vmem((1, FF), F32),
        "sums": vmem((12, 8, D), F32),
        "hidden_sums": vmem((8, FF), F32),
        "w_qkv": vmem((D, PAIRS * D), BF),
        "w_out": vmem((D, D), BF),
        "w_up": vmem((D, FF), BF),
        "w_down": vmem((FF, D), BF),
        "wide": vmem((PAIRS, FF, 128), F32),
        "q_rows": vmem((lanes, D), BF),
        "q_t": vmem((HEADS, HD, lanes), BF),
        "k_t": vmem((HEADS, HD, LIVE), BF),
        "v_rows": vmem((LIVE, D), BF),
        "v_t": vmem((HEADS, HD, lanes), BF),
        "expo": vmem((HEADS, LIVE, lanes), BF),
        "inv": vmem((HEADS, 1, lanes), F32),
        "o_t": vmem((HEADS, HD, lanes), BF),
        "inverse_one": vmem((LIVE, 128), F32),
        "norm_low": vmem((LIVE, D), BF),
        "act": vmem((LIVE, FF), BF),
        "slope": vmem((LIVE, FF), BF),
        "d_f": vmem((LIVE, D), BF),
        "do_s": vmem((lanes, D), BF),
        "delta": vmem((HEADS, 1, lanes), F32),
        "dq_t": vmem((128, lanes), BF),
        "io_sem": pltpu.SemaphoreType.DMA((3,)),
    }


class Exchange:
    def __init__(self, refs):
        self.__dict__.update(refs)
        group, self.x = lax.axis_index("group"), lax.axis_index("item")
        self.z, self.y, self.c = group // 4, (group // 2) % 2, group % 2
        self.spot = 2 * self.y + self.x
        self.shard = 2 * group + self.x
        self.corner = (self.c == 1) & (self.spot == 3)

    def device(self, z, y, c, x):
        return (z * 4 + y * 2 + c, x)

    def line(self, step):
        return self.device((self.z + step) % PLANES, self.y, self.c, self.x)

    def plane_peer(self, step):
        y, x = (self.y + step // 4) % 2, (self.x + step % 2) % 2
        return self.device(self.z, y, (self.c + step // 2 % 2) % 2, x)

    def chip_peer(self, step):
        y, x = (self.y + step // 2) % 2, (self.x + step % 2) % 2
        return self.device(self.z, y, self.c, x)

    def spot_of(self, step):
        return 2 * ((self.y + step // 2) % 2) + (self.x + step % 2) % 2

    def core_peer(self):
        return self.device(self.z, self.y, 1 - self.c, self.x)

    def greet(self):
        barrier = pltpu.get_barrier_semaphore()
        peers = [self.line(step) for step in (1, 2, 3)] + [self.plane_peer(step) for step in range(1, 8)]
        for peer in peers:
            pl.semaphore_signal(barrier, inc=1, device_id=peer, device_id_type=MESH)

    def greeted(self):
        pl.semaphore_wait(pltpu.get_barrier_semaphore(), 10)

    def copy(self, source, target, send, recv, peer):
        return pltpu.make_async_remote_copy(
            src_ref=source, dst_ref=target, send_sem=send, recv_sem=recv, device_id=peer, device_id_type=MESH
        )


    def offsets(self):
        shift = STEP * self.shard
        return shift // 128, shift % 128

    def params_copy(self):
        return pltpu.make_async_copy(self.own_params, self.shard_flat, self.io_sem.at[2])

    def frame_own(self):
        self.params_copy().wait()
        rows, count = self.shard_sum.shape[1], self.shard_flat.shape[0]
        full, rest = count // 128, count % 128
        spread = self.shard_sum.at[0]
        spread[:full, :] = self.shard_flat[pl.ds(0, full * 128)].reshape(full, 128).astype(F32)
        spread[full:, :] = jnp.zeros((rows - full, 128), F32)
        if rest:
            spread[full : full + 1, :rest] = self.shard_flat[pl.ds(full * 128, rest)].reshape(1, rest).astype(F32)
        up, across = self.offsets()
        turned = pltpu.roll(spread[...], across, 1)
        late = iota((rows, 128), 1) >= across
        same = jnp.where(late, turned, 0.0).astype(BF)
        carried = jnp.where(late, 0.0, turned).astype(BF)
        gap = 3 * iota((FRAME, rows), 0) - up - iota((FRAME, rows), 1)
        for part in range(PAIRS):
            here = jnp.where(gap == -part, 1.0, 0.0).astype(BF)
            after = jnp.where(gap == 1 - part, 1.0, 0.0).astype(BF)
            frame = dot(here, same) + dot(after, carried)
            self.land[self.z, part, self.c, self.spot] = frame.astype(BF)

    def vectors_line(self, step):
        sems = self.par_send.at[step - 1], self.par_recv.at[0]
        return self.copy(self.vec_par, self.vec_par, *sems, self.line(step))

    def vectors_plane(self, step):
        sems = self.par_send.at[step + 2], self.par_recv.at[1]
        return self.copy(self.vec_par, self.vec_par, *sems, self.plane_peer(step))

    def send_vectors_line(self):
        @pl.when(self.corner & (self.z == PLANES - 1))
        def _():
            self.vec_par[...] = self.land[PLANES - 1, :, 1, 3, STEP:, :]
            for step in (1, 2, 3):
                self.vectors_line(step).start()

    def send_vectors_plane(self):
        @pl.when(self.corner & (self.z != PLANES - 1))
        def _():
            self.vectors_line(1).wait_recv()

        @pl.when(self.corner)
        def _():
            for step in range(1, 8):
                self.vectors_plane(step).start()

    def finish_vectors_plane(self):
        @pl.when(jnp.logical_not(self.corner))
        def _():
            self.vectors_plane(1).wait_recv()

    def parts(self, plane, part):
        return pl.ds(part, 1) if isinstance(plane, int) and plane == 0 else slice(None)

    def blocks(self, plane, part):
        return [part] if plane == 0 else range(PAIRS)

    def item(self, plane, part):
        return part if isinstance(plane, int) and plane == 0 else 2 + plane

    def gather_line(self, plane, part, step):
        piece = self.land.at[plane, self.parts(plane, part), self.c, self.spot]
        sems = self.line_send.at[part, step - 1], self.line_recv.at[self.item(plane, part)]
        return self.copy(piece, piece, *sems, self.line(step))

    def send_line(self, plane, part, steps):
        @pl.when(self.z == plane)
        def _():
            for step in steps:
                self.gather_line(plane, part, step).start()

    def gather_all(self, part, step, spot):
        piece = self.land.at[0, pl.ds(part, 1), self.c, spot]
        sems = self.flat_send.at[3 * part + step - 1], self.flat_recv.at[3 * part + step - 1]
        return self.copy(piece, piece, *sems, self.chip_peer(step))

    def gather_next(self, plane, step, spot):
        piece = self.land.at[plane, :, self.c, spot]
        index = 5 + 4 * plane + step - 1
        return self.copy(piece, piece, self.flat_send.at[index], self.flat_recv.at[index], self.chip_peer(step))

    def gather_half(self, plane, step, spot):
        rows = pl.ds((2 - step) * HALF, HALF)
        piece = self.land.at[plane, :, self.c, spot, rows]
        index = 5 + 4 * plane + step + 1
        return self.copy(piece, piece, self.flat_send.at[index], self.flat_recv.at[index], self.chip_peer(step))

    def wait_line(self, plane, part):
        @pl.when(self.z != plane)
        def _():
            self.gather_line(plane, part, 1).wait_recv()

    def send_all(self, part):
        self.wait_line(0, part)
        for step in (3, 2, 1):
            self.gather_all(part, step, self.spot).start()

    def plane_order(self):
        second = jnp.where(self.z == 0, 3, jnp.where(self.z == 1, 2, 1))
        third = jnp.where(self.z % 3 == 0, 2, 3)
        return jnp.maximum(self.z, 1), second, third

    def own_first(self, action):
        @pl.when(self.z != 0)
        def _():
            action()

    def others_first(self, *actions):
        @pl.when(self.z == 0)
        def _():
            for action in actions:
                action()

    def receive_line(self, plane):
        self.copy_line(plane).wait_recv()

    def copy_line(self, plane):
        piece = self.land.at[plane, :, self.c, self.spot]
        return self.copy(piece, piece, self.line_send.at[1, 0], self.line_recv.at[2 + plane], self.line(1))

    def send_next(self, plane):
        for step in (2, 1):
            self.gather_next(plane, step, self.spot).start()

    def send_halves(self, plane):
        self.gather_next(plane, 1, self.spot_of(1)).wait_recv()
        self.gather_half(plane, 2, self.spot_of(1)).start()
        self.gather_next(plane, 2, self.spot_of(2)).wait_recv()
        self.gather_half(plane, 1, self.spot_of(2)).start()

    def gather_core(self, plane, part, core):
        piece = self.land.at[plane, self.parts(plane, part), core]
        item = self.item(plane, part)
        return self.copy(piece, piece, self.core_send.at[item], self.core_recv.at[item], self.core_peer())

    def send_core(self, plane, part=0):
        if isinstance(plane, int) and plane == 0:
            for step in (3, 2, 1):
                self.gather_all(part, step, self.spot_of(step)).wait_recv()
        else:
            for step in (2, 1):
                self.gather_half(plane, step, self.spot_of(3)).wait_recv()
        self.gather_core(plane, part, self.c).start()

    def finish_gather(self, plane, part=0):
        self.gather_core(plane, part, 1 - self.c).wait_recv()
        for place in range(8):
            y, c, x = place // 4, (place // 2) % 2, place % 2
            chunk = 8 * plane + place
            for block in self.blocks(plane, part):
                frame = self.land[plane, block, c, 2 * y + x]
                self.flat[block, chunk * STEP : chunk * STEP + STEP, :] = frame[:STEP, :]
                if chunk:
                    before = (chunk - 1) % 8
                    spot = 2 * (before // 4) + before % 2
                    tail = self.land[(chunk - 1) // 8, block, (before // 2) % 2, spot, STEP:, :]
                    both = tail + frame[: FRAME - STEP, :]
                    self.flat[block, chunk * STEP : chunk * STEP + FRAME - STEP, :] = both

    def drain_gather(self):
        @pl.when(self.corner & (self.z == PLANES - 1))
        def _():
            for step in (1, 2, 3):
                self.vectors_line(step).wait_send()

        @pl.when(self.corner)
        def _():
            for step in range(1, 8):
                self.vectors_plane(step).wait_send()

        for plane in range(PLANES):
            for part in range(PAIRS if plane == 0 else 1):

                @pl.when(self.z == plane)
                def _():
                    for step in (1, 2, 3):
                        self.gather_line(plane, part, step).wait_send()

                if plane == 0:
                    for step in (1, 2, 3):
                        self.gather_all(part, step, self.spot).wait_send()
                else:
                    for step in (1, 2):
                        self.gather_next(plane, step, self.spot).wait_send()
                        self.gather_half(plane, step, self.spot).wait_send()
                self.gather_core(plane, part, self.c).wait_send()


    def sum_core(self, plane, part, y):
        row = pl.multiple_of(STEP * (8 * plane + 4 * y + 2 * (1 - self.c)), 16)
        parts, item = self.parts(plane, part), 2 * self.item(plane, part) + y
        return self.copy(
            self.grads.at[parts, pl.ds(row, TWO)],
            self.core_land.at[plane % 3, y, parts],
            self.sum_core_send.at[item],
            self.sum_core_recv.at[item],
            self.core_peer(),
        )

    def sum_all(self, part, step):
        index = 3 * part + step - 1
        return self.copy(
            self.land.at[0, pl.ds(part, 1), 0, self.spot_of(step)],
            self.all_land.at[step - 1, pl.ds(part, 1)],
            self.sum_flat_send.at[index],
            self.sum_flat_recv.at[index],
            self.chip_peer(step),
        )

    def sum_half(self, plane, step):
        index = 5 + 4 * plane + step - 1
        return self.copy(
            self.land.at[plane, :, 0, self.spot_of(3), pl.ds((step - 1) * HALF, HALF)],
            self.half_land.at[plane - 1, step - 1],
            self.sum_flat_send.at[index],
            self.sum_flat_recv.at[index],
            self.chip_peer(step),
        )

    def sum_next(self, plane, step):
        index = 5 + 4 * plane + step + 1
        return self.copy(
            self.land.at[plane, :, 0, self.spot_of(step)],
            self.next_land.at[plane - 1, step - 1],
            self.sum_flat_send.at[index],
            self.sum_flat_recv.at[index],
            self.chip_peer(step),
        )

    def sum_line(self, plane, part, slot):
        parts, item = self.parts(plane, part), self.item(plane, part)
        return self.copy(
            self.plane_sum.at[plane, parts],
            self.line_land.at[slot, parts],
            self.sum_line_send.at[item],
            self.sum_line_recv.at[3 * part + slot],
            self.device(plane, self.y, self.c, self.x),
        )

    def reduce_core(self, plane, part=0):
        for y in (0, 1):
            self.sum_core(plane, part, y).start()

    def add_core(self, plane, part):
        for y in (0, 1):
            self.sum_core(plane, part, y).wait_recv()
            for block in self.blocks(plane, part):
                for x in (0, 1):
                    row = pl.multiple_of(STEP * (8 * plane + 4 * y + 2 * self.c + x), 16)
                    own = self.grads[block, pl.ds(row, FRAME), :]
                    other = self.core_land[plane % 3, y, block, x * STEP : x * STEP + FRAME, :]
                    self.land[plane, block, 0, 2 * y + x] = own + other

    def reduce_all(self, part):
        self.add_core(0, part)
        for step in (3, 2, 1):
            self.sum_all(part, step).start()

    def reduce_halves(self, plane):
        self.add_core(plane, 0)
        for step in (1, 2):
            self.sum_half(plane, step).start()

    def reduce_next(self, plane):
        for step in (1, 2):
            self.sum_half(plane, step).wait_recv()
            rows = slice((step - 1) * HALF, step * HALF)
            spot = self.spot_of(3 - step)
            for block in range(PAIRS):
                own = self.land[plane, block, 0, spot, rows, :]
                self.land[plane, block, 0, spot, rows, :] = own + self.half_land[plane - 1, step - 1, block]
            self.sum_next(plane, 3 - step).start()

    def reduce_line(self, plane, part=0):
        if plane == 0:
            for step in (1, 2, 3):
                self.sum_all(part, step).wait_recv()
        else:
            for step in (1, 2):
                self.sum_next(plane, step).wait_recv()
        for block in self.blocks(plane, part):
            total = self.land[plane, block, 0, self.spot]
            if plane == 0:
                total = (total + self.all_land[0, block]) + (self.all_land[1, block] + self.all_land[2, block])
            else:
                total = total + (self.next_land[plane - 1, 0, block] + self.next_land[plane - 1, 1, block])
            self.plane_sum[plane, block] = total

        @pl.when(self.z != plane)
        def _():
            self.sum_line(plane, part, (self.z - plane + 2 * PLANES - 1) % PLANES).start()

    def vector_core(self):
        peer = self.core_peer()
        return self.copy(self.grad_vecs, self.vec_core, self.vec_send.at[0], self.vec_recv.at[0], peer)

    def vector_flat(self, slot):
        peer = self.device(self.z, 1, 1, 1)
        return self.copy(self.vec_sum, self.vec_flat.at[slot], self.vec_send.at[1], self.vec_recv.at[1 + slot], peer)

    def vector_line(self, slot):
        peer = self.device(PLANES - 1, 1, 1, 1)
        return self.copy(self.vec_sum, self.vec_line.at[slot], self.vec_send.at[2], self.vec_recv.at[4 + slot], peer)

    def reduce_vectors_core(self):
        @pl.when(self.c == 0)
        def _():
            self.vector_core().start()

    def reduce_vectors_flat(self):
        @pl.when(self.c == 1)
        def _():
            self.vector_core().wait_recv()
            self.vec_sum[...] = self.grad_vecs[...] + self.vec_core[...]

            @pl.when(self.spot != 3)
            def _():
                self.vector_flat(2 - self.spot).start()

    def reduce_vectors_line(self):
        @pl.when(self.corner)
        def _():
            for slot in range(3):
                self.vector_flat(slot).wait_recv()
            self.vec_sum[...] = self.vec_sum[...] + self.vec_flat[0] + self.vec_flat[1] + self.vec_flat[2]

            @pl.when(self.z != PLANES - 1)
            def _():
                self.vector_line(self.z).start()

    def finish_vectors(self):
        @pl.when(self.corner & (self.z == PLANES - 1))
        def _():
            total = self.vec_sum[...]
            for slot in range(3):
                self.vector_line(slot).wait_recv()
                total = total + self.vec_line[slot]
            for block in range(PAIRS):
                self.total[block, STEP:, :] = total[:, block * 128 : block * 128 + 128]

        @pl.when(self.c == 0)
        def _():
            self.vector_core().wait_send()

        @pl.when((self.c == 1) & (self.spot != 3))
        def _():
            self.vector_flat(0).wait_send()

        @pl.when(self.corner & (self.z != PLANES - 1))
        def _():
            self.vector_line(0).wait_send()

    def finish_line(self, plane, part=0):
        @pl.when(self.z == plane)
        def _():
            for slot in range(3):
                self.sum_line(plane, part, slot).wait_recv()
            for block in self.blocks(plane, part):
                total = self.plane_sum[plane, block].astype(F32)
                for slot in range(3):
                    total = total + self.line_land[slot, block].astype(F32)
                self.total[block] = total

    def drain_sum(self, plane, part=0):
        @pl.when(self.z != plane)
        def _():
            self.sum_line(plane, part, 0).wait_send()

        if plane == 0:
            for step in (1, 2, 3):
                self.sum_all(part, step).wait_send()
        else:
            for step in (1, 2):
                self.sum_half(plane, step).wait_send()
                self.sum_next(plane, step).wait_send()
        for y in (0, 1):
            self.sum_core(plane, part, y).wait_send()

    def unframe(self, parts, last):
        rows = self.shard_sum.shape[1]
        up, across = self.offsets()
        gap = iota((rows, FRAME), 0) + up - 3 * iota((rows, FRAME), 1)
        here = self.shard_sum[0] if last else jnp.zeros((rows, 128), F32)
        carried = self.shard_sum[1] if last else jnp.zeros((rows, 128), F32)
        for block in parts:
            total = self.total[block]
            high = total.astype(BF)
            both = jnp.concatenate([high, (total - high.astype(F32)).astype(BF)], axis=1)
            moved = dot(jnp.where(gap == block, 1.0, 0.0).astype(BF), both)
            here = here + (moved[:, :128] + moved[:, 128:])
            moved = dot(jnp.where(gap == block - 1, 1.0, 0.0).astype(BF), both)
            carried = carried + (moved[:, :128] + moved[:, 128:])
        if last:
            mixed = jnp.where(iota((rows, 128), 1) >= across, here, carried)
            mixed = pltpu.roll(mixed, (128 - across) % 128, 1)
            count = self.own_grad.shape[0]
            full, rest = count // 128, count % 128
            self.own_grad[pl.ds(0, full * 128)] = mixed[:full, :].reshape(full * 128)
            if rest:
                self.own_grad[pl.ds(full * 128, rest)] = mixed[full, :rest]
        else:
            self.shard_sum[0] = here
            self.shard_sum[1] = carried


def exchange_refs(count):
    vmem, dma = pltpu.VMEM, pltpu.SemaphoreType.DMA
    return {
        "grads": vmem((PAIRS, ALL_ROWS, 128), BF),
        "grad_vecs": vmem((16, D), F32),
        "land": vmem((PLANES, PAIRS, 2, 4, FRAME, 128), BF),
        "core_land": vmem((3, 2, PAIRS, TWO, 128), BF),
        "all_land": vmem((3, PAIRS, FRAME, 128), BF),
        "half_land": vmem((PLANES - 1, 2, PAIRS, HALF, 128), BF),
        "next_land": vmem((PLANES - 1, 2, PAIRS, FRAME, 128), BF),
        "plane_sum": vmem((PLANES, PAIRS, FRAME, 128), BF),
        "line_land": vmem((3, PAIRS, FRAME, 128), BF),
        "total": vmem((PAIRS, FRAME, 128), F32),
        "shard_flat": vmem((count,), BF),
        "shard_sum": vmem((2, -(-count // 1024) * 8, 128), F32),
        "vec_par": vmem((PAIRS, 16, 128), BF),
        "vec_core": vmem((16, D), F32),
        "vec_sum": vmem((16, D), F32),
        "vec_flat": vmem((3, 16, D), F32),
        "vec_line": vmem((3, 16, D), F32),
        "line_send": dma((PAIRS, 3)),
        "line_recv": dma((6,)),
        "flat_send": dma((21,)),
        "flat_recv": dma((21,)),
        "core_send": dma((6,)),
        "core_recv": dma((6,)),
        "sum_core_send": dma((12,)),
        "sum_core_recv": dma((12,)),
        "sum_flat_send": dma((21,)),
        "sum_flat_recv": dma((21,)),
        "sum_line_send": dma((6,)),
        "sum_line_recv": dma((9,)),
        "par_send": dma((10,)),
        "par_recv": dma((2,)),
        "vec_send": dma((3,)),
        "vec_recv": dma((7,)),
    }


def whole_kernel(names, *refs):
    refs = dict(zip(names, refs))
    refs["flat"] = refs["grads"]
    layer, swap = Layer(refs), Exchange(refs)
    swap.params_copy().start()
    layer.load()
    swap.greet()
    swap.frame_own()
    layer.start()
    swap.greeted()
    swap.send_vectors_line()
    for part in range(PAIRS):
        swap.send_line(0, part, (3, 2, 1))
    swap.send_line(3, 0, (1, 2, 3))
    swap.send_line(2, 0, (3, 2, 1))
    swap.send_line(1, 0, (3,))
    own, second, third = swap.plane_order()
    swap.own_first(lambda: swap.send_next(own))
    swap.send_all(0)
    swap.send_line(1, 0, (2, 1))
    swap.send_vectors_plane()
    swap.send_all(1)
    swap.send_core(0, 0)
    swap.own_first(lambda: swap.send_halves(own))
    swap.send_all(2)
    swap.others_first(lambda: swap.receive_line(own), lambda: swap.send_next(own))
    swap.finish_vectors_plane()
    layer.load_vectors()
    swap.finish_gather(0, 0)
    layer.query_key_value(0)
    layer.attend_first(0)
    swap.receive_line(second)
    swap.send_next(second)
    swap.send_core(0, 1)

    layer.attend_step(0, 1)
    swap.others_first(lambda: swap.send_halves(own))
    swap.finish_gather(0, 1)
    layer.query_key_value(1)
    layer.attend_step(1, 2)
    swap.receive_line(third)
    swap.send_next(third)
    swap.send_core(0, 2)
    layer.attend_step(2, 3)
    swap.finish_gather(0, 2)
    layer.query_key_value(2)
    layer.attend_step(3, 4)
    swap.send_halves(second)
    swap.send_core(own)
    layer.attend_step(4, 5)
    swap.send_halves(third)
    layer.attend_step(5, None)
    swap.send_core(second)
    swap.send_core(third)
    swap.finish_gather(1)
    layer.after_attention()
    swap.finish_gather(2)
    layer.up_weights()

    def before_down():
        swap.finish_gather(3)
        layer.down_weights()

    layer.feed_forward(before_down)
    for block in range(PAIRS):
        layer.grads[block, ROW_VEC:, :] = jnp.zeros((ALL_ROWS - ROW_VEC, 128), BF)
    layer.down_grad(D, FF)
    swap.reduce_core(3)
    layer.down_grad(0, D)
    swap.drain_gather()
    layer.hidden_grad()
    swap.reduce_halves(3)
    layer.up_grad(D // 2)
    swap.reduce_core(2)
    layer.first_norm_grad((0,))
    layer.up_grad(0)
    swap.reduce_next(3)
    swap.reduce_halves(2)
    layer.first_norm_grad((1, 2))
    layer.out_grad()
    swap.reduce_core(1)

    layer.pair_backward(0, {3: lambda: swap.reduce_halves(1), 7: lambda: swap.reduce_next(2)})
    swap.reduce_core(0, 0)
    swap.reduce_next(1)
    swap.reduce_line(3)
    layer.pair_backward(1, {7: lambda: swap.reduce_all(0)})
    swap.reduce_core(0, 1)
    swap.reduce_line(2)
    swap.reduce_line(1)
    layer.pair_backward(2, {7: lambda: swap.reduce_all(1)})
    swap.reduce_core(0, 2)
    swap.reduce_line(0, 0)
    layer.vector_grads()
    swap.reduce_vectors_core()

    def last_flat():
        swap.reduce_all(2)
        swap.reduce_vectors_flat()
        swap.reduce_line(0, 1)

    layer.input_grad_step({1: last_flat})
    swap.reduce_line(0, 2)
    swap.reduce_vectors_line()
    for plane in (1, 2, 3):
        swap.drain_sum(plane)
        swap.finish_line(plane)
    for part in (0, 1):
        swap.drain_sum(0, part)
        swap.finish_line(0, part)
    swap.finish_vectors()
    swap.unframe((0, 1), False)
    swap.drain_sum(0, 2)
    swap.finish_line(0, 2)
    swap.unframe((2,), True)


def whole_layer(tokens, cotangent, own_params, subnets, lengths):
    rows = tokens.shape[0]
    scratch = scratch_refs() | exchange_refs(own_params.shape[0])
    inputs = ["tokens", "cotangent", "own_params", "subnets", "lengths"]
    outputs = ["layer_out", "input_grad", "own_grad"]
    spaces = [pl.ANY] * 3 + [pltpu.SMEM] * 2
    return pl.pallas_call(
        functools.partial(whole_kernel, inputs + outputs + list(scratch)),
        out_shape=(
            pltpu.VMEM((rows, D), BF),
            pltpu.VMEM((rows, D), F32),
            pltpu.VMEM(own_params.shape, F32),
        ),
        in_specs=[pl.BlockSpec(memory_space=space) for space in spaces],
        out_specs=[pl.BlockSpec(memory_space=pltpu.VMEM)] * 3,
        scratch_shapes=list(scratch.values()),
        compiler_params=pltpu.CompilerParams(
            vmem_limit_bytes=VMEM_LIMIT, collective_id=0, has_side_effects=True
        ),
    )(tokens, cotangent, own_params, subnets, lengths)


def emit_kernel(*refs):
    sems, half = refs[-1], len(refs) // 2
    copies = [pltpu.make_async_copy(refs[i], refs[half + i], sems.at[i]) for i in range(half)]
    for copy in copies:
        copy.start()
    for copy in copies:
        copy.wait()


def emit(*arrays):
    return pl.pallas_call(
        emit_kernel,
        out_shape=[jax.ShapeDtypeStruct(array.shape, array.dtype) for array in arrays],
        in_specs=[pl.BlockSpec(memory_space=pltpu.VMEM)] * len(arrays),
        out_specs=[pl.BlockSpec(memory_space=pl.ANY)] * len(arrays),
        scratch_shapes=[pltpu.SemaphoreType.DMA((len(arrays),))],
        compiler_params=pltpu.CompilerParams(vmem_limit_bytes=8 * 2**20),
    )(*arrays)


def local_kernel(names, *refs):
    refs = dict(zip(names, refs))
    refs["vec_par"] = refs["flat"].at[:, ROW_VEC:, :]
    layer = Layer(refs)
    layer.load()
    layer.start()
    layer.load_vectors()
    for pair in range(PAIRS):
        layer.query_key_value(pair)
    layer.attend_first(0)

    for head in range(HEADS):
        layer.attend_step(head, head + 1 if head + 1 < HEADS else None)
    layer.after_attention()
    layer.up_weights()
    layer.feed_forward(layer.down_weights)
    layer.down_grad(0, FF)
    layer.hidden_grad()
    layer.up_grad(0)
    layer.up_grad(D // 2)
    layer.first_norm_grad(range(LIVE // TILE))
    layer.out_grad()
    for pair in range(PAIRS):
        layer.pair_backward(pair, {})
    layer.input_grad_step({})
    layer.vector_grads()
    for block in range(PAIRS):
        layer.grads[block, ROW_VEC:, :] = layer.grad_vecs[:, block * 128 : block * 128 + 128].astype(BF)


def local_layer(tokens, cotangent, flat, subnets, lengths):
    rows = tokens.shape[0]
    scratch = scratch_refs() | {"grad_vecs": pltpu.VMEM((16, D), F32)}
    inputs = ["tokens", "cotangent", "flat", "subnets", "lengths"]
    outputs = ["layer_out", "input_grad", "grads"]
    spaces = [pl.ANY] * 2 + [pltpu.VMEM] + [pltpu.SMEM] * 2
    return pl.pallas_call(
        functools.partial(local_kernel, inputs + outputs + list(scratch)),
        out_shape=(
            jax.ShapeDtypeStruct((rows, D), BF),
            jax.ShapeDtypeStruct((rows, D), F32),
            jax.ShapeDtypeStruct((PAIRS, ALL_ROWS, 128), BF),
        ),
        in_specs=[pl.BlockSpec(memory_space=space) for space in spaces],
        out_specs=[pl.BlockSpec(memory_space=pltpu.VMEM)] * 3,
        scratch_shapes=list(scratch.values()),
        compiler_params=pltpu.CompilerParams(vmem_limit_bytes=VMEM_LIMIT),
    )(tokens, cotangent, flat, subnets, lengths)


def on_device(tokens, cotangent, params, subnets, lengths):
    flat = lax.all_gather(params, ("group", "item"), axis=0, tiled=True)
    flat = flat.reshape(-1, D)
    whole = flat.shape[0]
    flat = jnp.pad(flat, ((0, ALL_ROWS - whole), (0, 0)))
    flat = jnp.swapaxes(flat.reshape(ALL_ROWS, PAIRS, 128), 0, 1)
    layer_out, input_grad, grads = local_layer(tokens[0], cotangent[0], flat, subnets, lengths[0])
    grad = jnp.swapaxes(grads[:, :whole], 0, 1).astype(F32).reshape(-1)
    param_grad = lax.psum_scatter(grad, ("group", "item"), scatter_dimension=0, tiled=True)
    return layer_out[None], input_grad[None], param_grad


def on_known_device(tokens, cotangent, params, subnets, lengths):
    results = whole_layer(tokens[0], cotangent[0], params, subnets, lengths[0])
    layer_out, input_grad, own_grad = emit(*results)
    return layer_out[None], input_grad[None], own_grad


def solution(mesh):
    in_specs = (
        P("group", "item", None),
        P("group", "item", None),
        P(("group", "item")),
        P("group", None),
        P("group", "item", None),
    )
    out_specs = (P("group", "item", None), P("group", "item", None), P(("group", "item")))
    known = mesh.shape["group"] == 16 and mesh.shape["item"] == 2
    return jax.shard_map(
        on_known_device if known else on_device, mesh=mesh, in_specs=in_specs, out_specs=out_specs, check_vma=False
    )
```

```python
import functools

import jax
import jax.numpy as jnp
from jax import lax
from jax.experimental import pallas as pl
from jax.experimental.pallas import tpu as pltpu
from jax.sharding import PartitionSpec as P

HD = 64
HEADS = 6
D = 384
FF = 1536
LIVE = 960
PAIRS = HEADS // 2
CHUNKS = FF // D
BLOCK = 256
TILE = 320
WIDE = 512
BIG = 1e30
BF = jnp.bfloat16
F32 = jnp.float32
ROW_Q, ROW_K, ROW_V, ROW_O, ROW_UP, ROW_DOWN, ROW_VEC = 0, 384, 768, 1152, 1536, 3072, 4608
ALL_ROWS = 4624
STEP, FRAME, TWO, HALF = 144, 160, 304, 80
PLANES = 4
MESH = pl.DeviceIdType.MESH
VMEM_LIMIT = 61 * 2**20


def dot(left, right):
    return jnp.dot(left, right, preferred_element_type=F32)


def dot_nt(left, right):
    return lax.dot_general(left, right, (((1,), (1,)), ((), ())), preferred_element_type=F32)


def dot_tn(left, right):
    return lax.dot_general(left, right, (((0,), (0,)), ((), ())), preferred_element_type=F32)


def iota(shape, axis):
    return lax.broadcasted_iota(jnp.int32, shape, axis)


def lanes_at(start, size=128):
    return pl.ds(pl.multiple_of(start, 128), size)


def below(shape, axis, bound):
    return jnp.where(iota(shape, axis) < bound, 1.0, 0.0).astype(F32)


def key_range(block):
    first = max(0, block * BLOCK - 479) // 96 * 96
    last = min(LIVE, -(-(block * BLOCK + BLOCK + 479) // 32) * 32)
    return first, last


def gelu_parts(z):
    cdf = 0.5 + 0.5 * lax.erf(z * 0.7071067811865476)
    bell = jnp.exp(-0.5 * (z * z)) * 0.3989422804014327
    return z * cdf, cdf + z * bell


def norm_forward(hidden, gain, shift, feature, inv_count):
    center = (hidden - jnp.sum(hidden * feature, axis=-1, keepdims=True) * inv_count) * feature
    inverse = lax.rsqrt(jnp.sum(center * center, axis=-1, keepdims=True) * inv_count + 1e-05)
    normed = center * inverse
    return normed * gain + shift, normed, inverse


def norm_backward(grad, normed, inverse, gain, feature, inv_count):
    scaled = grad * gain
    first = jnp.sum(scaled, axis=-1, keepdims=True) * inv_count
    second = jnp.sum(scaled * normed, axis=-1, keepdims=True) * inv_count
    return inverse * (scaled - first - normed * second) * feature


def col_sum(value):
    return jnp.sum(value, axis=0, keepdims=True)


class Layer:
    def __init__(self, refs):
        self.__dict__.update(refs)
        self.d_f, self.norm_low = self.low.at[0], self.low.at[1]
        self.cot = self.layer_out
        self.d_a, self.dot_t = self.xm, self.v_t
        for index, name in enumerate(("norm_one", "normed_one", "grad_second")):
            setattr(self, name, self.hold.at[:, index * D : index * D + D])
        self.lanes = self.expo.shape[2]
        width, heads, hidden = self.subnets[0, 0], self.subnets[0, 1], self.subnets[0, 2]
        self.width, self.attend, self.hidden = width, heads * HD, hidden
        self.inv_count = 1.0 / jnp.full((1, 1), width, jnp.int32).astype(F32)

    def row_mask(self, cols, bound, offset=0):
        return jnp.where(iota((1, cols), 1) + offset < bound, 1.0, 0.0).astype(F32)

    def col_mask(self, rows, bound, offset=0):
        return jnp.where(iota((rows, 1), 0) + offset < bound, 1.0, 0.0).astype(F32)

    def feature(self):
        return self.row_mask(D, self.width)

    def vector(self, index):
        mask = self.attend if index < 2 else self.width
        return self.vecs[4 + index : 5 + index, :] * self.row_mask(D, mask)

    def add_sum(self, index, value, first):
        part = value[:8, :]
        for start in range(8, value.shape[0], 8):
            part = part + value[start : start + 8, :]
        if first:
            self.sums[index] = part
        else:
            self.sums[index] += part


    def tokens_copy(self):
        return pltpu.make_async_copy(self.tokens.at[pl.ds(0, LIVE)], self.xm, self.io_sem.at[0])

    def cotangent_copy(self):
        return pltpu.make_async_copy(self.cotangent.at[pl.ds(0, LIVE)], self.cot.at[pl.ds(0, LIVE)], self.io_sem.at[1])

    def load(self):
        self.tokens_copy().start()
        self.cotangent_copy().start()

    def start(self):
        pad = self.lanes - LIVE
        self.input_grad[LIVE:, :] = jnp.zeros((self.input_grad.shape[0] - LIVE, D), F32)
        self.cot[LIVE:, :] = jnp.zeros((self.cot.shape[0] - LIVE, D), BF)
        self.dot_t[:, :, LIVE:] = jnp.zeros((HEADS, HD, pad), BF)
        self.q_t[:, :, LIVE:] = jnp.zeros((HEADS, HD, pad), BF)
        self.delta[:, :, LIVE:] = jnp.zeros((HEADS, 1, pad), F32)
        self.do_s[LIVE:, :] = jnp.zeros((pad, D), BF)
        self.q_rows[LIVE:, :] = jnp.zeros((pad, D), BF)
        ends = []
        total = 0
        for index in range(4):
            total = total + self.lengths[0, index]
            ends.append(total)
        lane = iota((HD, self.lanes), 1)
        seg = sum((lane >= end).astype(jnp.int32) for end in ends)
        part = iota((HD, self.lanes), 0)
        self.far[...] = jnp.where((part < 4) & (part != seg), -BIG, 0.0).astype(BF)
        row = iota((LIVE, 128), 0)
        seg = sum((row >= end).astype(jnp.int32) for end in ends[:3])
        self.hot[...] = jnp.where(iota((LIVE, 128), 1) - HD == seg, 1.0, 0.0).astype(BF)
        fe = self.feature().astype(BF)
        self.tokens_copy().wait()
        for rows in row_tiles():
            self.xm[rows, :] = self.xm[rows, :] * fe
        for part in range(PAIRS):
            lanes = slice(part * 128, part * 128 + 128)
            self.xt[lanes, :] = self.xm[:, lanes].T

    def load_vectors(self):
        for part in range(PAIRS):
            lanes = slice(part * 128, part * 128 + 128)
            self.vecs[:, lanes] = self.vec_par[part].astype(F32)
        for chunk in range(CHUNKS):
            cols = slice(chunk * D, chunk * D + D)
            self.bias[:, cols] = self.vecs[chunk : chunk + 1, :] * self.row_mask(D, self.hidden, chunk * D)


    def query_key_value(self, pair):
        lanes = lanes_at(pair * 128)
        seen = self.row_mask(128, self.attend, pair * 128)
        mask = self.col_mask(D, self.width) * seen
        for index, row in enumerate((ROW_Q, ROW_K, ROW_V)):
            weight = (self.flat[pair, row : row + D, :].astype(F32) * mask).astype(BF)
            self.w_qkv[:, lanes_at(pair * D + index * 128)] = weight
        bias_q, bias_v = self.vecs[4:5, lanes] * seen, self.vecs[5:6, lanes] * seen
        weight = self.w_qkv[:, lanes_at(pair * D, D)]
        for start in range(0, LIVE, BLOCK):
            rows = slice(start, min(start + BLOCK, LIVE))
            size = rows.stop - rows.start
            even = iota((size, 128), 1) < HD
            out = dot(self.xm[rows, :], weight)
            q = (out[:, :128] + bias_q).astype(BF)
            self.q_rows[rows, lanes] = q
            k32 = out[:, 128:256]
            k = k32.astype(BF)
            hot = self.hot[rows, :]
            for head, moved in ((2 * pair, k32), (2 * pair + 1, pltpu.roll(k32, HD, 1))):
                place, cols = self.keys_place(head)
                self.low[place, rows, cols] = jnp.where(even, moved, hot.astype(F32)).astype(BF)
            v = (out[:, 256:] + bias_v).astype(BF)
            self.v_rows[rows, lanes] = v
            turned = (q * jnp.asarray(0.125, BF)).T
            self.q_t[2 * pair, :, rows] = turned[:HD, :]
            self.q_t[2 * pair + 1, :, rows] = turned[HD:, :]
            turned = k.T
            self.k_t[2 * pair, :, rows] = turned[:HD, :]
            self.k_t[2 * pair + 1, :, rows] = turned[HD:, :]
            turned = v.T
            self.v_t[2 * pair, :, rows] = turned[:HD, :]
            self.v_t[2 * pair + 1, :, rows] = turned[HD:, :]

    def keys_place(self, head):
        return head // PAIRS, lanes_at(head % PAIRS * 128)

    def score(self, head, block):
        cols = slice(block * BLOCK, block * BLOCK + BLOCK)
        first, last = key_range(block)
        right = jnp.concatenate([self.q_t[head, :, cols], self.far[:, cols]], axis=0)
        place, lanes = self.keys_place(head)
        self.hold[first:last, cols] = dot(self.low[place, first:last, lanes], right)

    def soft(self, head, block):
        cols = slice(block * BLOCK, block * BLOCK + BLOCK)
        first, last = key_range(block)
        scores = self.hold[first:last, cols]
        expo = jnp.exp(scores - jnp.max(scores, axis=0, keepdims=True))
        inv = 1.0 / jnp.sum(expo, axis=0, keepdims=True)
        expo = expo.astype(BF)
        self.expo[head, first:last, cols] = expo
        self.inv[head, :, cols] = inv
        return expo, inv

    def attend_first(self, head):
        for block in range(self.lanes // BLOCK):
            self.score(head, block)

    def attend_step(self, head, after):
        for block in range(self.lanes // BLOCK):
            cols = slice(block * BLOCK, block * BLOCK + BLOCK)
            first, last = key_range(block)
            expo, inv = self.soft(head, block)
            self.score(after, block)
            mixed = dot(self.v_t[head, :, first:last], expo) * inv
            self.o_t[head, :, cols] = mixed.astype(BF)

    def after_attention(self):
        mask = self.col_mask(D, self.attend) * self.feature()
        for part in range(PAIRS):
            lanes = slice(part * 128, part * 128 + 128)
            rows = self.flat[part, ROW_O : ROW_O + D, :].astype(F32)
            self.w_out[:, lanes] = (rows * mask[:, lanes]).astype(BF)
        fe, bias, gain, shift = self.feature(), self.vector(2), self.vector(3), self.vector(4)
        for start in range(0, LIVE, BLOCK):
            size = min(BLOCK, LIVE - start)
            rows = slice(start, start + size)
            mixed = self.o_t[:, :, start : start + BLOCK].reshape(D, BLOCK)
            attended = dot_tn(mixed, self.w_out[...])[:size, :]
            hidden = self.xm[rows, :].astype(F32) + attended + bias
            norm, normed, inverse = norm_forward(hidden, gain, shift, fe, self.inv_count)
            self.norm_one[rows, :] = norm
            self.normed_one[rows, :] = normed
            self.inverse_one[rows, :] = jnp.broadcast_to(inverse, (size, 128))
            self.norm_low[rows, :] = norm.astype(BF)

    def up_weights(self):
        for part in range(PAIRS):
            self.wide[part] = self.flat[part, ROW_UP : ROW_UP + FF, :].astype(F32)
        for chunk in range(CHUNKS):
            mask = self.col_mask(D, self.width) * self.row_mask(D, self.hidden, chunk * D)
            for part in range(PAIRS):
                lanes = slice(part * 128, part * 128 + 128)
                piece = self.wide[part, pl.ds(chunk, D, stride=CHUNKS), :]
                self.w_up[:, chunk * D + part * 128 : chunk * D + part * 128 + 128] = (
                    piece * mask[:, lanes]
                ).astype(BF)

    def down_weights(self):
        mask = self.feature()
        for chunk in range(CHUNKS):
            rows = slice(chunk * D, chunk * D + D)
            hidden = self.col_mask(D, self.hidden, chunk * D)
            for part in range(PAIRS):
                lanes = slice(part * 128, part * 128 + 128)
                piece = self.flat[part, ROW_DOWN + chunk * D : ROW_DOWN + chunk * D + D, :].astype(F32)
                self.w_down[rows, lanes] = (piece * (hidden * mask[:, lanes])).astype(BF)

    def up_tile(self, rows):
        low = self.norm_low[rows, :]
        for start in range(0, FF, BLOCK):
            cols = slice(start, start + BLOCK)
            act, slope = gelu_parts(dot(low, self.w_up[:, cols]) + self.bias[:, cols])
            self.act[rows, cols] = act.astype(BF)
            self.slope[rows, cols] = slope.astype(BF)

    def down_tile(self, rows):
        fe = self.feature()
        bias, gain, shift = self.vector(5), self.vector(6), self.vector(7)
        second = self.norm_one[rows, :] + dot(self.act[rows, :FF], self.w_down[...]) + bias
        result, normed, inverse = norm_forward(second, gain, shift, fe, self.inv_count)
        grad = self.cot[rows, :].astype(F32)
        self.cot[rows, :] = result.astype(BF)
        grad_second = norm_backward(grad, normed, inverse, gain, fe, self.inv_count)
        self.grad_second[rows, :] = grad_second
        low = grad_second.astype(BF)
        self.d_f[rows, :] = low
        first = rows.start == 0
        self.add_sum(10, grad * normed, first)
        self.add_sum(11, grad, first)
        self.add_sum(9, low.astype(F32), first)

    def feed_forward(self, before_down):
        for rows in row_tiles():
            self.up_tile(rows)
        before_down()
        self.cotangent_copy().wait()
        for rows in row_tiles():
            self.down_tile(rows)


    def down_grad(self, start, stop):
        fe = self.feature()
        for first in range(start, stop, WIDE):
            size = min(WIDE, stop - first)
            grad = dot_tn(self.d_f[...], self.act[:, first : first + size]).astype(BF).T
            grad = grad * (self.col_mask(size, self.hidden, first) * fe).astype(BF)
            for part in range(PAIRS):
                lanes = slice(part * 128, part * 128 + 128)
                self.grads[part, ROW_DOWN + first : ROW_DOWN + first + size, :] = grad[:, lanes]

    def hidden_tile(self, rows):
        d_f = self.d_f[rows, :]
        for start in range(0, FF, BLOCK):
            cols = slice(start, start + BLOCK)
            grad = dot_nt(d_f, self.w_down[cols, :])
            dz = (grad * self.slope[rows, cols].astype(F32)).astype(BF)
            self.slope[rows, cols] = dz
            part = dz[:8, :].astype(F32)
            for row in range(8, rows.stop - rows.start, 8):
                part = part + dz[row : row + 8, :].astype(F32)
            if rows.start == 0:
                self.hidden_sums[:, cols] = part
            else:
                self.hidden_sums[:, cols] += part

    def first_norm_tile(self, rows):
        gain, fe = self.vector(3), self.feature()
        normed = self.normed_one[rows, :]
        grad = self.grad_second[rows, :] + dot_nt(self.slope[rows, :], self.w_up[...])
        grad_first = norm_backward(grad, normed, self.inverse_one[rows, :1], gain, fe, self.inv_count)
        self.norm_one[rows, :] = grad_first
        low = grad_first.astype(BF)
        self.d_a[rows, :] = low
        first = rows.start == 0
        self.add_sum(7, grad * normed, first)
        self.add_sum(8, grad, first)
        self.add_sum(6, low.astype(F32), first)

    def hidden_grad(self):
        for rows in row_tiles():
            self.hidden_tile(rows)

    def first_norm_grad(self, tiles):
        for index in tiles:
            self.first_norm_tile(row_tiles()[index])

    def up_grad(self, start):
        half = D // 2
        low = self.norm_low[:, start : start + half]
        for first in range(0, FF, WIDE):
            mask = self.col_mask(half, self.width, start) * self.row_mask(WIDE, self.hidden, first)
            grad = dot_tn(low, self.slope[:, first : first + WIDE]) * mask
            for lane in range(0, WIDE, 128):
                chunk, part = (first + lane) // D, (first + lane) % D // 128
                rows = pl.ds(start * CHUNKS + chunk, half, stride=CHUNKS)
                self.wide[part, rows, :] = grad[:, lane : lane + 128]
        rows = slice(start * CHUNKS, (start + half) * CHUNKS)
        for part in range(PAIRS):
            self.grads[part, ROW_UP + rows.start : ROW_UP + rows.stop, :] = self.wide[part, rows, :].astype(BF)

    def out_grad(self):
        fe = self.feature()
        d_a = self.d_a[...]
        half = D // 2
        for start in (0, half):
            rows = slice(start, start + half)
            heads = range(start // HD, (start + half) // HD)
            mask = self.col_mask(half, self.attend, start) * fe
            o_t = self.o_t[heads.start : heads.stop, :, :LIVE].reshape(half, LIVE)
            grad = (dot(o_t, d_a) * mask).astype(BF)
            for part in range(PAIRS):
                lanes = slice(part * 128, part * 128 + 128)
                self.grads[part, ROW_O + start : ROW_O + start + half, :] = grad[:, lanes]
            mixed = dot_nt(self.w_out[rows, :], d_a)
            for head in heads:
                own = mixed[head * HD - start : head * HD - start + HD, :] * self.inv[head, :, :LIVE]
                self.delta[head, :, :LIVE] = col_sum(own * self.o_t[head, :, :LIVE].astype(F32))
                self.dot_t[head, :, :LIVE] = own.astype(BF)
        for pair in range(PAIRS):
            both = self.dot_t[2 * pair : 2 * pair + 2, :, :LIVE].reshape(128, LIVE)
            self.do_s[:LIVE, pair * 128 : pair * 128 + 128] = both.T

    def score_place(self, odd, block):
        if not odd:
            return self.act, block * BLOCK
        return ((self.act, 4 * BLOCK), (self.act, 5 * BLOCK), (self.slope, PAIRS * D), (self.d_f, 0))[block]

    def first_lane(self, pair, index):
        return lanes_at(pair * D + index * 128)

    def prob_grad(self, pair, odd, block):
        cols = slice(block * BLOCK, block * BLOCK + BLOCK)
        first, last = key_range(block)
        right = self.dot_t[2 * pair + odd, :, cols]
        none = jnp.zeros_like(right)
        right = jnp.concatenate([none, right] if odd else [right, none], axis=0)
        return dot(self.v_rows[first:last, lanes_at(pair * 128)], right)

    def score_grad(self, pair, odd, block, grad):
        head = 2 * pair + odd
        cols = slice(block * BLOCK, block * BLOCK + BLOCK)
        first, last = key_range(block)
        grad = self.expo[head, first:last, cols].astype(F32) * (grad - self.delta[head, :, cols])
        grad = grad.astype(BF)
        place, start = self.score_place(odd, block)
        place[first:last, start : start + BLOCK] = grad
        return grad

    def query_grad(self, pair, odd, block, grad):
        head = 2 * pair + odd
        cols = slice(block * BLOCK, block * BLOCK + BLOCK)
        first, last = key_range(block)
        dq = dot(self.k_t[head, :, first:last], grad) * 0.125
        self.dq_t[odd * HD : odd * HD + HD, cols] = dq.astype(BF)

    def pair_backward(self, pair, hooks):
        lanes = lanes_at(pair * 128)
        blocks = self.lanes // BLOCK
        ranges = [key_range(block) for block in range(blocks)]
        edges = sorted({edge for both in ranges for edge in both})
        cuts = []
        for low, high in zip(edges[:-1], edges[1:]):
            used = [b for b in range(blocks) if ranges[b][0] <= low and high <= ranges[b][1]]
            cuts.append((slice(low, high), slice(used[0] * BLOCK, used[-1] * BLOCK + BLOCK)))
        own = [jnp.where((iota((1, 128), 1) >= HD) == bool(odd), 1.0, 0.0).astype(BF) for odd in (0, 1)]
        d_out = [self.do_s[:, lanes] * own[odd] for odd in (0, 1)]
        items = [(odd, block) for odd in (0, 1) for block in range(blocks)]
        grad = self.prob_grad(pair, *items[0])
        for index, (odd, block) in enumerate(items):
            if index % 2 == 0 and index // 2 < len(cuts):
                rows, span = cuts[index // 2]
                dv = sum(dot(self.expo[2 * pair + odd_, rows, span], d_out[odd_][span]) for odd_ in (0, 1))
                self.slope[rows, self.first_lane(pair, 2)] = dv.astype(BF)
            after = self.prob_grad(pair, *items[index + 1]) if index + 1 < len(items) else None
            low = self.score_grad(pair, odd, block, grad)
            grad = after
            self.query_grad(pair, odd, block, low)
            if index in hooks:
                hooks[index]()
        queries = [self.q_rows[:, lanes] * own[odd] for odd in (0, 1)]
        for rows, span in cuts:
            dk = 0.0
            for odd in (0, 1):
                places = [self.score_place(odd, block) for block in range(span.start // BLOCK, span.stop // BLOCK)]
                first = 0
                for last in range(1, len(places) + 1):
                    if last == len(places) or places[last][0] is not places[first][0]:
                        place, start = places[first]
                        begin, size = span.start + first * BLOCK, (last - first) * BLOCK
                        dk = dk + dot(place[rows, start : start + size], queries[odd][begin : begin + size])
                        first = last
            self.slope[rows, self.first_lane(pair, 1)] = (dk * 0.125).astype(BF)
        self.slope[:, self.first_lane(pair, 0)] = self.dq_t[:, :LIVE].T
        mask = self.col_mask(D, self.width) * self.row_mask(128, self.attend, pair * 128)
        all_three = self.slope[:, lanes_at(pair * D, D)]
        grad = dot(self.xt[...], all_three)
        for index, row in enumerate((ROW_Q, ROW_K, ROW_V)):
            self.grads[pair, row : row + D, :] = (grad[:, index * 128 : index * 128 + 128] * mask).astype(BF)
        totals = dot(jnp.ones((8, LIVE), BF), all_three)
        self.sums[4, :, lanes] = totals[:, :128] * 0.125
        self.sums[5, :, lanes] = totals[:, 256:] * 0.125

    def input_grad_step(self, hooks):
        fe = self.feature()
        for index, rows in enumerate(row_tiles()):
            total = self.norm_one[rows, :] + dot_nt(self.slope[rows, : PAIRS * D], self.w_qkv[...])
            self.input_grad[rows, :] = total * fe
            if index in hooks:
                hooks[index]()

    def vector_grads(self):
        for index in range(12):
            if index < CHUNKS:
                total = jnp.sum(self.hidden_sums[:, index * D : index * D + D], axis=0, keepdims=True)
                mask = self.row_mask(D, self.hidden, index * D)
            else:
                total = jnp.sum(self.sums[index], axis=0, keepdims=True)
                mask = self.row_mask(D, self.attend if index < 6 else self.width)
            self.grad_vecs[index : index + 1, :] = total * mask
        self.grad_vecs[12:, :] = jnp.zeros((4, D), F32)


def row_tiles():
    return [slice(start, min(start + TILE, LIVE)) for start in range(0, LIVE, TILE)]


def scratch_refs():
    vmem = pltpu.VMEM
    lanes = -(-LIVE // BLOCK) * BLOCK
    return {
        "xm": vmem((LIVE, D), BF),
        "hold": vmem((LIVE, 3 * D), F32),
        "xt": vmem((D, LIVE), BF),
        "hot": vmem((LIVE, 128), BF),
        "far": vmem((HD, lanes), BF),
        "vecs": vmem((16, D), F32),
        "bias": vmem((1, FF), F32),
        "sums": vmem((12, 8, D), F32),
        "hidden_sums": vmem((8, FF), F32),
        "w_qkv": vmem((D, PAIRS * D), BF),
        "w_out": vmem((D, D), BF),
        "w_up": vmem((D, FF), BF),
        "w_down": vmem((FF, D), BF),
        "wide": vmem((PAIRS, FF, 128), F32),
        "q_rows": vmem((lanes, D), BF),
        "q_t": vmem((HEADS, HD, lanes), BF),
        "k_t": vmem((HEADS, HD, LIVE), BF),
        "v_rows": vmem((LIVE, D), BF),
        "v_t": vmem((HEADS, HD, lanes), BF),
        "expo": vmem((HEADS, LIVE, lanes), BF),
        "inv": vmem((HEADS, 1, lanes), F32),
        "o_t": vmem((HEADS, HD, lanes), BF),
        "inverse_one": vmem((LIVE, 128), F32),
        "low": vmem((2, LIVE, D), BF),
        "act": vmem((LIVE, FF), BF),
        "slope": vmem((LIVE, FF), BF),
        "do_s": vmem((lanes, D), BF),
        "delta": vmem((HEADS, 1, lanes), F32),
        "dq_t": vmem((128, lanes), BF),
        "io_sem": pltpu.SemaphoreType.DMA((3,)),
    }


class Exchange:
    def __init__(self, refs):
        self.__dict__.update(refs)
        group, self.x = lax.axis_index("group"), lax.axis_index("item")
        self.z, self.y, self.c = group // 4, (group // 2) % 2, group % 2
        self.spot = 2 * self.y + self.x
        self.shard = 2 * group + self.x
        self.corner = (self.c == 1) & (self.spot == 3)

    def device(self, z, y, c, x):
        return (z * 4 + y * 2 + c, x)

    def line(self, step):
        return self.device((self.z + step) % PLANES, self.y, self.c, self.x)

    def plane_peer(self, step):
        y, x = (self.y + step // 4) % 2, (self.x + step % 2) % 2
        return self.device(self.z, y, (self.c + step // 2 % 2) % 2, x)

    def chip_peer(self, step):
        y, x = (self.y + step // 2) % 2, (self.x + step % 2) % 2
        return self.device(self.z, y, self.c, x)

    def spot_of(self, step):
        return 2 * ((self.y + step // 2) % 2) + (self.x + step % 2) % 2

    def core_peer(self):
        return self.device(self.z, self.y, 1 - self.c, self.x)

    def greet(self):
        barrier = pltpu.get_barrier_semaphore()
        peers = [self.line(step) for step in (1, 2, 3)] + [self.plane_peer(step) for step in range(1, 8)]
        for peer in peers:
            pl.semaphore_signal(barrier, inc=1, device_id=peer, device_id_type=MESH)

    def greeted(self):
        pl.semaphore_wait(pltpu.get_barrier_semaphore(), 10)

    def copy(self, source, target, send, recv, peer):
        return pltpu.make_async_remote_copy(
            src_ref=source, dst_ref=target, send_sem=send, recv_sem=recv, device_id=peer, device_id_type=MESH
        )


    def offsets(self):
        shift = STEP * self.shard
        return shift // 128, shift % 128

    def params_copy(self):
        return pltpu.make_async_copy(self.own_params, self.shard_flat, self.io_sem.at[2])

    def frame_own(self):
        self.params_copy().wait()
        rows, count = self.shard_sum.shape[1], self.shard_flat.shape[0]
        full, rest = count // 128, count % 128
        spread = self.shard_sum.at[0]
        spread[:full, :] = self.shard_flat[pl.ds(0, full * 128)].reshape(full, 128).astype(F32)
        spread[full:, :] = jnp.zeros((rows - full, 128), F32)
        if rest:
            spread[full : full + 1, :rest] = self.shard_flat[pl.ds(full * 128, rest)].reshape(1, rest).astype(F32)
        up, across = self.offsets()
        turned = pltpu.roll(spread[...], across, 1)
        late = iota((rows, 128), 1) >= across
        same = jnp.where(late, turned, 0.0).astype(BF)
        carried = jnp.where(late, 0.0, turned).astype(BF)
        gap = 3 * iota((FRAME, rows), 0) - up - iota((FRAME, rows), 1)
        for part in range(PAIRS):
            here = jnp.where(gap == -part, 1.0, 0.0).astype(BF)
            after = jnp.where(gap == 1 - part, 1.0, 0.0).astype(BF)
            frame = dot(here, same) + dot(after, carried)
            self.land[self.z, part, self.c, self.spot] = frame.astype(BF)

    def vectors_line(self, step):
        sems = self.par_send.at[step - 1], self.par_recv.at[0]
        return self.copy(self.vec_par, self.vec_par, *sems, self.line(step))

    def vectors_plane(self, step):
        sems = self.par_send.at[step + 2], self.par_recv.at[1]
        return self.copy(self.vec_par, self.vec_par, *sems, self.plane_peer(step))

    def send_vectors_line(self):
        @pl.when(self.corner & (self.z == PLANES - 1))
        def _():
            self.vec_par[...] = self.land[PLANES - 1, :, 1, 3, STEP:, :]
            for step in (1, 2, 3):
                self.vectors_line(step).start()

    def send_vectors_plane(self):
        @pl.when(self.corner & (self.z != PLANES - 1))
        def _():
            self.vectors_line(1).wait_recv()

        @pl.when(self.corner)
        def _():
            for step in range(1, 8):
                self.vectors_plane(step).start()

    def finish_vectors_plane(self):
        @pl.when(jnp.logical_not(self.corner))
        def _():
            self.vectors_plane(1).wait_recv()

    def parts(self, plane, part):
        return pl.ds(part, 1) if isinstance(plane, int) and plane == 0 else slice(None)

    def blocks(self, plane, part):
        return [part] if plane == 0 else range(PAIRS)

    def item(self, plane, part):
        return part if isinstance(plane, int) and plane == 0 else 2 + plane

    def gather_line(self, plane, part, step):
        piece = self.land.at[plane, self.parts(plane, part), self.c, self.spot]
        sems = self.line_send.at[part, step - 1], self.line_recv.at[self.item(plane, part)]
        return self.copy(piece, piece, *sems, self.line(step))

    def send_line(self, plane, part, steps):
        @pl.when(self.z == plane)
        def _():
            for step in steps:
                self.gather_line(plane, part, step).start()

    def gather_all(self, part, step, spot):
        piece = self.land.at[0, pl.ds(part, 1), self.c, spot]
        sems = self.flat_send.at[3 * part + step - 1], self.flat_recv.at[3 * part + step - 1]
        return self.copy(piece, piece, *sems, self.chip_peer(step))

    def gather_next(self, plane, step, spot):
        piece = self.land.at[plane, :, self.c, spot]
        index = 5 + 4 * plane + step - 1
        return self.copy(piece, piece, self.flat_send.at[index], self.flat_recv.at[index], self.chip_peer(step))

    def gather_half(self, plane, step, spot):
        rows = pl.ds((2 - step) * HALF, HALF)
        piece = self.land.at[plane, :, self.c, spot, rows]
        index = 5 + 4 * plane + step + 1
        return self.copy(piece, piece, self.flat_send.at[index], self.flat_recv.at[index], self.chip_peer(step))

    def wait_line(self, plane, part):
        @pl.when(self.z != plane)
        def _():
            self.gather_line(plane, part, 1).wait_recv()

    def send_all(self, part):
        self.wait_line(0, part)
        for step in (3, 2, 1):
            self.gather_all(part, step, self.spot).start()

    def plane_order(self):
        second = jnp.where(self.z == 0, 3, jnp.where(self.z == 1, 2, 1))
        third = jnp.where(self.z % 3 == 0, 2, 3)
        return jnp.maximum(self.z, 1), second, third

    def own_first(self, action):
        @pl.when(self.z != 0)
        def _():
            action()

    def others_first(self, *actions):
        @pl.when(self.z == 0)
        def _():
            for action in actions:
                action()

    def receive_line(self, plane):
        self.copy_line(plane).wait_recv()

    def copy_line(self, plane):
        piece = self.land.at[plane, :, self.c, self.spot]
        return self.copy(piece, piece, self.line_send.at[1, 0], self.line_recv.at[2 + plane], self.line(1))

    def send_next(self, plane):
        for step in (2, 1):
            self.gather_next(plane, step, self.spot).start()

    def send_halves(self, plane):
        self.gather_next(plane, 1, self.spot_of(1)).wait_recv()
        self.gather_half(plane, 2, self.spot_of(1)).start()
        self.gather_next(plane, 2, self.spot_of(2)).wait_recv()
        self.gather_half(plane, 1, self.spot_of(2)).start()

    def gather_core(self, plane, part, core):
        piece = self.land.at[plane, self.parts(plane, part), core]
        item = self.item(plane, part)
        return self.copy(piece, piece, self.core_send.at[item], self.core_recv.at[item], self.core_peer())

    def send_core(self, plane, part=0):
        if isinstance(plane, int) and plane == 0:
            for step in (3, 2, 1):
                self.gather_all(part, step, self.spot_of(step)).wait_recv()
        else:
            for step in (2, 1):
                self.gather_half(plane, step, self.spot_of(3)).wait_recv()
        self.gather_core(plane, part, self.c).start()

    def finish_gather(self, plane, part=0):
        self.gather_core(plane, part, 1 - self.c).wait_recv()
        for place in range(8):
            y, c, x = place // 4, (place // 2) % 2, place % 2
            chunk = 8 * plane + place
            for block in self.blocks(plane, part):
                frame = self.land[plane, block, c, 2 * y + x]
                self.flat[block, chunk * STEP : chunk * STEP + STEP, :] = frame[:STEP, :]
                if chunk:
                    before = (chunk - 1) % 8
                    spot = 2 * (before // 4) + before % 2
                    tail = self.land[(chunk - 1) // 8, block, (before // 2) % 2, spot, STEP:, :]
                    both = tail + frame[: FRAME - STEP, :]
                    self.flat[block, chunk * STEP : chunk * STEP + FRAME - STEP, :] = both

    def drain_gather(self):
        @pl.when(self.corner & (self.z == PLANES - 1))
        def _():
            for step in (1, 2, 3):
                self.vectors_line(step).wait_send()

        @pl.when(self.corner)
        def _():
            for step in range(1, 8):
                self.vectors_plane(step).wait_send()

        for plane in range(PLANES):
            for part in range(PAIRS if plane == 0 else 1):

                @pl.when(self.z == plane)
                def _():
                    for step in (1, 2, 3):
                        self.gather_line(plane, part, step).wait_send()

                if plane == 0:
                    for step in (1, 2, 3):
                        self.gather_all(part, step, self.spot).wait_send()
                else:
                    for step in (1, 2):
                        self.gather_next(plane, step, self.spot).wait_send()
                        self.gather_half(plane, step, self.spot).wait_send()
                self.gather_core(plane, part, self.c).wait_send()


    def sum_core(self, plane, part, y):
        row = pl.multiple_of(STEP * (8 * plane + 4 * y + 2 * (1 - self.c)), 16)
        parts, item = self.parts(plane, part), 2 * self.item(plane, part) + y
        return self.copy(
            self.grads.at[parts, pl.ds(row, TWO)],
            self.core_land.at[plane % 3, y, parts],
            self.sum_core_send.at[item],
            self.sum_core_recv.at[item],
            self.core_peer(),
        )

    def sum_all(self, part, step):
        index = 3 * part + step - 1
        return self.copy(
            self.land.at[0, pl.ds(part, 1), 0, self.spot_of(step)],
            self.all_land.at[step - 1, pl.ds(part, 1)],
            self.sum_flat_send.at[index],
            self.sum_flat_recv.at[index],
            self.chip_peer(step),
        )

    def sum_half(self, plane, step):
        index = 5 + 4 * plane + step - 1
        return self.copy(
            self.land.at[plane, :, 0, self.spot_of(3), pl.ds((step - 1) * HALF, HALF)],
            self.half_land.at[plane - 1, step - 1],
            self.sum_flat_send.at[index],
            self.sum_flat_recv.at[index],
            self.chip_peer(step),
        )

    def sum_next(self, plane, step):
        index = 5 + 4 * plane + step + 1
        return self.copy(
            self.land.at[plane, :, 0, self.spot_of(step)],
            self.next_land.at[plane - 1, step - 1],
            self.sum_flat_send.at[index],
            self.sum_flat_recv.at[index],
            self.chip_peer(step),
        )

    def sum_line(self, plane, part, slot):
        parts, item = self.parts(plane, part), self.item(plane, part)
        return self.copy(
            self.plane_sum.at[plane, parts],
            self.line_land.at[slot, parts],
            self.sum_line_send.at[item],
            self.sum_line_recv.at[3 * part + slot],
            self.device(plane, self.y, self.c, self.x),
        )

    def reduce_core(self, plane, part=0):
        for y in (0, 1):
            self.sum_core(plane, part, y).start()

    def add_core(self, plane, part):
        for y in (0, 1):
            self.sum_core(plane, part, y).wait_recv()
            for block in self.blocks(plane, part):
                for x in (0, 1):
                    row = pl.multiple_of(STEP * (8 * plane + 4 * y + 2 * self.c + x), 16)
                    own = self.grads[block, pl.ds(row, FRAME), :]
                    other = self.core_land[plane % 3, y, block, x * STEP : x * STEP + FRAME, :]
                    self.land[plane, block, 0, 2 * y + x] = own + other

    def reduce_all(self, part):
        self.add_core(0, part)
        for step in (3, 2, 1):
            self.sum_all(part, step).start()

    def reduce_halves(self, plane):
        self.add_core(plane, 0)
        for step in (1, 2):
            self.sum_half(plane, step).start()

    def reduce_next(self, plane):
        for step in (1, 2):
            self.sum_half(plane, step).wait_recv()
            rows = slice((step - 1) * HALF, step * HALF)
            spot = self.spot_of(3 - step)
            for block in range(PAIRS):
                own = self.land[plane, block, 0, spot, rows, :]
                self.land[plane, block, 0, spot, rows, :] = own + self.half_land[plane - 1, step - 1, block]
            self.sum_next(plane, 3 - step).start()

    def reduce_line(self, plane, part=0):
        if plane == 0:
            for step in (1, 2, 3):
                self.sum_all(part, step).wait_recv()
        else:
            for step in (1, 2):
                self.sum_next(plane, step).wait_recv()
        for block in self.blocks(plane, part):
            total = self.land[plane, block, 0, self.spot]
            if plane == 0:
                total = (total + self.all_land[0, block]) + (self.all_land[1, block] + self.all_land[2, block])
            else:
                total = total + (self.next_land[plane - 1, 0, block] + self.next_land[plane - 1, 1, block])
            self.plane_sum[plane, block] = total

        @pl.when(self.z != plane)
        def _():
            self.sum_line(plane, part, (self.z - plane + 2 * PLANES - 1) % PLANES).start()

    def vector_core(self):
        peer = self.core_peer()
        return self.copy(self.grad_vecs, self.vec_core, self.vec_send.at[0], self.vec_recv.at[0], peer)

    def vector_flat(self, slot):
        peer = self.device(self.z, 1, 1, 1)
        return self.copy(self.vec_sum, self.vec_flat.at[slot], self.vec_send.at[1], self.vec_recv.at[1 + slot], peer)

    def vector_line(self, slot):
        peer = self.device(PLANES - 1, 1, 1, 1)
        return self.copy(self.vec_sum, self.vec_line.at[slot], self.vec_send.at[2], self.vec_recv.at[4 + slot], peer)

    def reduce_vectors_core(self):
        @pl.when(self.c == 0)
        def _():
            self.vector_core().start()

    def reduce_vectors_flat(self):
        @pl.when(self.c == 1)
        def _():
            self.vector_core().wait_recv()
            self.vec_sum[...] = self.grad_vecs[...] + self.vec_core[...]

            @pl.when(self.spot != 3)
            def _():
                self.vector_flat(2 - self.spot).start()

    def reduce_vectors_line(self):
        @pl.when(self.corner)
        def _():
            for slot in range(3):
                self.vector_flat(slot).wait_recv()
            self.vec_sum[...] = self.vec_sum[...] + self.vec_flat[0] + self.vec_flat[1] + self.vec_flat[2]

            @pl.when(self.z != PLANES - 1)
            def _():
                self.vector_line(self.z).start()

    def finish_vectors(self):
        @pl.when(self.corner & (self.z == PLANES - 1))
        def _():
            total = self.vec_sum[...]
            for slot in range(3):
                self.vector_line(slot).wait_recv()
                total = total + self.vec_line[slot]
            for block in range(PAIRS):
                self.total[block, STEP:, :] = total[:, block * 128 : block * 128 + 128]

        @pl.when(self.c == 0)
        def _():
            self.vector_core().wait_send()

        @pl.when((self.c == 1) & (self.spot != 3))
        def _():
            self.vector_flat(0).wait_send()

        @pl.when(self.corner & (self.z != PLANES - 1))
        def _():
            self.vector_line(0).wait_send()

    def finish_line(self, plane, part=0):
        @pl.when(self.z == plane)
        def _():
            for slot in range(3):
                self.sum_line(plane, part, slot).wait_recv()
            for block in self.blocks(plane, part):
                total = self.plane_sum[plane, block].astype(F32)
                for slot in range(3):
                    total = total + self.line_land[slot, block].astype(F32)
                self.total[block] = total

    def drain_sum(self, plane, part=0):
        @pl.when(self.z != plane)
        def _():
            self.sum_line(plane, part, 0).wait_send()

        if plane == 0:
            for step in (1, 2, 3):
                self.sum_all(part, step).wait_send()
        else:
            for step in (1, 2):
                self.sum_half(plane, step).wait_send()
                self.sum_next(plane, step).wait_send()
        for y in (0, 1):
            self.sum_core(plane, part, y).wait_send()

    def unframe(self, parts, last):
        rows = self.shard_sum.shape[1]
        up, across = self.offsets()
        gap = iota((rows, FRAME), 0) + up - 3 * iota((rows, FRAME), 1)
        here = self.shard_sum[0] if last else jnp.zeros((rows, 128), F32)
        carried = self.shard_sum[1] if last else jnp.zeros((rows, 128), F32)
        for block in parts:
            total = self.total[block]
            high = total.astype(BF)
            both = jnp.concatenate([high, (total - high.astype(F32)).astype(BF)], axis=1)
            moved = dot(jnp.where(gap == block, 1.0, 0.0).astype(BF), both)
            here = here + (moved[:, :128] + moved[:, 128:])
            moved = dot(jnp.where(gap == block - 1, 1.0, 0.0).astype(BF), both)
            carried = carried + (moved[:, :128] + moved[:, 128:])
        if last:
            mixed = jnp.where(iota((rows, 128), 1) >= across, here, carried)
            mixed = pltpu.roll(mixed, (128 - across) % 128, 1)
            count = self.own_grad.shape[0]
            full, rest = count // 128, count % 128
            self.own_grad[pl.ds(0, full * 128)] = mixed[:full, :].reshape(full * 128)
            if rest:
                self.own_grad[pl.ds(full * 128, rest)] = mixed[full, :rest]
        else:
            self.shard_sum[0] = here
            self.shard_sum[1] = carried


def exchange_refs(count):
    vmem, dma = pltpu.VMEM, pltpu.SemaphoreType.DMA
    return {
        "grads": vmem((PAIRS, ALL_ROWS, 128), BF),
        "grad_vecs": vmem((16, D), F32),
        "land": vmem((PLANES, PAIRS, 2, 4, FRAME, 128), BF),
        "core_land": vmem((3, 2, PAIRS, TWO, 128), BF),
        "all_land": vmem((3, PAIRS, FRAME, 128), BF),
        "half_land": vmem((PLANES - 1, 2, PAIRS, HALF, 128), BF),
        "next_land": vmem((PLANES - 1, 2, PAIRS, FRAME, 128), BF),
        "plane_sum": vmem((PLANES, PAIRS, FRAME, 128), BF),
        "line_land": vmem((3, PAIRS, FRAME, 128), BF),
        "total": vmem((PAIRS, FRAME, 128), F32),
        "shard_flat": vmem((count,), BF),
        "shard_sum": vmem((2, -(-count // 1024) * 8, 128), F32),
        "vec_par": vmem((PAIRS, 16, 128), BF),
        "vec_core": vmem((16, D), F32),
        "vec_sum": vmem((16, D), F32),
        "vec_flat": vmem((3, 16, D), F32),
        "vec_line": vmem((3, 16, D), F32),
        "line_send": dma((PAIRS, 3)),
        "line_recv": dma((6,)),
        "flat_send": dma((21,)),
        "flat_recv": dma((21,)),
        "core_send": dma((6,)),
        "core_recv": dma((6,)),
        "sum_core_send": dma((12,)),
        "sum_core_recv": dma((12,)),
        "sum_flat_send": dma((21,)),
        "sum_flat_recv": dma((21,)),
        "sum_line_send": dma((6,)),
        "sum_line_recv": dma((9,)),
        "par_send": dma((10,)),
        "par_recv": dma((2,)),
        "vec_send": dma((3,)),
        "vec_recv": dma((7,)),
    }


def whole_kernel(names, *refs):
    refs = dict(zip(names, refs))
    refs["flat"] = refs["grads"]
    layer, swap = Layer(refs), Exchange(refs)
    swap.params_copy().start()
    layer.load()
    swap.greet()
    swap.frame_own()
    layer.start()
    swap.greeted()
    swap.send_vectors_line()
    for part in range(PAIRS):
        swap.send_line(0, part, (3, 2, 1))
    swap.send_line(3, 0, (1, 2, 3))
    swap.send_line(2, 0, (3, 2, 1))
    swap.send_line(1, 0, (3,))
    own, second, third = swap.plane_order()
    swap.own_first(lambda: swap.send_next(own))
    swap.send_all(0)
    swap.send_line(1, 0, (2, 1))
    swap.send_vectors_plane()
    swap.send_all(1)
    swap.send_core(0, 0)
    swap.own_first(lambda: swap.send_halves(own))
    swap.send_all(2)
    swap.others_first(lambda: swap.receive_line(own), lambda: swap.send_next(own))
    swap.finish_vectors_plane()
    layer.load_vectors()
    swap.finish_gather(0, 0)
    layer.query_key_value(0)
    layer.attend_first(0)
    swap.receive_line(second)
    swap.send_next(second)
    swap.send_core(0, 1)


    @pl.loop(0, PAIRS)
    def _(pair):
        layer.attend_step(2 * pair, 2 * pair + 1)

        @pl.when(pair == 0)
        def _():
            swap.others_first(lambda: swap.send_halves(own))

        @pl.when(pair == 1)
        def _():
            swap.receive_line(third)
            swap.send_next(third)

        @pl.when(pair == 2)
        def _():
            swap.send_halves(third)

        @pl.when(pair < PAIRS - 1)
        def _():
            swap.finish_gather(0, pair + 1)
            layer.query_key_value(pair + 1)

        layer.attend_step(2 * pair + 1, jnp.minimum(2 * pair + 2, HEADS - 1))

        @pl.when(pair == 0)
        def _():
            swap.send_core(0, 2)

        @pl.when(pair == 1)
        def _():
            swap.send_halves(second)
            swap.send_core(own)

    swap.send_core(second)
    swap.send_core(third)
    swap.finish_gather(1)
    layer.after_attention()
    swap.finish_gather(2)
    layer.up_weights()

    def before_down():
        swap.finish_gather(3)
        layer.down_weights()

    layer.feed_forward(before_down)
    for block in range(PAIRS):
        layer.grads[block, ROW_VEC:, :] = jnp.zeros((ALL_ROWS - ROW_VEC, 128), BF)
    layer.down_grad(D, FF)
    swap.reduce_core(3)
    layer.down_grad(0, D)
    swap.drain_gather()
    layer.hidden_grad()
    swap.reduce_halves(3)
    layer.up_grad(D // 2)
    swap.reduce_core(2)
    layer.first_norm_grad((0,))
    layer.up_grad(0)
    swap.reduce_next(3)
    swap.reduce_halves(2)
    layer.first_norm_grad((1, 2))
    layer.out_grad()
    swap.reduce_core(1)


    @pl.loop(0, PAIRS)
    def _(pair):
        def early():
            @pl.when(pair == 0)
            def _():
                swap.reduce_halves(1)

        def late():
            @pl.when(pair == 0)
            def _():
                swap.reduce_next(2)

            @pl.when(pair > 0)
            def _():
                swap.reduce_all(pair - 1)

        layer.pair_backward(pair, {3: early, 7: late})
        swap.reduce_core(0, pair)

        @pl.when(pair == 0)
        def _():
            swap.reduce_next(1)
            swap.reduce_line(3)

        @pl.when(pair == 1)
        def _():
            swap.reduce_line(2)
            swap.reduce_line(1)

    swap.reduce_line(0, 0)
    layer.vector_grads()
    swap.reduce_vectors_core()

    def last_flat():
        swap.reduce_all(2)
        swap.reduce_vectors_flat()
        swap.reduce_line(0, 1)

    layer.input_grad_step({1: last_flat})
    swap.reduce_line(0, 2)
    swap.reduce_vectors_line()
    for plane in (1, 2, 3):
        swap.drain_sum(plane)
        swap.finish_line(plane)
    for part in (0, 1):
        swap.drain_sum(0, part)
        swap.finish_line(0, part)
    swap.finish_vectors()
    swap.unframe((0, 1), False)
    swap.drain_sum(0, 2)
    swap.finish_line(0, 2)
    swap.unframe((2,), True)


def whole_layer(tokens, cotangent, own_params, subnets, lengths):
    rows = tokens.shape[0]
    scratch = scratch_refs() | exchange_refs(own_params.shape[0])
    inputs = ["tokens", "cotangent", "own_params", "subnets", "lengths"]
    outputs = ["layer_out", "input_grad", "own_grad"]
    spaces = [pl.ANY] * 3 + [pltpu.SMEM] * 2
    return pl.pallas_call(
        functools.partial(whole_kernel, inputs + outputs + list(scratch)),
        out_shape=(
            pltpu.VMEM((rows, D), BF),
            pltpu.VMEM((rows, D), F32),
            pltpu.VMEM(own_params.shape, F32),
        ),
        in_specs=[pl.BlockSpec(memory_space=space) for space in spaces],
        out_specs=[pl.BlockSpec(memory_space=pltpu.VMEM)] * 3,
        scratch_shapes=list(scratch.values()),
        compiler_params=pltpu.CompilerParams(
            vmem_limit_bytes=VMEM_LIMIT, collective_id=0, has_side_effects=True
        ),
    )(tokens, cotangent, own_params, subnets, lengths)


def emit_kernel(*refs):
    sems, half = refs[-1], len(refs) // 2
    copies = [pltpu.make_async_copy(refs[i], refs[half + i], sems.at[i]) for i in range(half)]
    for copy in copies:
        copy.start()
    for copy in copies:
        copy.wait()


def emit(*arrays):
    return pl.pallas_call(
        emit_kernel,
        out_shape=[jax.ShapeDtypeStruct(array.shape, array.dtype) for array in arrays],
        in_specs=[pl.BlockSpec(memory_space=pltpu.VMEM)] * len(arrays),
        out_specs=[pl.BlockSpec(memory_space=pl.ANY)] * len(arrays),
        scratch_shapes=[pltpu.SemaphoreType.DMA((len(arrays),))],
        compiler_params=pltpu.CompilerParams(vmem_limit_bytes=8 * 2**20),
    )(*arrays)


def local_kernel(names, *refs):
    refs = dict(zip(names, refs))
    refs["vec_par"] = refs["flat"].at[:, ROW_VEC:, :]
    layer = Layer(refs)
    layer.load()
    layer.start()
    layer.load_vectors()
    for pair in range(PAIRS):
        layer.query_key_value(pair)
    layer.attend_first(0)

    @pl.loop(0, HEADS)
    def _(head):
        layer.attend_step(head, jnp.minimum(head + 1, HEADS - 1))

    layer.after_attention()
    layer.up_weights()
    layer.feed_forward(layer.down_weights)
    layer.down_grad(0, FF)
    layer.hidden_grad()
    layer.up_grad(0)
    layer.up_grad(D // 2)
    layer.first_norm_grad(range(LIVE // TILE))
    layer.out_grad()
    @pl.loop(0, PAIRS)
    def _(pair):
        layer.pair_backward(pair, {})

    layer.input_grad_step({})
    layer.vector_grads()
    for block in range(PAIRS):
        layer.grads[block, ROW_VEC:, :] = layer.grad_vecs[:, block * 128 : block * 128 + 128].astype(BF)


def local_layer(tokens, cotangent, flat, subnets, lengths):
    rows = tokens.shape[0]
    scratch = scratch_refs() | {"grad_vecs": pltpu.VMEM((16, D), F32)}
    inputs = ["tokens", "cotangent", "flat", "subnets", "lengths"]
    outputs = ["layer_out", "input_grad", "grads"]
    spaces = [pl.ANY] * 2 + [pltpu.VMEM] + [pltpu.SMEM] * 2
    return pl.pallas_call(
        functools.partial(local_kernel, inputs + outputs + list(scratch)),
        out_shape=(
            jax.ShapeDtypeStruct((rows, D), BF),
            jax.ShapeDtypeStruct((rows, D), F32),
            jax.ShapeDtypeStruct((PAIRS, ALL_ROWS, 128), BF),
        ),
        in_specs=[pl.BlockSpec(memory_space=space) for space in spaces],
        out_specs=[pl.BlockSpec(memory_space=pltpu.VMEM)] * 3,
        scratch_shapes=list(scratch.values()),
        compiler_params=pltpu.CompilerParams(vmem_limit_bytes=VMEM_LIMIT),
    )(tokens, cotangent, flat, subnets, lengths)


def on_device(tokens, cotangent, params, subnets, lengths):
    flat = lax.all_gather(params, ("group", "item"), axis=0, tiled=True)
    flat = flat.reshape(-1, D)
    whole = flat.shape[0]
    flat = jnp.pad(flat, ((0, ALL_ROWS - whole), (0, 0)))
    flat = jnp.swapaxes(flat.reshape(ALL_ROWS, PAIRS, 128), 0, 1)
    layer_out, input_grad, grads = local_layer(tokens[0], cotangent[0], flat, subnets, lengths[0])
    grad = jnp.swapaxes(grads[:, :whole], 0, 1).astype(F32).reshape(-1)
    param_grad = lax.psum_scatter(grad, ("group", "item"), scatter_dimension=0, tiled=True)
    return layer_out[None], input_grad[None], param_grad


def on_known_device(tokens, cotangent, params, subnets, lengths):
    results = whole_layer(tokens[0], cotangent[0], params, subnets, lengths[0])
    layer_out, input_grad, own_grad = emit(*results)
    return layer_out[None], input_grad[None], own_grad


def solution(mesh):
    in_specs = (
        P("group", "item", None),
        P("group", "item", None),
        P(("group", "item")),
        P("group", None),
        P("group", "item", None),
    )
    out_specs = (P("group", "item", None), P("group", "item", None), P(("group", "item")))
    known = mesh.shape["group"] == 16 and mesh.shape["item"] == 2
    return jax.shard_map(
        on_known_device if known else on_device, mesh=mesh, in_specs=in_specs, out_specs=out_specs, check_vma=False
    )
```

```python
import functools

import jax
import jax.numpy as jnp
from jax import lax
from jax.experimental import pallas as pl
from jax.experimental.pallas import tpu as pltpu
from jax.sharding import PartitionSpec as P

HD = 64
HEADS = 6
D = 384
FF = 1536
LIVE = 960
PAIRS = HEADS // 2
CHUNKS = FF // D
BLOCK = 256
TILE = 320
WIDE = 512
BIG = 1e30
BF = jnp.bfloat16
F32 = jnp.float32
ROW_Q, ROW_K, ROW_V, ROW_O, ROW_UP, ROW_DOWN, ROW_VEC = 0, 384, 768, 1152, 1536, 3072, 4608
ALL_ROWS = 4624
STEP, FRAME, TWO, HALF = 144, 160, 304, 80
PLANES = 4
MESH = pl.DeviceIdType.MESH
VMEM_LIMIT = 61 * 2**20


def dot(left, right):
    return jnp.dot(left, right, preferred_element_type=F32)


def dot_nt(left, right):
    return lax.dot_general(left, right, (((1,), (1,)), ((), ())), preferred_element_type=F32)


def dot_tn(left, right):
    return lax.dot_general(left, right, (((0,), (0,)), ((), ())), preferred_element_type=F32)


def iota(shape, axis):
    return lax.broadcasted_iota(jnp.int32, shape, axis)


def lanes_at(start, size=128):
    return pl.ds(pl.multiple_of(start, 128), size)


def below(shape, axis, bound):
    return jnp.where(iota(shape, axis) < bound, 1.0, 0.0).astype(F32)


def key_range(block):
    first = max(0, block * BLOCK - 479) // 96 * 96
    last = min(LIVE, -(-(block * BLOCK + BLOCK + 479) // 32) * 32)
    return first, last


def gelu_parts(z):
    cdf = 0.5 + 0.5 * lax.erf(z * 0.7071067811865476)
    bell = jnp.exp2((z * z) * -0.7213475204444817 - 1.3257480647361593)
    return z * cdf, cdf + z * bell


def norm_forward(hidden, gain, shift, feature, inv_count):
    center = (hidden - jnp.sum(hidden * feature, axis=-1, keepdims=True) * inv_count) * feature
    inverse = lax.rsqrt(jnp.sum(center * center, axis=-1, keepdims=True) * inv_count + 1e-05)
    normed = center * inverse
    return normed * gain + shift, normed, inverse


def norm_backward(grad, normed, inverse, gain, feature, inv_count):
    scaled = grad * gain
    first = jnp.sum(scaled, axis=-1, keepdims=True) * inv_count
    second = jnp.sum(scaled * normed, axis=-1, keepdims=True) * inv_count
    return inverse * (scaled - first - normed * second) * feature


def col_sum(value):
    return jnp.sum(value, axis=0, keepdims=True)


class Layer:
    def __init__(self, refs):
        self.__dict__.update(refs)
        self.d_f, self.norm_low = self.low.at[0], self.low.at[1]
        self.cot = self.layer_out
        self.d_a, self.dot_t = self.xm, self.v_t
        for index, name in enumerate(("norm_one", "normed_one", "grad_second")):
            setattr(self, name, self.hold.at[:, index * D : index * D + D])
        self.lanes = self.expo.shape[2]
        width, heads, hidden = self.subnets[0, 0], self.subnets[0, 1], self.subnets[0, 2]
        self.width, self.attend, self.hidden = width, heads * HD, hidden
        self.inv_count = 1.0 / jnp.full((1, 1), width, jnp.int32).astype(F32)

    def row_mask(self, cols, bound, offset=0):
        return jnp.where(iota((1, cols), 1) + offset < bound, 1.0, 0.0).astype(F32)

    def col_mask(self, rows, bound, offset=0):
        return jnp.where(iota((rows, 1), 0) + offset < bound, 1.0, 0.0).astype(F32)

    def feature(self):
        return self.row_mask(D, self.width)

    def vector(self, index):
        mask = self.attend if index < 2 else self.width
        return self.vecs[4 + index : 5 + index, :] * self.row_mask(D, mask)

    def add_sum(self, index, value, first):
        part = value[:8, :]
        for start in range(8, value.shape[0], 8):
            part = part + value[start : start + 8, :]
        if first:
            self.sums[index] = part
        else:
            self.sums[index] += part


    def tokens_copy(self):
        return pltpu.make_async_copy(self.tokens.at[pl.ds(0, LIVE)], self.xm, self.io_sem.at[0])

    def cotangent_copy(self):
        return pltpu.make_async_copy(self.cotangent.at[pl.ds(0, LIVE)], self.cot.at[pl.ds(0, LIVE)], self.io_sem.at[1])

    def load(self):
        self.tokens_copy().start()
        self.cotangent_copy().start()

    def start(self):
        pad = self.lanes - LIVE
        self.input_grad[LIVE:, :] = jnp.zeros((self.input_grad.shape[0] - LIVE, D), F32)
        self.cot[LIVE:, :] = jnp.zeros((self.cot.shape[0] - LIVE, D), BF)
        self.dot_t[:, :, LIVE:] = jnp.zeros((HEADS, HD, pad), BF)
        self.q_t[:, :, LIVE:] = jnp.zeros((HEADS, HD, pad), BF)
        self.delta[:, :, LIVE:] = jnp.zeros((HEADS, 1, pad), F32)
        self.do_s[LIVE:, :] = jnp.zeros((pad, D), BF)
        self.q_rows[LIVE:, :] = jnp.zeros((pad, D), BF)
        ends = []
        total = 0
        for index in range(4):
            total = total + self.lengths[0, index]
            ends.append(total)
        lane = iota((HD, self.lanes), 1)
        seg = sum((lane >= end).astype(jnp.int32) for end in ends)
        part = iota((HD, self.lanes), 0)
        self.far[...] = jnp.where((part < 4) & (part != seg), -BIG, 0.0).astype(BF)
        row = iota((LIVE, 128), 0)
        seg = sum((row >= end).astype(jnp.int32) for end in ends[:3])
        self.hot[...] = jnp.where(iota((LIVE, 128), 1) - HD == seg, 1.0, 0.0).astype(BF)
        fe = self.feature().astype(BF)
        self.tokens_copy().wait()
        for rows in row_tiles():
            self.xm[rows, :] = self.xm[rows, :] * fe
        for part in range(PAIRS):
            lanes = slice(part * 128, part * 128 + 128)
            self.xt[lanes, :] = self.xm[:, lanes].T
        self.xt[D:, :] = jnp.ones((self.xt.shape[0] - D, LIVE), BF)

    def load_vectors(self):
        for part in range(PAIRS):
            lanes = slice(part * 128, part * 128 + 128)
            self.vecs[:, lanes] = self.vec_par[part].astype(F32)
        for chunk in range(CHUNKS):
            cols = slice(chunk * D, chunk * D + D)
            self.bias[:, cols] = self.vecs[chunk : chunk + 1, :] * self.row_mask(D, self.hidden, chunk * D)


    def query_key_value(self, pair):
        lanes = lanes_at(pair * 128)
        seen = self.row_mask(128, self.attend, pair * 128)
        mask = self.col_mask(D, self.width) * seen
        for index, row in enumerate((ROW_Q, ROW_K, ROW_V)):
            weight = (self.flat[pair, row : row + D, :].astype(F32) * mask).astype(BF)
            self.w_qkv[:, lanes_at(pair * D + index * 128)] = weight
        bias_q, bias_v = self.vecs[4:5, lanes] * seen, self.vecs[5:6, lanes] * seen
        weight = self.w_qkv[:, lanes_at(pair * D, D)]
        for start in range(0, LIVE, BLOCK):
            rows = slice(start, min(start + BLOCK, LIVE))
            size = rows.stop - rows.start
            even = iota((size, 128), 1) < HD
            out = dot(self.xm[rows, :], weight)
            q = (out[:, :128] + bias_q).astype(BF)
            self.q_rows[rows, lanes] = q
            k32 = out[:, 128:256]
            k = k32.astype(BF)
            hot = self.hot[rows, :]
            for head, moved in ((2 * pair, k32), (2 * pair + 1, pltpu.roll(k32, HD, 1))):
                place, cols = self.keys_place(head)
                self.low[place, rows, cols] = jnp.where(even, moved, hot.astype(F32)).astype(BF)
            v = (out[:, 256:] + bias_v).astype(BF)
            self.v_rows[rows, lanes] = v
            turned = (q * jnp.asarray(0.125, BF)).T
            self.q_t[2 * pair, :, rows] = turned[:HD, :]
            self.q_t[2 * pair + 1, :, rows] = turned[HD:, :]
            turned = k.T
            self.k_t[2 * pair, :, rows] = turned[:HD, :]
            self.k_t[2 * pair + 1, :, rows] = turned[HD:, :]
            turned = v.T
            self.v_t[2 * pair, :, rows] = turned[:HD, :]
            self.v_t[2 * pair + 1, :, rows] = turned[HD:, :]

    def keys_place(self, head):
        return head // PAIRS, lanes_at(head % PAIRS * 128)

    def score(self, head, block):
        cols = slice(block * BLOCK, block * BLOCK + BLOCK)
        first, last = key_range(block)
        right = jnp.concatenate([self.q_t[head, :, cols], self.far[:, cols]], axis=0)
        place, lanes = self.keys_place(head)
        self.hold[first:last, cols] = dot(self.low[place, first:last, lanes], right)

    def soft(self, head, block):
        cols = slice(block * BLOCK, block * BLOCK + BLOCK)
        first, last = key_range(block)
        scores = self.hold[first:last, cols]
        expo = jnp.exp(scores - jnp.max(scores, axis=0, keepdims=True))
        inv = 1.0 / jnp.sum(expo, axis=0, keepdims=True)
        expo = expo.astype(BF)
        self.expo[head, first:last, cols] = expo
        self.inv[head, :, cols] = inv
        return expo, inv

    def attend_first(self, head):
        for block in range(self.lanes // BLOCK):
            self.score(head, block)

    def attend_step(self, head, after):
        for block in range(self.lanes // BLOCK):
            cols = slice(block * BLOCK, block * BLOCK + BLOCK)
            first, last = key_range(block)
            expo, inv = self.soft(head, block)
            self.score(after, block)
            mixed = dot(self.v_t[head, :, first:last], expo) * inv
            self.o_t[head, :, cols] = mixed.astype(BF)

    def after_attention(self):
        mask = self.col_mask(D, self.attend) * self.feature()
        for part in range(PAIRS):
            lanes = slice(part * 128, part * 128 + 128)
            rows = self.flat[part, ROW_O : ROW_O + D, :].astype(F32)
            self.w_out[:, lanes] = (rows * mask[:, lanes]).astype(BF)
        fe, bias, gain, shift = self.feature(), self.vector(2), self.vector(3), self.vector(4)
        for start in range(0, LIVE, BLOCK):
            size = min(BLOCK, LIVE - start)
            rows = slice(start, start + size)
            mixed = self.o_t[:, :, start : start + BLOCK].reshape(D, BLOCK)
            attended = dot_tn(mixed, self.w_out[...])[:size, :]
            hidden = self.xm[rows, :].astype(F32) + attended + bias
            norm, normed, inverse = norm_forward(hidden, gain, shift, fe, self.inv_count)
            self.norm_one[rows, :] = norm
            self.normed_one[rows, :] = normed
            self.inverse_one[rows, :] = jnp.broadcast_to(inverse, (size, 128))
            self.norm_low[rows, :] = norm.astype(BF)

    def up_weights(self, start):
        half = D // 2
        rows = slice(start * CHUNKS, (start + half) * CHUNKS)
        for part in range(PAIRS):
            self.wide[part, rows, :] = self.flat[part, ROW_UP + rows.start : ROW_UP + rows.stop, :].astype(F32)
        inside = self.col_mask(half, self.width, start)
        for chunk in range(CHUNKS):
            mask = inside * self.row_mask(D, self.hidden, chunk * D)
            for part in range(PAIRS):
                lanes = slice(part * 128, part * 128 + 128)
                piece = self.wide[part, pl.ds(rows.start + chunk, half, stride=CHUNKS), :]
                self.w_up[start : start + half, chunk * D + part * 128 : chunk * D + part * 128 + 128] = (
                    piece * mask[:, lanes]
                ).astype(BF)

    def down_weights(self):
        mask = self.feature()
        for chunk in range(CHUNKS):
            rows = slice(chunk * D, chunk * D + D)
            hidden = self.col_mask(D, self.hidden, chunk * D)
            for part in range(PAIRS):
                lanes = slice(part * 128, part * 128 + 128)
                piece = self.flat[part, ROW_DOWN + chunk * D : ROW_DOWN + chunk * D + D, :].astype(F32)
                self.w_down[rows, lanes] = (piece * (hidden * mask[:, lanes])).astype(BF)

    def up_tile(self, rows):
        low = self.norm_low[rows, :]
        for start in range(0, FF, BLOCK):
            cols = slice(start, start + BLOCK)
            act, slope = gelu_parts(dot(low, self.w_up[:, cols]) + self.bias[:, cols])
            self.act[rows, cols] = act.astype(BF)
            self.slope[rows, cols] = slope.astype(BF)

    def down_tile(self, rows):
        fe = self.feature()
        bias, gain, shift = self.vector(5), self.vector(6), self.vector(7)
        second = self.norm_one[rows, :] + dot(self.act[rows, :FF], self.w_down[...]) + bias
        result, normed, inverse = norm_forward(second, gain, shift, fe, self.inv_count)
        grad = self.cot[rows, :].astype(F32)
        self.cot[rows, :] = result.astype(BF)
        grad_second = norm_backward(grad, normed, inverse, gain, fe, self.inv_count)
        self.grad_second[rows, :] = grad_second
        low = grad_second.astype(BF)
        self.d_f[rows, :] = low
        first = rows.start == 0
        self.add_sum(10, grad * normed, first)
        self.add_sum(11, grad, first)
        self.add_sum(9, low.astype(F32), first)

    def feed_forward(self, before_down):
        for rows in row_tiles():
            self.up_tile(rows)
        before_down()
        self.cotangent_copy().wait()
        for rows in row_tiles():
            self.down_tile(rows)


    def down_grad(self, start, stop):
        fe = self.feature()
        for first in range(start, stop, WIDE):
            size = min(WIDE, stop - first)
            grad = dot_tn(self.d_f[...], self.act[:, first : first + size]).astype(BF).T
            grad = grad * (self.col_mask(size, self.hidden, first) * fe).astype(BF)
            for part in range(PAIRS):
                lanes = slice(part * 128, part * 128 + 128)
                self.grads[part, ROW_DOWN + first : ROW_DOWN + first + size, :] = grad[:, lanes]

    def hidden_tile(self, rows):
        d_f = self.d_f[rows, :]
        for start in range(0, FF, BLOCK):
            cols = slice(start, start + BLOCK)
            grad = dot_nt(d_f, self.w_down[cols, :])
            dz = (grad * self.slope[rows, cols].astype(F32)).astype(BF)
            self.slope[rows, cols] = dz
            part = dz[:8, :].astype(F32)
            for row in range(8, rows.stop - rows.start, 8):
                part = part + dz[row : row + 8, :].astype(F32)
            if rows.start == 0:
                self.hidden_sums[:, cols] = part
            else:
                self.hidden_sums[:, cols] += part

    def first_norm_tile(self, rows):
        gain, fe = self.vector(3), self.feature()
        normed = self.normed_one[rows, :]
        grad = self.grad_second[rows, :] + dot_nt(self.slope[rows, :], self.w_up[...])
        grad_first = norm_backward(grad, normed, self.inverse_one[rows, :1], gain, fe, self.inv_count)
        self.norm_one[rows, :] = grad_first
        low = grad_first.astype(BF)
        self.d_a[rows, :] = low
        first = rows.start == 0
        self.add_sum(7, grad * normed, first)
        self.add_sum(8, grad, first)
        self.add_sum(6, low.astype(F32), first)

    def hidden_grad(self):
        for rows in row_tiles():
            self.hidden_tile(rows)

    def first_norm_grad(self, tiles):
        for index in tiles:
            self.first_norm_tile(row_tiles()[index])

    def up_grad(self, start):
        half = D // 2
        low = self.norm_low[:, start : start + half]
        for first in range(0, FF, WIDE):
            mask = self.col_mask(half, self.width, start) * self.row_mask(WIDE, self.hidden, first)
            grad = dot_tn(low, self.slope[:, first : first + WIDE]) * mask
            for lane in range(0, WIDE, 128):
                chunk, part = (first + lane) // D, (first + lane) % D // 128
                rows = pl.ds(start * CHUNKS + chunk, half, stride=CHUNKS)
                self.wide[part, rows, :] = grad[:, lane : lane + 128]
        rows = slice(start * CHUNKS, (start + half) * CHUNKS)
        for part in range(PAIRS):
            self.grads[part, ROW_UP + rows.start : ROW_UP + rows.stop, :] = self.wide[part, rows, :].astype(BF)

    def out_grad(self):
        fe = self.feature()
        d_a = self.d_a[...]
        half = D // 2
        for start in (0, half):
            rows = slice(start, start + half)
            heads = range(start // HD, (start + half) // HD)
            mask = self.col_mask(half, self.attend, start) * fe
            o_t = self.o_t[heads.start : heads.stop, :, :LIVE].reshape(half, LIVE)
            grad = (dot(o_t, d_a) * mask).astype(BF)
            for part in range(PAIRS):
                lanes = slice(part * 128, part * 128 + 128)
                self.grads[part, ROW_O + start : ROW_O + start + half, :] = grad[:, lanes]
            mixed = dot_nt(self.w_out[rows, :], d_a)
            for head in heads:
                own = mixed[head * HD - start : head * HD - start + HD, :] * self.inv[head, :, :LIVE]
                self.delta[head, :, :LIVE] = col_sum(own * self.o_t[head, :, :LIVE].astype(F32))
                self.dot_t[head, :, :LIVE] = own.astype(BF)
        for pair in range(PAIRS):
            both = self.dot_t[2 * pair : 2 * pair + 2, :, :LIVE].reshape(128, LIVE)
            self.do_s[:LIVE, pair * 128 : pair * 128 + 128] = both.T

    def score_place(self, odd, block):
        if not odd:
            return self.act, block * BLOCK
        return ((self.act, 4 * BLOCK), (self.act, 5 * BLOCK), (self.slope, PAIRS * D), (self.d_f, 0))[block]

    def first_lane(self, pair, index):
        return lanes_at(pair * D + index * 128)

    def prob_grad(self, pair, odd, block):
        cols = slice(block * BLOCK, block * BLOCK + BLOCK)
        first, last = key_range(block)
        right = self.dot_t[2 * pair + odd, :, cols]
        none = jnp.zeros_like(right)
        right = jnp.concatenate([none, right] if odd else [right, none], axis=0)
        return dot(self.v_rows[first:last, lanes_at(pair * 128)], right)

    def score_grad(self, pair, odd, block, grad):
        head = 2 * pair + odd
        cols = slice(block * BLOCK, block * BLOCK + BLOCK)
        first, last = key_range(block)
        grad = self.expo[head, first:last, cols].astype(F32) * (grad - self.delta[head, :, cols])
        grad = grad.astype(BF)
        place, start = self.score_place(odd, block)
        place[first:last, start : start + BLOCK] = grad
        return grad

    def query_grad(self, pair, odd, block, grad):
        head = 2 * pair + odd
        cols = slice(block * BLOCK, block * BLOCK + BLOCK)
        first, last = key_range(block)
        dq = dot(self.k_t[head, :, first:last], grad) * 0.125
        self.dq_t[odd * HD : odd * HD + HD, cols] = dq.astype(BF)

    def pair_backward(self, pair, hooks):
        lanes = lanes_at(pair * 128)
        blocks = self.lanes // BLOCK
        ranges = [key_range(block) for block in range(blocks)]
        edges = sorted({edge for both in ranges for edge in both})
        cuts = []
        for low, high in zip(edges[:-1], edges[1:]):
            used = [b for b in range(blocks) if ranges[b][0] <= low and high <= ranges[b][1]]
            cuts.append((slice(low, high), slice(used[0] * BLOCK, used[-1] * BLOCK + BLOCK)))
        own = [jnp.where((iota((1, 128), 1) >= HD) == bool(odd), 1.0, 0.0).astype(BF) for odd in (0, 1)]
        d_out = [self.do_s[:, lanes] * own[odd] for odd in (0, 1)]
        items = [(odd, block) for odd in (0, 1) for block in range(blocks)]
        grad = self.prob_grad(pair, *items[0])
        for index, (odd, block) in enumerate(items):
            if index % 2 == 0 and index // 2 < len(cuts):
                rows, span = cuts[index // 2]
                dv = sum(dot(self.expo[2 * pair + odd_, rows, span], d_out[odd_][span]) for odd_ in (0, 1))
                self.slope[rows, self.first_lane(pair, 2)] = dv.astype(BF)
            after = self.prob_grad(pair, *items[index + 1]) if index + 1 < len(items) else None
            low = self.score_grad(pair, odd, block, grad)
            grad = after
            self.query_grad(pair, odd, block, low)
            if index in hooks:
                hooks[index]()
        queries = [self.q_rows[:, lanes] * own[odd] for odd in (0, 1)]
        for rows, span in cuts:
            dk = 0.0
            for odd in (0, 1):
                places = [self.score_place(odd, block) for block in range(span.start // BLOCK, span.stop // BLOCK)]
                first = 0
                for last in range(1, len(places) + 1):
                    if last == len(places) or places[last][0] is not places[first][0]:
                        place, start = places[first]
                        begin, size = span.start + first * BLOCK, (last - first) * BLOCK
                        dk = dk + dot(place[rows, start : start + size], queries[odd][begin : begin + size])
                        first = last
            self.slope[rows, self.first_lane(pair, 1)] = (dk * 0.125).astype(BF)
        self.slope[:, self.first_lane(pair, 0)] = self.dq_t[:, :LIVE].T
        mask = self.col_mask(D, self.width) * self.row_mask(128, self.attend, pair * 128)
        all_three = self.slope[:, lanes_at(pair * D, D)]
        grad = dot(self.xt[...], all_three)
        for index, row in enumerate((ROW_Q, ROW_K, ROW_V)):
            self.grads[pair, row : row + D, :] = (grad[:D, index * 128 : index * 128 + 128] * mask).astype(BF)
        self.sums[4, :, lanes] = grad[D : D + 8, :128] * 0.125
        self.sums[5, :, lanes] = grad[D : D + 8, 256:] * 0.125

    def input_grad_step(self, hooks):
        fe = self.feature()
        for index, rows in enumerate(row_tiles()):
            total = self.norm_one[rows, :] + dot_nt(self.slope[rows, : PAIRS * D], self.w_qkv[...])
            self.input_grad[rows, :] = total * fe
            if index in hooks:
                hooks[index]()

    def vector_grads(self):
        for index in range(12):
            if index < CHUNKS:
                total = jnp.sum(self.hidden_sums[:, index * D : index * D + D], axis=0, keepdims=True)
                mask = self.row_mask(D, self.hidden, index * D)
            else:
                total = jnp.sum(self.sums[index], axis=0, keepdims=True)
                mask = self.row_mask(D, self.attend if index < 6 else self.width)
            self.grad_vecs[index : index + 1, :] = total * mask
        self.grad_vecs[12:, :] = jnp.zeros((4, D), F32)


def row_tiles():
    return [slice(start, min(start + TILE, LIVE)) for start in range(0, LIVE, TILE)]


def scratch_refs():
    vmem = pltpu.VMEM
    lanes = -(-LIVE // BLOCK) * BLOCK
    return {
        "xm": vmem((LIVE, D), BF),
        "hold": vmem((LIVE, 3 * D), F32),
        "xt": vmem((D + 16, LIVE), BF),
        "hot": vmem((LIVE, 128), BF),
        "far": vmem((HD, lanes), BF),
        "vecs": vmem((16, D), F32),
        "bias": vmem((1, FF), F32),
        "sums": vmem((12, 8, D), F32),
        "hidden_sums": vmem((8, FF), F32),
        "w_qkv": vmem((D, PAIRS * D), BF),
        "w_out": vmem((D, D), BF),
        "w_up": vmem((D, FF), BF),
        "w_down": vmem((FF, D), BF),
        "wide": vmem((PAIRS, FF, 128), F32),
        "q_rows": vmem((lanes, D), BF),
        "q_t": vmem((HEADS, HD, lanes), BF),
        "k_t": vmem((HEADS, HD, LIVE), BF),
        "v_rows": vmem((LIVE, D), BF),
        "v_t": vmem((HEADS, HD, lanes), BF),
        "expo": vmem((HEADS, LIVE, lanes), BF),
        "inv": vmem((HEADS, 1, lanes), F32),
        "o_t": vmem((HEADS, HD, lanes), BF),
        "inverse_one": vmem((LIVE, 128), F32),
        "low": vmem((2, LIVE, D), BF),
        "act": vmem((LIVE, FF), BF),
        "slope": vmem((LIVE, FF), BF),
        "do_s": vmem((lanes, D), BF),
        "delta": vmem((HEADS, 1, lanes), F32),
        "dq_t": vmem((128, lanes), BF),
        "io_sem": pltpu.SemaphoreType.DMA((3,)),
    }


class Exchange:
    def __init__(self, refs):
        self.__dict__.update(refs)
        group, self.x = lax.axis_index("group"), lax.axis_index("item")
        self.z, self.y, self.c = group // 4, (group // 2) % 2, group % 2
        self.spot = 2 * self.y + self.x
        self.shard = 2 * group + self.x
        self.corner = (self.c == 1) & (self.spot == 3)

    def device(self, z, y, c, x):
        return (z * 4 + y * 2 + c, x)

    def line(self, step):
        return self.device((self.z + step) % PLANES, self.y, self.c, self.x)

    def plane_peer(self, step):
        y, x = (self.y + step // 4) % 2, (self.x + step % 2) % 2
        return self.device(self.z, y, (self.c + step // 2 % 2) % 2, x)

    def chip_peer(self, step):
        y, x = (self.y + step // 2) % 2, (self.x + step % 2) % 2
        return self.device(self.z, y, self.c, x)

    def spot_of(self, step):
        return 2 * ((self.y + step // 2) % 2) + (self.x + step % 2) % 2

    def core_peer(self):
        return self.device(self.z, self.y, 1 - self.c, self.x)

    def greet(self):
        barrier = pltpu.get_barrier_semaphore()
        peers = [self.line(step) for step in (1, 2, 3)] + [self.plane_peer(step) for step in range(1, 8)]
        for peer in peers:
            pl.semaphore_signal(barrier, inc=1, device_id=peer, device_id_type=MESH)

    def greeted(self):
        pl.semaphore_wait(pltpu.get_barrier_semaphore(), 10)

    def copy(self, source, target, send, recv, peer):
        return pltpu.make_async_remote_copy(
            src_ref=source, dst_ref=target, send_sem=send, recv_sem=recv, device_id=peer, device_id_type=MESH
        )


    def offsets(self):
        shift = STEP * self.shard
        return shift // 128, shift % 128

    def params_copy(self):
        return pltpu.make_async_copy(self.own_params, self.shard_flat, self.io_sem.at[2])

    def frame_own(self):
        self.params_copy().wait()
        rows, count = self.shard_sum.shape[1], self.shard_flat.shape[0]
        full, rest = count // 128, count % 128
        spread = self.shard_sum.at[0]
        spread[:full, :] = self.shard_flat[pl.ds(0, full * 128)].reshape(full, 128).astype(F32)
        spread[full:, :] = jnp.zeros((rows - full, 128), F32)
        if rest:
            spread[full : full + 1, :rest] = self.shard_flat[pl.ds(full * 128, rest)].reshape(1, rest).astype(F32)
        up, across = self.offsets()
        turned = pltpu.roll(spread[...], across, 1)
        late = iota((rows, 128), 1) >= across
        same = jnp.where(late, turned, 0.0).astype(BF)
        carried = jnp.where(late, 0.0, turned).astype(BF)
        gap = 3 * iota((FRAME, rows), 0) - up - iota((FRAME, rows), 1)
        for part in range(PAIRS):
            here = jnp.where(gap == -part, 1.0, 0.0).astype(BF)
            after = jnp.where(gap == 1 - part, 1.0, 0.0).astype(BF)
            frame = dot(here, same) + dot(after, carried)
            self.land[self.z, part, self.c, self.spot] = frame.astype(BF)

    def vectors_line(self, step):
        sems = self.par_send.at[step - 1], self.par_recv.at[0]
        return self.copy(self.vec_par, self.vec_par, *sems, self.line(step))

    def vectors_plane(self, step):
        sems = self.par_send.at[step + 2], self.par_recv.at[1]
        return self.copy(self.vec_par, self.vec_par, *sems, self.plane_peer(step))

    def send_vectors_line(self):
        @pl.when(self.corner & (self.z == PLANES - 1))
        def _():
            self.vec_par[...] = self.land[PLANES - 1, :, 1, 3, STEP:, :]
            for step in (1, 2, 3):
                self.vectors_line(step).start()

    def send_vectors_plane(self):
        @pl.when(self.corner & (self.z != PLANES - 1))
        def _():
            self.vectors_line(1).wait_recv()

        @pl.when(self.corner)
        def _():
            for step in range(1, 8):
                self.vectors_plane(step).start()

    def finish_vectors_plane(self):
        @pl.when(jnp.logical_not(self.corner))
        def _():
            self.vectors_plane(1).wait_recv()

    def parts(self, plane, part):
        return pl.ds(part, 1) if isinstance(plane, int) and plane == 0 else slice(None)

    def blocks(self, plane, part):
        return [part] if plane == 0 else range(PAIRS)

    def item(self, plane, part):
        return part if isinstance(plane, int) and plane == 0 else 2 + plane

    def gather_line(self, plane, part, step):
        piece = self.land.at[plane, self.parts(plane, part), self.c, self.spot]
        sems = self.line_send.at[part, step - 1], self.line_recv.at[self.item(plane, part)]
        return self.copy(piece, piece, *sems, self.line(step))

    def send_line(self, plane, part, steps):
        @pl.when(self.z == plane)
        def _():
            for step in steps:
                self.gather_line(plane, part, step).start()

    def gather_all(self, part, step, spot):
        piece = self.land.at[0, pl.ds(part, 1), self.c, spot]
        sems = self.flat_send.at[3 * part + step - 1], self.flat_recv.at[3 * part + step - 1]
        return self.copy(piece, piece, *sems, self.chip_peer(step))

    def gather_next(self, plane, step, spot):
        piece = self.land.at[plane, :, self.c, spot]
        index = 5 + 4 * plane + step - 1
        return self.copy(piece, piece, self.flat_send.at[index], self.flat_recv.at[index], self.chip_peer(step))

    def gather_half(self, plane, step, spot):
        rows = pl.ds((2 - step) * HALF, HALF)
        piece = self.land.at[plane, :, self.c, spot, rows]
        index = 5 + 4 * plane + step + 1
        return self.copy(piece, piece, self.flat_send.at[index], self.flat_recv.at[index], self.chip_peer(step))

    def wait_line(self, plane, part):
        @pl.when(self.z != plane)
        def _():
            self.gather_line(plane, part, 1).wait_recv()

    def send_all(self, part):
        self.wait_line(0, part)
        for step in (3, 2, 1):
            self.gather_all(part, step, self.spot).start()

    def plane_order(self):
        second = jnp.where(self.z == 0, 3, jnp.where(self.z == 1, 2, 1))
        third = jnp.where(self.z % 3 == 0, 2, 3)
        return jnp.maximum(self.z, 1), second, third

    def own_first(self, action):
        @pl.when(self.z != 0)
        def _():
            action()

    def others_first(self, *actions):
        @pl.when(self.z == 0)
        def _():
            for action in actions:
                action()

    def receive_line(self, plane):
        self.copy_line(plane).wait_recv()

    def copy_line(self, plane):
        piece = self.land.at[plane, :, self.c, self.spot]
        return self.copy(piece, piece, self.line_send.at[1, 0], self.line_recv.at[2 + plane], self.line(1))

    def send_next(self, plane):
        for step in (2, 1):
            self.gather_next(plane, step, self.spot).start()

    def send_halves(self, plane):
        self.gather_next(plane, 1, self.spot_of(1)).wait_recv()
        self.gather_half(plane, 2, self.spot_of(1)).start()
        self.gather_next(plane, 2, self.spot_of(2)).wait_recv()
        self.gather_half(plane, 1, self.spot_of(2)).start()

    def gather_core(self, plane, part, core):
        piece = self.land.at[plane, self.parts(plane, part), core]
        item = self.item(plane, part)
        return self.copy(piece, piece, self.core_send.at[item], self.core_recv.at[item], self.core_peer())

    def send_core(self, plane, part=0):
        if isinstance(plane, int) and plane == 0:
            for step in (3, 2, 1):
                self.gather_all(part, step, self.spot_of(step)).wait_recv()
        else:
            for step in (2, 1):
                self.gather_half(plane, step, self.spot_of(3)).wait_recv()
        self.gather_core(plane, part, self.c).start()

    def finish_gather(self, plane, part=0):
        self.gather_core(plane, part, 1 - self.c).wait_recv()
        for place in range(8):
            y, c, x = place // 4, (place // 2) % 2, place % 2
            chunk = 8 * plane + place
            for block in self.blocks(plane, part):
                frame = self.land[plane, block, c, 2 * y + x]
                self.flat[block, chunk * STEP : chunk * STEP + STEP, :] = frame[:STEP, :]
                if chunk:
                    before = (chunk - 1) % 8
                    spot = 2 * (before // 4) + before % 2
                    tail = self.land[(chunk - 1) // 8, block, (before // 2) % 2, spot, STEP:, :]
                    both = tail + frame[: FRAME - STEP, :]
                    self.flat[block, chunk * STEP : chunk * STEP + FRAME - STEP, :] = both

    def drain_gather(self):
        @pl.when(self.corner & (self.z == PLANES - 1))
        def _():
            for step in (1, 2, 3):
                self.vectors_line(step).wait_send()

        @pl.when(self.corner)
        def _():
            for step in range(1, 8):
                self.vectors_plane(step).wait_send()

        for plane in range(PLANES):
            for part in range(PAIRS if plane == 0 else 1):

                @pl.when(self.z == plane)
                def _():
                    for step in (1, 2, 3):
                        self.gather_line(plane, part, step).wait_send()

                if plane == 0:
                    for step in (1, 2, 3):
                        self.gather_all(part, step, self.spot).wait_send()
                else:
                    for step in (1, 2):
                        self.gather_next(plane, step, self.spot).wait_send()
                        self.gather_half(plane, step, self.spot).wait_send()
                self.gather_core(plane, part, self.c).wait_send()


    def sum_core(self, plane, part, y):
        row = pl.multiple_of(STEP * (8 * plane + 4 * y + 2 * (1 - self.c)), 16)
        parts, item = self.parts(plane, part), 2 * self.item(plane, part) + y
        return self.copy(
            self.grads.at[parts, pl.ds(row, TWO)],
            self.core_land.at[plane % 3, y, parts],
            self.sum_core_send.at[item],
            self.sum_core_recv.at[item],
            self.core_peer(),
        )

    def sum_all(self, part, step):
        index = 3 * part + step - 1
        return self.copy(
            self.land.at[0, pl.ds(part, 1), 0, self.spot_of(step)],
            self.all_land.at[step - 1, pl.ds(part, 1)],
            self.sum_flat_send.at[index],
            self.sum_flat_recv.at[index],
            self.chip_peer(step),
        )

    def sum_half(self, plane, step):
        index = 5 + 4 * plane + step - 1
        return self.copy(
            self.land.at[plane, :, 0, self.spot_of(3), pl.ds((step - 1) * HALF, HALF)],
            self.half_land.at[plane - 1, step - 1],
            self.sum_flat_send.at[index],
            self.sum_flat_recv.at[index],
            self.chip_peer(step),
        )

    def sum_next(self, plane, step):
        index = 5 + 4 * plane + step + 1
        return self.copy(
            self.land.at[plane, :, 0, self.spot_of(step)],
            self.next_land.at[plane - 1, step - 1],
            self.sum_flat_send.at[index],
            self.sum_flat_recv.at[index],
            self.chip_peer(step),
        )

    def sum_line(self, plane, part, slot):
        parts, item = self.parts(plane, part), self.item(plane, part)
        return self.copy(
            self.plane_sum.at[plane, parts],
            self.line_land.at[slot, parts],
            self.sum_line_send.at[item],
            self.sum_line_recv.at[3 * part + slot],
            self.device(plane, self.y, self.c, self.x),
        )

    def reduce_core(self, plane, part=0):
        for y in (0, 1):
            self.sum_core(plane, part, y).start()

    def add_core(self, plane, part):
        for y in (0, 1):
            self.sum_core(plane, part, y).wait_recv()
            for block in self.blocks(plane, part):
                for x in (0, 1):
                    row = pl.multiple_of(STEP * (8 * plane + 4 * y + 2 * self.c + x), 16)
                    own = self.grads[block, pl.ds(row, FRAME), :]
                    other = self.core_land[plane % 3, y, block, x * STEP : x * STEP + FRAME, :]
                    self.land[plane, block, 0, 2 * y + x] = own + other

    def reduce_all(self, part):
        self.add_core(0, part)
        for step in (3, 2, 1):
            self.sum_all(part, step).start()

    def reduce_halves(self, plane):
        self.add_core(plane, 0)
        for step in (1, 2):
            self.sum_half(plane, step).start()

    def reduce_next(self, plane):
        for step in (1, 2):
            self.sum_half(plane, step).wait_recv()
            rows = slice((step - 1) * HALF, step * HALF)
            spot = self.spot_of(3 - step)
            for block in range(PAIRS):
                own = self.land[plane, block, 0, spot, rows, :]
                self.land[plane, block, 0, spot, rows, :] = own + self.half_land[plane - 1, step - 1, block]
            self.sum_next(plane, 3 - step).start()

    def reduce_line(self, plane, part=0):
        if plane == 0:
            for step in (1, 2, 3):
                self.sum_all(part, step).wait_recv()
        else:
            for step in (1, 2):
                self.sum_next(plane, step).wait_recv()
        for block in self.blocks(plane, part):
            total = self.land[plane, block, 0, self.spot]
            if plane == 0:
                total = (total + self.all_land[0, block]) + (self.all_land[1, block] + self.all_land[2, block])
            else:
                total = total + (self.next_land[plane - 1, 0, block] + self.next_land[plane - 1, 1, block])
            self.plane_sum[plane, block] = total

        @pl.when(self.z != plane)
        def _():
            self.sum_line(plane, part, (self.z - plane + 2 * PLANES - 1) % PLANES).start()

    def vector_core(self):
        peer = self.core_peer()
        return self.copy(self.grad_vecs, self.vec_core, self.vec_send.at[0], self.vec_recv.at[0], peer)

    def vector_flat(self, slot):
        peer = self.device(self.z, 1, 1, 1)
        return self.copy(self.vec_sum, self.vec_flat.at[slot], self.vec_send.at[1], self.vec_recv.at[1 + slot], peer)

    def vector_line(self, slot):
        peer = self.device(PLANES - 1, 1, 1, 1)
        return self.copy(self.vec_sum, self.vec_line.at[slot], self.vec_send.at[2], self.vec_recv.at[4 + slot], peer)

    def reduce_vectors_core(self):
        @pl.when(self.c == 0)
        def _():
            self.vector_core().start()

    def reduce_vectors_flat(self):
        @pl.when(self.c == 1)
        def _():
            self.vector_core().wait_recv()
            self.vec_sum[...] = self.grad_vecs[...] + self.vec_core[...]

            @pl.when(self.spot != 3)
            def _():
                self.vector_flat(2 - self.spot).start()

    def reduce_vectors_line(self):
        @pl.when(self.corner)
        def _():
            for slot in range(3):
                self.vector_flat(slot).wait_recv()
            self.vec_sum[...] = self.vec_sum[...] + self.vec_flat[0] + self.vec_flat[1] + self.vec_flat[2]

            @pl.when(self.z != PLANES - 1)
            def _():
                self.vector_line(self.z).start()

    def finish_vectors(self):
        @pl.when(self.corner & (self.z == PLANES - 1))
        def _():
            total = self.vec_sum[...]
            for slot in range(3):
                self.vector_line(slot).wait_recv()
                total = total + self.vec_line[slot]
            for block in range(PAIRS):
                self.total[block, STEP:, :] = total[:, block * 128 : block * 128 + 128]

        @pl.when(self.c == 0)
        def _():
            self.vector_core().wait_send()

        @pl.when((self.c == 1) & (self.spot != 3))
        def _():
            self.vector_flat(0).wait_send()

        @pl.when(self.corner & (self.z != PLANES - 1))
        def _():
            self.vector_line(0).wait_send()

    def finish_line(self, plane, part=0):
        @pl.when(self.z == plane)
        def _():
            for slot in range(3):
                self.sum_line(plane, part, slot).wait_recv()
            for block in self.blocks(plane, part):
                total = self.plane_sum[plane, block].astype(F32)
                for slot in range(3):
                    total = total + self.line_land[slot, block].astype(F32)
                self.total[block] = total

    def drain_sum(self, plane, part=0):
        @pl.when(self.z != plane)
        def _():
            self.sum_line(plane, part, 0).wait_send()

        if plane == 0:
            for step in (1, 2, 3):
                self.sum_all(part, step).wait_send()
        else:
            for step in (1, 2):
                self.sum_half(plane, step).wait_send()
                self.sum_next(plane, step).wait_send()
        for y in (0, 1):
            self.sum_core(plane, part, y).wait_send()

    def unframe(self, parts, last):
        rows = self.shard_sum.shape[1]
        up, across = self.offsets()
        gap = iota((rows, FRAME), 0) + up - 3 * iota((rows, FRAME), 1)
        here = self.shard_sum[0] if last else jnp.zeros((rows, 128), F32)
        carried = self.shard_sum[1] if last else jnp.zeros((rows, 128), F32)
        for block in parts:
            total = self.total[block]
            high = total.astype(BF)
            both = jnp.concatenate([high, (total - high.astype(F32)).astype(BF)], axis=1)
            moved = dot(jnp.where(gap == block, 1.0, 0.0).astype(BF), both)
            here = here + (moved[:, :128] + moved[:, 128:])
            moved = dot(jnp.where(gap == block - 1, 1.0, 0.0).astype(BF), both)
            carried = carried + (moved[:, :128] + moved[:, 128:])
        if last:
            mixed = jnp.where(iota((rows, 128), 1) >= across, here, carried)
            mixed = pltpu.roll(mixed, (128 - across) % 128, 1)
            count = self.own_grad.shape[0]
            full, rest = count // 128, count % 128
            self.own_grad[pl.ds(0, full * 128)] = mixed[:full, :].reshape(full * 128)
            if rest:
                self.own_grad[pl.ds(full * 128, rest)] = mixed[full, :rest]
        else:
            self.shard_sum[0] = here
            self.shard_sum[1] = carried


def exchange_refs(count):
    vmem, dma = pltpu.VMEM, pltpu.SemaphoreType.DMA
    return {
        "grads": vmem((PAIRS, ALL_ROWS, 128), BF),
        "grad_vecs": vmem((16, D), F32),
        "land": vmem((PLANES, PAIRS, 2, 4, FRAME, 128), BF),
        "core_land": vmem((3, 2, PAIRS, TWO, 128), BF),
        "all_land": vmem((3, PAIRS, FRAME, 128), BF),
        "half_land": vmem((PLANES - 1, 2, PAIRS, HALF, 128), BF),
        "next_land": vmem((PLANES - 1, 2, PAIRS, FRAME, 128), BF),
        "plane_sum": vmem((PLANES, PAIRS, FRAME, 128), BF),
        "line_land": vmem((3, PAIRS, FRAME, 128), BF),
        "total": vmem((PAIRS, FRAME, 128), F32),
        "shard_flat": vmem((count,), BF),
        "shard_sum": vmem((2, -(-count // 1024) * 8, 128), F32),
        "vec_par": vmem((PAIRS, 16, 128), BF),
        "vec_core": vmem((16, D), F32),
        "vec_sum": vmem((16, D), F32),
        "vec_flat": vmem((3, 16, D), F32),
        "vec_line": vmem((3, 16, D), F32),
        "line_send": dma((PAIRS, 3)),
        "line_recv": dma((6,)),
        "flat_send": dma((21,)),
        "flat_recv": dma((21,)),
        "core_send": dma((6,)),
        "core_recv": dma((6,)),
        "sum_core_send": dma((12,)),
        "sum_core_recv": dma((12,)),
        "sum_flat_send": dma((21,)),
        "sum_flat_recv": dma((21,)),
        "sum_line_send": dma((6,)),
        "sum_line_recv": dma((9,)),
        "par_send": dma((10,)),
        "par_recv": dma((2,)),
        "vec_send": dma((3,)),
        "vec_recv": dma((7,)),
    }


def whole_kernel(names, *refs):
    refs = dict(zip(names, refs))
    refs["flat"] = refs["grads"]
    layer, swap = Layer(refs), Exchange(refs)
    swap.params_copy().start()
    layer.load()
    swap.greet()
    swap.frame_own()
    layer.start()
    swap.greeted()
    swap.send_vectors_line()
    for part in range(PAIRS):
        swap.send_line(0, part, (3, 2, 1))
    swap.send_line(3, 0, (1, 2, 3))
    swap.send_line(2, 0, (3, 2, 1))
    swap.send_line(1, 0, (3,))
    own, second, third = swap.plane_order()
    swap.own_first(lambda: swap.send_next(own))
    swap.send_all(0)
    swap.send_line(1, 0, (2, 1))
    swap.send_vectors_plane()
    swap.send_all(1)
    swap.send_core(0, 0)
    swap.own_first(lambda: swap.send_halves(own))
    swap.send_all(2)
    swap.others_first(lambda: swap.receive_line(own), lambda: swap.send_next(own))
    swap.finish_vectors_plane()
    layer.load_vectors()
    swap.finish_gather(0, 0)
    layer.query_key_value(0)
    layer.attend_first(0)
    swap.receive_line(second)
    swap.send_next(second)
    swap.send_core(0, 1)


    @pl.loop(0, PAIRS)
    def _(pair):
        layer.attend_step(2 * pair, 2 * pair + 1)

        @pl.when(pair == 0)
        def _():
            swap.others_first(lambda: swap.send_halves(own))
            swap.receive_line(third)
            swap.send_next(third)

        @pl.when(pair == 1)
        def _():
            swap.send_halves(second)

        @pl.when(pair == 2)
        def _():
            swap.send_halves(third)

        @pl.when(pair < PAIRS - 1)
        def _():
            swap.finish_gather(0, pair + 1)
            layer.query_key_value(pair + 1)

        layer.attend_step(2 * pair + 1, jnp.minimum(2 * pair + 2, HEADS - 1))

        @pl.when(pair == 0)
        def _():
            swap.send_core(0, 2)

        @pl.when(pair == 1)
        def _():
            swap.send_core(own)

    swap.send_core(second)
    swap.send_core(third)
    swap.finish_gather(1)
    layer.after_attention()
    layer.up_weights(0)
    swap.finish_gather(2)
    layer.up_weights(D // 2)

    def before_down():
        swap.finish_gather(3)
        layer.down_weights()

    layer.feed_forward(before_down)
    for block in range(PAIRS):
        layer.grads[block, ROW_VEC:, :] = jnp.zeros((ALL_ROWS - ROW_VEC, 128), BF)
    layer.down_grad(D, FF)
    swap.reduce_core(3)
    layer.down_grad(0, D)
    swap.drain_gather()
    layer.hidden_grad()
    swap.reduce_halves(3)
    layer.up_grad(D // 2)
    swap.reduce_core(2)
    layer.first_norm_grad((0,))
    layer.up_grad(0)
    swap.reduce_next(3)
    swap.reduce_halves(2)
    layer.first_norm_grad((1, 2))
    layer.out_grad()
    swap.reduce_core(1)


    @pl.loop(0, PAIRS)
    def _(pair):
        def early():
            @pl.when(pair == 0)
            def _():
                swap.reduce_halves(1)

        def late():
            @pl.when(pair == 0)
            def _():
                swap.reduce_next(2)

            @pl.when(pair == PAIRS - 1)
            def _():
                swap.reduce_line(0, 0)

            @pl.when(pair > 0)
            def _():
                swap.reduce_all(pair - 1)

        layer.pair_backward(pair, {3: early, 7: late})
        swap.reduce_core(0, pair)

        @pl.when(pair == 0)
        def _():
            swap.reduce_next(1)
            swap.reduce_line(3)

        @pl.when(pair == 1)
        def _():
            swap.reduce_line(2)
            swap.reduce_line(1)

    layer.vector_grads()
    swap.reduce_vectors_core()

    def last_flat():
        swap.reduce_all(2)
        swap.reduce_vectors_flat()
        swap.reduce_line(0, 1)

    layer.input_grad_step({1: last_flat})
    swap.reduce_line(0, 2)
    swap.reduce_vectors_line()
    for plane in (1, 2, 3):
        swap.drain_sum(plane)
        swap.finish_line(plane)
    for part in (0, 1):
        swap.drain_sum(0, part)
        swap.finish_line(0, part)
    swap.finish_vectors()
    swap.unframe((0, 1), False)
    swap.drain_sum(0, 2)
    swap.finish_line(0, 2)
    swap.unframe((2,), True)


def whole_layer(tokens, cotangent, own_params, subnets, lengths):
    rows = tokens.shape[0]
    scratch = scratch_refs() | exchange_refs(own_params.shape[0])
    inputs = ["tokens", "cotangent", "own_params", "subnets", "lengths"]
    outputs = ["layer_out", "input_grad", "own_grad"]
    spaces = [pl.ANY] * 3 + [pltpu.SMEM] * 2
    return pl.pallas_call(
        functools.partial(whole_kernel, inputs + outputs + list(scratch)),
        out_shape=(
            pltpu.VMEM((rows, D), BF),
            pltpu.VMEM((rows, D), F32),
            pltpu.VMEM(own_params.shape, F32),
        ),
        in_specs=[pl.BlockSpec(memory_space=space) for space in spaces],
        out_specs=[pl.BlockSpec(memory_space=pltpu.VMEM)] * 3,
        scratch_shapes=list(scratch.values()),
        compiler_params=pltpu.CompilerParams(
            vmem_limit_bytes=VMEM_LIMIT, collective_id=0, has_side_effects=True
        ),
    )(tokens, cotangent, own_params, subnets, lengths)


def emit_kernel(*refs):
    sems, half = refs[-1], len(refs) // 2
    copies = [pltpu.make_async_copy(refs[i], refs[half + i], sems.at[i]) for i in range(half)]
    for copy in copies:
        copy.start()
    for copy in copies:
        copy.wait()


def emit(*arrays):
    return pl.pallas_call(
        emit_kernel,
        out_shape=[jax.ShapeDtypeStruct(array.shape, array.dtype) for array in arrays],
        in_specs=[pl.BlockSpec(memory_space=pltpu.VMEM)] * len(arrays),
        out_specs=[pl.BlockSpec(memory_space=pl.ANY)] * len(arrays),
        scratch_shapes=[pltpu.SemaphoreType.DMA((len(arrays),))],
        compiler_params=pltpu.CompilerParams(vmem_limit_bytes=8 * 2**20),
    )(*arrays)


def local_kernel(names, *refs):
    refs = dict(zip(names, refs))
    refs["vec_par"] = refs["flat"].at[:, ROW_VEC:, :]
    layer = Layer(refs)
    layer.load()
    layer.start()
    layer.load_vectors()
    for pair in range(PAIRS):
        layer.query_key_value(pair)
    layer.attend_first(0)

    @pl.loop(0, HEADS)
    def _(head):
        layer.attend_step(head, jnp.minimum(head + 1, HEADS - 1))

    layer.after_attention()
    layer.up_weights(0)
    layer.up_weights(D // 2)
    layer.feed_forward(layer.down_weights)
    layer.down_grad(0, FF)
    layer.hidden_grad()
    layer.up_grad(0)
    layer.up_grad(D // 2)
    layer.first_norm_grad(range(LIVE // TILE))
    layer.out_grad()
    @pl.loop(0, PAIRS)
    def _(pair):
        layer.pair_backward(pair, {})

    layer.input_grad_step({})
    layer.vector_grads()
    for block in range(PAIRS):
        layer.grads[block, ROW_VEC:, :] = layer.grad_vecs[:, block * 128 : block * 128 + 128].astype(BF)


def local_layer(tokens, cotangent, flat, subnets, lengths):
    rows = tokens.shape[0]
    scratch = scratch_refs() | {"grad_vecs": pltpu.VMEM((16, D), F32)}
    inputs = ["tokens", "cotangent", "flat", "subnets", "lengths"]
    outputs = ["layer_out", "input_grad", "grads"]
    spaces = [pl.ANY] * 2 + [pltpu.VMEM] + [pltpu.SMEM] * 2
    return pl.pallas_call(
        functools.partial(local_kernel, inputs + outputs + list(scratch)),
        out_shape=(
            jax.ShapeDtypeStruct((rows, D), BF),
            jax.ShapeDtypeStruct((rows, D), F32),
            jax.ShapeDtypeStruct((PAIRS, ALL_ROWS, 128), BF),
        ),
        in_specs=[pl.BlockSpec(memory_space=space) for space in spaces],
        out_specs=[pl.BlockSpec(memory_space=pltpu.VMEM)] * 3,
        scratch_shapes=list(scratch.values()),
        compiler_params=pltpu.CompilerParams(vmem_limit_bytes=VMEM_LIMIT),
    )(tokens, cotangent, flat, subnets, lengths)


def on_device(tokens, cotangent, params, subnets, lengths):
    flat = lax.all_gather(params, ("group", "item"), axis=0, tiled=True)
    flat = flat.reshape(-1, D)
    whole = flat.shape[0]
    flat = jnp.pad(flat, ((0, ALL_ROWS - whole), (0, 0)))
    flat = jnp.swapaxes(flat.reshape(ALL_ROWS, PAIRS, 128), 0, 1)
    layer_out, input_grad, grads = local_layer(tokens[0], cotangent[0], flat, subnets, lengths[0])
    grad = jnp.swapaxes(grads[:, :whole], 0, 1).astype(F32).reshape(-1)
    param_grad = lax.psum_scatter(grad, ("group", "item"), scatter_dimension=0, tiled=True)
    return layer_out[None], input_grad[None], param_grad


def on_known_device(tokens, cotangent, params, subnets, lengths):
    results = whole_layer(tokens[0], cotangent[0], params, subnets, lengths[0])
    layer_out, input_grad, own_grad = emit(*results)
    return layer_out[None], input_grad[None], own_grad


def solution(mesh):
    in_specs = (
        P("group", "item", None),
        P("group", "item", None),
        P(("group", "item")),
        P("group", None),
        P("group", "item", None),
    )
    out_specs = (P("group", "item", None), P("group", "item", None), P(("group", "item")))
    known = mesh.shape["group"] == 16 and mesh.shape["item"] == 2
    return jax.shard_map(
        on_known_device if known else on_device, mesh=mesh, in_specs=in_specs, out_specs=out_specs, check_vma=False
    )
```

```python
import functools

import jax
import jax.numpy as jnp
from jax import lax
from jax.experimental import pallas as pl
from jax.experimental.pallas import tpu as pltpu
from jax.sharding import PartitionSpec as P

HD = 64
HEADS = 6
D = 384
FF = 1536
LIVE = 960
PAIRS = HEADS // 2
CHUNKS = FF // D
BLOCK = 256
TILE = 320
WIDE = 512
BIG = 1e30
BF = jnp.bfloat16
F32 = jnp.float32
ROW_Q, ROW_K, ROW_V, ROW_O, ROW_UP, ROW_DOWN, ROW_VEC = 0, 384, 768, 1152, 1536, 3072, 4608
ALL_ROWS = 4624
STEP, FRAME, TWO, HALF = 144, 160, 304, 80
PLANES = 4
MESH = pl.DeviceIdType.MESH
VMEM_LIMIT = 61 * 2**20
PIECES = ((0, 64), (64, 96))


def dot(left, right):
    return jnp.dot(left, right, preferred_element_type=F32)


def dot_nt(left, right):
    return lax.dot_general(left, right, (((1,), (1,)), ((), ())), preferred_element_type=F32)


def dot_tn(left, right):
    return lax.dot_general(left, right, (((0,), (0,)), ((), ())), preferred_element_type=F32)


def iota(shape, axis):
    return lax.broadcasted_iota(jnp.int32, shape, axis)


def lanes_at(start, size=128):
    return pl.ds(pl.multiple_of(start, 128), size)


def below(shape, axis, bound):
    return jnp.where(iota(shape, axis) < bound, 1.0, 0.0).astype(F32)


def key_range(block):
    first = max(0, block * BLOCK - 479) // 96 * 96
    last = min(LIVE, -(-(block * BLOCK + BLOCK + 479) // 32) * 32)
    return first, last


def gelu_parts(z):
    cdf = 0.5 + 0.5 * lax.erf(z * 0.7071067811865476)
    bell = jnp.exp2((z * z) * -0.7213475204444817 - 1.3257480647361593)
    return z * cdf, cdf + z * bell


def norm_forward(hidden, gain, shift, feature, inv_count):
    center = (hidden - jnp.sum(hidden * feature, axis=-1, keepdims=True) * inv_count) * feature
    inverse = lax.rsqrt(jnp.sum(center * center, axis=-1, keepdims=True) * inv_count + 1e-05)
    normed = center * inverse
    return normed * gain + shift, normed, inverse


def norm_backward(grad, normed, inverse, gain, feature, inv_count):
    scaled = grad * gain
    first = jnp.sum(scaled, axis=-1, keepdims=True) * inv_count
    second = jnp.sum(scaled * normed, axis=-1, keepdims=True) * inv_count
    return inverse * (scaled - first - normed * second) * feature


def col_sum(value):
    return jnp.sum(value, axis=0, keepdims=True)


class Layer:
    def __init__(self, refs):
        self.__dict__.update(refs)
        self.d_f, self.norm_low = self.low.at[0], self.low.at[1]
        self.cot = self.layer_out
        self.d_a, self.dot_t = self.xm, self.v_t
        for index, name in enumerate(("norm_one", "normed_one", "grad_second")):
            setattr(self, name, self.hold.at[:, index * D : index * D + D])
        self.lanes = self.expo.shape[2]
        width, heads, hidden = self.subnets[0, 0], self.subnets[0, 1], self.subnets[0, 2]
        self.width, self.attend, self.hidden = width, heads * HD, hidden
        self.inv_count = 1.0 / jnp.full((1, 1), width, jnp.int32).astype(F32)

    def row_mask(self, cols, bound, offset=0):
        return jnp.where(iota((1, cols), 1) + offset < bound, 1.0, 0.0).astype(F32)

    def col_mask(self, rows, bound, offset=0):
        return jnp.where(iota((rows, 1), 0) + offset < bound, 1.0, 0.0).astype(F32)

    def feature(self):
        return self.row_mask(D, self.width)

    def vector(self, index):
        mask = self.attend if index < 2 else self.width
        return self.vecs[4 + index : 5 + index, :] * self.row_mask(D, mask)

    def add_sum(self, index, value, first):
        part = value[:8, :]
        for start in range(8, value.shape[0], 8):
            part = part + value[start : start + 8, :]
        if first:
            self.sums[index] = part
        else:
            self.sums[index] += part


    def tokens_copy(self):
        return pltpu.make_async_copy(self.tokens.at[pl.ds(0, LIVE)], self.xm, self.io_sem.at[0])

    def cotangent_copy(self):
        return pltpu.make_async_copy(self.cotangent.at[pl.ds(0, LIVE)], self.cot.at[pl.ds(0, LIVE)], self.io_sem.at[1])

    def load(self):
        self.tokens_copy().start()
        self.cotangent_copy().start()

    def start(self):
        pad = self.lanes - LIVE
        self.input_grad[LIVE:, :] = jnp.zeros((self.input_grad.shape[0] - LIVE, D), F32)
        self.cot[LIVE:, :] = jnp.zeros((self.cot.shape[0] - LIVE, D), BF)
        self.dot_t[:, :, LIVE:] = jnp.zeros((HEADS, HD, pad), BF)
        self.q_t[:, :, LIVE:] = jnp.zeros((HEADS, HD, pad), BF)
        self.delta[:, :, LIVE:] = jnp.zeros((HEADS, 1, pad), F32)
        self.do_s[LIVE:, :] = jnp.zeros((pad, D), BF)
        self.q_rows[LIVE:, :] = jnp.zeros((pad, D), BF)
        ends = []
        total = 0
        for index in range(4):
            total = total + self.lengths[0, index]
            ends.append(total)
        lane = iota((HD, self.lanes), 1)
        seg = sum((lane >= end).astype(jnp.int32) for end in ends)
        part = iota((HD, self.lanes), 0)
        self.far[...] = jnp.where((part < 4) & (part != seg), -BIG, 0.0).astype(BF)
        row = iota((LIVE, 128), 0)
        seg = sum((row >= end).astype(jnp.int32) for end in ends[:3])
        self.hot[...] = jnp.where(iota((LIVE, 128), 1) - HD == seg, 1.0, 0.0).astype(BF)
        fe = self.feature().astype(BF)
        self.tokens_copy().wait()
        for rows in row_tiles():
            self.xm[rows, :] = self.xm[rows, :] * fe
        for part in range(PAIRS):
            lanes = slice(part * 128, part * 128 + 128)
            self.xt[lanes, :] = self.xm[:, lanes].T
        self.xt[D:, :] = jnp.ones((self.xt.shape[0] - D, LIVE), BF)

    def load_vectors(self):
        for part in range(PAIRS):
            lanes = slice(part * 128, part * 128 + 128)
            self.vecs[:, lanes] = self.vec_par[part].astype(F32)
        for chunk in range(CHUNKS):
            cols = slice(chunk * D, chunk * D + D)
            self.bias[:, cols] = self.vecs[chunk : chunk + 1, :] * self.row_mask(D, self.hidden, chunk * D)


    def query_key_value(self, pair):
        lanes = lanes_at(pair * 128)
        seen = self.row_mask(128, self.attend, pair * 128)
        mask = self.col_mask(D, self.width) * seen
        for index, row in enumerate((ROW_Q, ROW_K, ROW_V)):
            weight = (self.flat[pair, row : row + D, :].astype(F32) * mask).astype(BF)
            self.w_qkv[:, lanes_at(pair * D + index * 128)] = weight
        bias_q, bias_v = self.vecs[4:5, lanes] * seen, self.vecs[5:6, lanes] * seen
        weight = self.w_qkv[:, lanes_at(pair * D, D)]
        for start in range(0, LIVE, BLOCK):
            rows = slice(start, min(start + BLOCK, LIVE))
            size = rows.stop - rows.start
            even = iota((size, 128), 1) < HD
            out = dot(self.xm[rows, :], weight)
            q = (out[:, :128] + bias_q).astype(BF)
            self.q_rows[rows, lanes] = q
            k32 = out[:, 128:256]
            k = k32.astype(BF)
            hot = self.hot[rows, :]
            for head, moved in ((2 * pair, k32), (2 * pair + 1, pltpu.roll(k32, HD, 1))):
                place, cols = self.keys_place(head)
                self.low[place, rows, cols] = jnp.where(even, moved, hot.astype(F32)).astype(BF)
            v = (out[:, 256:] + bias_v).astype(BF)
            self.v_rows[rows, lanes] = v
            turned = (q * jnp.asarray(0.125, BF)).T
            self.q_t[2 * pair, :, rows] = turned[:HD, :]
            self.q_t[2 * pair + 1, :, rows] = turned[HD:, :]
            turned = k.T
            self.k_t[2 * pair, :, rows] = turned[:HD, :]
            self.k_t[2 * pair + 1, :, rows] = turned[HD:, :]
            turned = v.T
            self.v_t[2 * pair, :, rows] = turned[:HD, :]
            self.v_t[2 * pair + 1, :, rows] = turned[HD:, :]

    def keys_place(self, head):
        return head // PAIRS, lanes_at(head % PAIRS * 128)

    def score(self, head, block):
        cols = slice(block * BLOCK, block * BLOCK + BLOCK)
        first, last = key_range(block)
        right = jnp.concatenate([self.q_t[head, :, cols], self.far[:, cols]], axis=0)
        place, lanes = self.keys_place(head)
        self.hold[first:last, cols] = dot(self.low[place, first:last, lanes], right)

    def soft(self, head, block):
        cols = slice(block * BLOCK, block * BLOCK + BLOCK)
        first, last = key_range(block)
        scores = self.hold[first:last, cols]
        expo = jnp.exp(scores - jnp.max(scores, axis=0, keepdims=True))
        inv = 1.0 / jnp.sum(expo, axis=0, keepdims=True)
        expo = expo.astype(BF)
        self.expo[head, first:last, cols] = expo
        self.inv[head, :, cols] = inv
        return expo, inv

    def attend_first(self, head):
        for block in range(self.lanes // BLOCK):
            self.score(head, block)

    def attend_step(self, head, after):
        for block in range(self.lanes // BLOCK):
            cols = slice(block * BLOCK, block * BLOCK + BLOCK)
            first, last = key_range(block)
            expo, inv = self.soft(head, block)
            self.score(after, block)
            mixed = dot(self.v_t[head, :, first:last], expo) * inv
            self.o_t[head, :, cols] = mixed.astype(BF)

    def after_attention(self):
        fe, bias, gain, shift = self.feature(), self.vector(2), self.vector(3), self.vector(4)
        for start in range(0, LIVE, BLOCK):
            size = min(BLOCK, LIVE - start)
            rows = slice(start, start + size)
            mixed = self.o_t[:, :, start : start + BLOCK].reshape(D, BLOCK)
            attended = dot_tn(mixed, self.w_out[...])[:size, :]
            hidden = self.xm[rows, :].astype(F32) + attended + bias
            norm, normed, inverse = norm_forward(hidden, gain, shift, fe, self.inv_count)
            self.norm_one[rows, :] = norm
            self.normed_one[rows, :] = normed
            self.inverse_one[rows, :] = jnp.broadcast_to(inverse, (size, 128))
            self.norm_low[rows, :] = norm.astype(BF)

    def up_weights(self, start):
        half = D // 2
        rows = slice(start * CHUNKS, (start + half) * CHUNKS)
        for part in range(PAIRS):
            self.wide[part, rows, :] = self.flat[part, ROW_UP + rows.start : ROW_UP + rows.stop, :].astype(F32)
        inside = self.col_mask(half, self.width, start)
        for chunk in range(CHUNKS):
            mask = inside * self.row_mask(D, self.hidden, chunk * D)
            for part in range(PAIRS):
                lanes = slice(part * 128, part * 128 + 128)
                piece = self.wide[part, pl.ds(rows.start + chunk, half, stride=CHUNKS), :]
                self.w_up[start : start + half, chunk * D + part * 128 : chunk * D + part * 128 + 128] = (
                    piece * mask[:, lanes]
                ).astype(BF)

    def up_tile(self, rows):
        low = self.norm_low[rows, :]
        for start in range(0, FF, BLOCK):
            cols = slice(start, start + BLOCK)
            act, slope = gelu_parts(dot(low, self.w_up[:, cols]) + self.bias[:, cols])
            self.act[rows, cols] = act.astype(BF)
            self.slope[rows, cols] = (slope * self.row_mask(BLOCK, self.hidden, start)).astype(BF)

    def down_tile(self, rows):
        fe = self.feature()
        bias, gain, shift = self.vector(5), self.vector(6), self.vector(7)
        second = self.norm_one[rows, :] + dot(self.act[rows, :FF], self.w_down[...]) + bias
        result, normed, inverse = norm_forward(second, gain, shift, fe, self.inv_count)
        grad = self.cot[rows, :].astype(F32)
        self.cot[rows, :] = result.astype(BF)
        grad_second = norm_backward(grad, normed, inverse, gain, fe, self.inv_count)
        self.grad_second[rows, :] = grad_second
        low = grad_second.astype(BF)
        self.d_f[rows, :] = low
        first = rows.start == 0
        self.add_sum(10, grad * normed, first)
        self.add_sum(11, grad, first)
        self.add_sum(9, low.astype(F32), first)


    def feed_forward(self, before_down):
        for rows in row_tiles():
            self.up_tile(rows)
        before_down()
        self.cotangent_copy().wait()
        for rows in row_tiles():
            self.down_tile(rows)


    def down_grad(self, start, stop):
        fe = self.feature()
        for first in range(start, stop, WIDE):
            size = min(WIDE, stop - first)
            grad = dot_tn(self.d_f[...], self.act[:, first : first + size]).astype(BF).T
            grad = grad * (self.col_mask(size, self.hidden, first) * fe).astype(BF)
            for part in range(PAIRS):
                lanes = slice(part * 128, part * 128 + 128)
                self.grads[part, ROW_DOWN + first : ROW_DOWN + first + size, :] = grad[:, lanes]

    def hidden_tile(self, rows):
        d_f = self.d_f[rows, :]
        for start in range(0, FF, BLOCK):
            cols = slice(start, start + BLOCK)
            grad = dot_nt(d_f, self.w_down[cols, :])
            dz = (grad * self.slope[rows, cols].astype(F32)).astype(BF)
            self.slope[rows, cols] = dz
            part = dz[:8, :].astype(F32)
            for row in range(8, rows.stop - rows.start, 8):
                part = part + dz[row : row + 8, :].astype(F32)
            if rows.start == 0:
                self.hidden_sums[:, cols] = part
            else:
                self.hidden_sums[:, cols] += part

    def first_norm_tile(self, rows):
        gain, fe = self.vector(3), self.feature()
        normed = self.normed_one[rows, :]
        grad = self.grad_second[rows, :] + dot_nt(self.slope[rows, :], self.w_up[...])
        grad_first = norm_backward(grad, normed, self.inverse_one[rows, :1], gain, fe, self.inv_count)
        self.norm_one[rows, :] = grad_first
        low = grad_first.astype(BF)
        self.d_a[rows, :] = low
        first = rows.start == 0
        self.add_sum(7, grad * normed, first)
        self.add_sum(8, grad, first)
        self.add_sum(6, low.astype(F32), first)

    def hidden_grad(self):
        for rows in row_tiles():
            self.hidden_tile(rows)

    def first_norm_grad(self, tiles):
        for index in tiles:
            self.first_norm_tile(row_tiles()[index])

    def up_grad(self, start):
        half = D // 2
        low = self.norm_low[:, start : start + half]
        for first in range(0, FF, WIDE):
            mask = self.col_mask(half, self.width, start) * self.row_mask(WIDE, self.hidden, first)
            grad = dot_tn(low, self.slope[:, first : first + WIDE]) * mask
            for lane in range(0, WIDE, 128):
                chunk, part = (first + lane) // D, (first + lane) % D // 128
                rows = pl.ds(start * CHUNKS + chunk, half, stride=CHUNKS)
                self.wide[part, rows, :] = grad[:, lane : lane + 128]
        rows = slice(start * CHUNKS, (start + half) * CHUNKS)
        for part in range(PAIRS):
            self.grads[part, ROW_UP + rows.start : ROW_UP + rows.stop, :] = self.wide[part, rows, :].astype(BF)

    def out_grad(self):
        fe = self.feature()
        d_a = self.d_a[...]
        half = D // 2
        for start in (0, half):
            rows = slice(start, start + half)
            heads = range(start // HD, (start + half) // HD)
            mask = self.col_mask(half, self.attend, start) * fe
            o_t = self.o_t[heads.start : heads.stop, :, :LIVE].reshape(half, LIVE)
            grad = (dot(o_t, d_a) * mask).astype(BF)
            for part in range(PAIRS):
                lanes = slice(part * 128, part * 128 + 128)
                self.grads[part, ROW_O + start : ROW_O + start + half, :] = grad[:, lanes]
            mixed = dot_nt(self.w_out[rows, :], d_a)
            for head in heads:
                own = mixed[head * HD - start : head * HD - start + HD, :] * self.inv[head, :, :LIVE]
                self.delta[head, :, :LIVE] = col_sum(own * self.o_t[head, :, :LIVE].astype(F32))
                self.dot_t[head, :, :LIVE] = own.astype(BF)
        for pair in range(PAIRS):
            both = self.dot_t[2 * pair : 2 * pair + 2, :, :LIVE].reshape(128, LIVE)
            self.do_s[:LIVE, pair * 128 : pair * 128 + 128] = both.T

    def score_place(self, odd, block):
        if not odd:
            return self.act, block * BLOCK
        return ((self.act, 4 * BLOCK), (self.act, 5 * BLOCK), (self.slope, PAIRS * D), (self.d_f, 0))[block]

    def first_lane(self, pair, index):
        return lanes_at(pair * D + index * 128)

    def prob_grad(self, pair, odd, block):
        cols = slice(block * BLOCK, block * BLOCK + BLOCK)
        first, last = key_range(block)
        right = self.dot_t[2 * pair + odd, :, cols]
        none = jnp.zeros_like(right)
        right = jnp.concatenate([none, right] if odd else [right, none], axis=0)
        return dot(self.v_rows[first:last, lanes_at(pair * 128)], right)

    def score_grad(self, pair, odd, block, grad):
        head = 2 * pair + odd
        cols = slice(block * BLOCK, block * BLOCK + BLOCK)
        first, last = key_range(block)
        grad = self.expo[head, first:last, cols].astype(F32) * (grad - self.delta[head, :, cols])
        grad = grad.astype(BF)
        place, start = self.score_place(odd, block)
        place[first:last, start : start + BLOCK] = grad
        return grad

    def query_grad(self, pair, odd, block, grad):
        head = 2 * pair + odd
        cols = slice(block * BLOCK, block * BLOCK + BLOCK)
        first, last = key_range(block)
        dq = dot(self.k_t[head, :, first:last], grad) * 0.125
        self.dq_t[odd * HD : odd * HD + HD, cols] = dq.astype(BF)

    def pair_backward(self, pair, hooks):
        lanes = lanes_at(pair * 128)
        blocks = self.lanes // BLOCK
        ranges = [key_range(block) for block in range(blocks)]
        edges = sorted({edge for both in ranges for edge in both})
        cuts = []
        for low, high in zip(edges[:-1], edges[1:]):
            used = [b for b in range(blocks) if ranges[b][0] <= low and high <= ranges[b][1]]
            cuts.append((slice(low, high), slice(used[0] * BLOCK, used[-1] * BLOCK + BLOCK)))
        own = [jnp.where((iota((1, 128), 1) >= HD) == bool(odd), 1.0, 0.0).astype(BF) for odd in (0, 1)]
        d_out = [self.do_s[:, lanes] * own[odd] for odd in (0, 1)]
        items = [(odd, block) for odd in (0, 1) for block in range(blocks)]
        grad = self.prob_grad(pair, *items[0])
        for index, (odd, block) in enumerate(items):
            if index % 2 == 0 and index // 2 < len(cuts):
                rows, span = cuts[index // 2]
                dv = sum(dot(self.expo[2 * pair + odd_, rows, span], d_out[odd_][span]) for odd_ in (0, 1))
                self.slope[rows, self.first_lane(pair, 2)] = dv.astype(BF)
            after = self.prob_grad(pair, *items[index + 1]) if index + 1 < len(items) else None
            low = self.score_grad(pair, odd, block, grad)
            grad = after
            self.query_grad(pair, odd, block, low)
            if index in hooks:
                hooks[index]()
        queries = [self.q_rows[:, lanes] * own[odd] for odd in (0, 1)]
        for rows, span in cuts:
            dk = 0.0
            for odd in (0, 1):
                places = [self.score_place(odd, block) for block in range(span.start // BLOCK, span.stop // BLOCK)]
                first = 0
                for last in range(1, len(places) + 1):
                    if last == len(places) or places[last][0] is not places[first][0]:
                        place, start = places[first]
                        begin, size = span.start + first * BLOCK, (last - first) * BLOCK
                        dk = dk + dot(place[rows, start : start + size], queries[odd][begin : begin + size])
                        first = last
            self.slope[rows, self.first_lane(pair, 1)] = (dk * 0.125).astype(BF)
        self.slope[:, self.first_lane(pair, 0)] = self.dq_t[:, :LIVE].T
        mask = self.col_mask(D, self.width) * self.row_mask(128, self.attend, pair * 128)
        all_three = self.slope[:, lanes_at(pair * D, D)]
        grad = dot(self.xt[...], all_three)
        for index, row in enumerate((ROW_Q, ROW_K, ROW_V)):
            self.grads[pair, row : row + D, :] = (grad[:D, index * 128 : index * 128 + 128] * mask).astype(BF)
        self.sums[4, :, lanes] = grad[D : D + 8, :128] * 0.125
        self.sums[5, :, lanes] = grad[D : D + 8, 256:] * 0.125

    def input_grad_step(self, hooks):
        fe = self.feature()
        for index, rows in enumerate(row_tiles()):
            total = self.norm_one[rows, :] + dot_nt(self.slope[rows, : PAIRS * D], self.w_qkv[...])
            self.input_grad[rows, :] = total * fe
            if index in hooks:
                hooks[index]()

    def vector_grads(self):
        for index in range(12):
            if index < CHUNKS:
                total = jnp.sum(self.hidden_sums[:, index * D : index * D + D], axis=0, keepdims=True)
                mask = self.row_mask(D, self.hidden, index * D)
            else:
                total = jnp.sum(self.sums[index], axis=0, keepdims=True)
                mask = self.row_mask(D, self.attend if index < 6 else self.width)
            self.grad_vecs[index : index + 1, :] = total * mask
        self.grad_vecs[12:, :] = jnp.zeros((4, D), F32)


def row_tiles():
    return [slice(start, min(start + TILE, LIVE)) for start in range(0, LIVE, TILE)]


def scratch_refs():
    vmem = pltpu.VMEM
    lanes = -(-LIVE // BLOCK) * BLOCK
    return {
        "xm": vmem((LIVE, D), BF),
        "hold": vmem((LIVE, 3 * D), F32),
        "xt": vmem((D + 16, LIVE), BF),
        "hot": vmem((LIVE, 128), BF),
        "far": vmem((HD, lanes), BF),
        "vecs": vmem((16, D), F32),
        "bias": vmem((1, FF), F32),
        "sums": vmem((12, 8, D), F32),
        "hidden_sums": vmem((8, FF), F32),
        "w_qkv": vmem((D, PAIRS * D), BF),
        "w_out": vmem((D, D), BF),
        "w_up": vmem((D, FF), BF),
        "w_down": vmem((FF, D), BF),
        "wide": vmem((PAIRS, FF, 128), F32),
        "q_rows": vmem((lanes, D), BF),
        "q_t": vmem((HEADS, HD, lanes), BF),
        "k_t": vmem((HEADS, HD, LIVE), BF),
        "v_rows": vmem((LIVE, D), BF),
        "v_t": vmem((HEADS, HD, lanes), BF),
        "expo": vmem((HEADS, LIVE, lanes), BF),
        "inv": vmem((HEADS, 1, lanes), F32),
        "o_t": vmem((HEADS, HD, lanes), BF),
        "inverse_one": vmem((LIVE, 128), F32),
        "low": vmem((2, LIVE, D), BF),
        "act": vmem((LIVE, FF), BF),
        "slope": vmem((LIVE, FF), BF),
        "do_s": vmem((lanes, D), BF),
        "delta": vmem((HEADS, 1, lanes), F32),
        "dq_t": vmem((128, lanes), BF),
        "io_sem": pltpu.SemaphoreType.DMA((3,)),
    }


class Exchange:
    def __init__(self, refs):
        self.__dict__.update(refs)
        group, self.x = lax.axis_index("group"), lax.axis_index("item")
        self.z, self.y, self.c = group // 4, (group // 2) % 2, group % 2
        self.spot = 2 * self.y + self.x
        self.shard = 2 * group + self.x
        self.corner = (self.c == 1) & (self.spot == 3)

    def device(self, z, y, c, x):
        return (z * 4 + y * 2 + c, x)

    def line(self, step):
        return self.device((self.z + step) % PLANES, self.y, self.c, self.x)

    def plane_peer(self, step):
        y, x = (self.y + step // 4) % 2, (self.x + step % 2) % 2
        return self.device(self.z, y, (self.c + step // 2 % 2) % 2, x)

    def chip_peer(self, step):
        y, x = (self.y + step // 2) % 2, (self.x + step % 2) % 2
        return self.device(self.z, y, self.c, x)

    def spot_of(self, step):
        return 2 * ((self.y + step // 2) % 2) + (self.x + step % 2) % 2

    def core_peer(self):
        return self.device(self.z, self.y, 1 - self.c, self.x)

    def greet(self):
        barrier = pltpu.get_barrier_semaphore()
        peers = [self.line(step) for step in (1, 2, 3)] + [self.plane_peer(step) for step in range(1, 8)]
        for peer in peers:
            pl.semaphore_signal(barrier, inc=1, device_id=peer, device_id_type=MESH)

    def greeted(self):
        pl.semaphore_wait(pltpu.get_barrier_semaphore(), 10)

    def copy(self, source, target, send, recv, peer):
        return pltpu.make_async_remote_copy(
            src_ref=source, dst_ref=target, send_sem=send, recv_sem=recv, device_id=peer, device_id_type=MESH
        )


    def offsets(self):
        shift = STEP * self.shard
        return shift // 128, shift % 128

    def params_copy(self):
        return pltpu.make_async_copy(self.own_params, self.shard_flat, self.io_sem.at[2])

    def frame_own(self):
        self.params_copy().wait()
        rows, count = self.shard_sum.shape[1], self.shard_flat.shape[0]
        full, rest = count // 128, count % 128
        spread = self.shard_sum.at[0]
        spread[:full, :] = self.shard_flat[pl.ds(0, full * 128)].reshape(full, 128).astype(F32)
        spread[full:, :] = jnp.zeros((rows - full, 128), F32)
        if rest:
            spread[full : full + 1, :rest] = self.shard_flat[pl.ds(full * 128, rest)].reshape(1, rest).astype(F32)
        up, across = self.offsets()
        turned = pltpu.roll(spread[...], across, 1)
        late = iota((rows, 128), 1) >= across
        same = jnp.where(late, turned, 0.0).astype(BF)
        carried = jnp.where(late, 0.0, turned).astype(BF)
        gap = 3 * iota((FRAME, rows), 0) - up - iota((FRAME, rows), 1)
        for part in range(PAIRS):
            here = jnp.where(gap == -part, 1.0, 0.0).astype(BF)
            after = jnp.where(gap == 1 - part, 1.0, 0.0).astype(BF)
            frame = dot(here, same) + dot(after, carried)
            self.land[self.z, part, self.c, self.spot] = frame.astype(BF)

    def vectors_line(self, step):
        sems = self.par_send.at[step - 1], self.par_recv.at[0]
        return self.copy(self.vec_par, self.vec_par, *sems, self.line(step))

    def vectors_plane(self, step):
        sems = self.par_send.at[step + 2], self.par_recv.at[1]
        return self.copy(self.vec_par, self.vec_par, *sems, self.plane_peer(step))

    def send_vectors_line(self):
        @pl.when(self.corner & (self.z == PLANES - 1))
        def _():
            self.vec_par[...] = self.land[PLANES - 1, :, 1, 3, STEP:, :]
            for step in (1, 2, 3):
                self.vectors_line(step).start()

    def send_vectors_plane(self):
        @pl.when(self.corner & (self.z != PLANES - 1))
        def _():
            self.vectors_line(1).wait_recv()

        @pl.when(self.corner)
        def _():
            for step in range(1, 8):
                self.vectors_plane(step).start()

    def finish_vectors_plane(self):
        @pl.when(jnp.logical_not(self.corner))
        def _():
            self.vectors_plane(1).wait_recv()

    def parts(self, plane, part):
        return pl.ds(part, 1) if isinstance(plane, int) and plane == 0 else slice(None)

    def blocks(self, plane, part):
        return [part] if plane == 0 else range(PAIRS)

    def item(self, plane, part):
        return part if isinstance(plane, int) and plane == 0 else 2 + plane

    def gather_line(self, plane, part, step):
        piece = self.land.at[plane, self.parts(plane, part), self.c, self.spot]
        sems = self.line_send.at[part, step - 1], self.line_recv.at[self.item(plane, part)]
        return self.copy(piece, piece, *sems, self.line(step))

    def send_line(self, plane, part, steps):
        @pl.when(self.z == plane)
        def _():
            for step in steps:
                self.gather_line(plane, part, step).start()

    def gather_all(self, part, step, spot):
        piece = self.land.at[0, pl.ds(part, 1), self.c, spot]
        sems = self.flat_send.at[3 * part + step - 1], self.flat_recv.at[3 * part + step - 1]
        return self.copy(piece, piece, *sems, self.chip_peer(step))

    def gather_next(self, plane, step, spot):
        piece = self.land.at[plane, :, self.c, spot]
        index = 5 + 4 * plane + step - 1
        return self.copy(piece, piece, self.flat_send.at[index], self.flat_recv.at[index], self.chip_peer(step))

    def gather_half(self, plane, step, spot):
        rows = pl.ds((2 - step) * HALF, HALF)
        piece = self.land.at[plane, :, self.c, spot, rows]
        index = 5 + 4 * plane + step + 1
        return self.copy(piece, piece, self.flat_send.at[index], self.flat_recv.at[index], self.chip_peer(step))

    def wait_line(self, plane, part):
        @pl.when(self.z != plane)
        def _():
            self.gather_line(plane, part, 1).wait_recv()

    def send_all(self, part):
        self.wait_line(0, part)
        for step in (3, 2, 1):
            self.gather_all(part, step, self.spot).start()

    def plane_order(self):
        second = jnp.where(self.z == 0, 3, jnp.where(self.z == 1, 2, 1))
        third = jnp.where(self.z % 3 == 0, 2, 3)
        return jnp.maximum(self.z, 1), second, third

    def own_first(self, action):
        @pl.when(self.z != 0)
        def _():
            action()

    def others_first(self, *actions):
        @pl.when(self.z == 0)
        def _():
            for action in actions:
                action()

    def receive_line(self, plane):
        self.copy_line(plane).wait_recv()

    def copy_line(self, plane):
        piece = self.land.at[plane, :, self.c, self.spot]
        return self.copy(piece, piece, self.line_send.at[1, 0], self.line_recv.at[2 + plane], self.line(1))

    def send_next(self, plane):
        for step in (2, 1):
            self.gather_next(plane, step, self.spot).start()

    def send_halves(self, plane):
        self.gather_next(plane, 1, self.spot_of(1)).wait_recv()
        self.gather_half(plane, 2, self.spot_of(1)).start()
        self.gather_next(plane, 2, self.spot_of(2)).wait_recv()
        self.gather_half(plane, 1, self.spot_of(2)).start()

    def gather_core(self, plane, part, core):
        piece = self.land.at[plane, self.parts(plane, part), core]
        item = self.item(plane, part)
        return self.copy(piece, piece, self.core_send.at[item], self.core_recv.at[item], self.core_peer())

    def send_core(self, plane, part=0):
        if isinstance(plane, int) and plane == 0:
            for step in (3, 2, 1):
                self.gather_all(part, step, self.spot_of(step)).wait_recv()
        else:
            for step in (2, 1):
                self.gather_half(plane, step, self.spot_of(3)).wait_recv()
        self.gather_core(plane, part, self.c).start()

    def keep(self, block, row, value):
        if not isinstance(block, int) or row >= ROW_VEC:
            self.flat[block, row : row + value.shape[0], :] = value
            return
        lanes = slice(block * 128, block * 128 + 128)
        for first, last, matrix in (
            (0, ROW_O, None),
            (ROW_O, ROW_UP, self.w_out),
            (ROW_UP, ROW_DOWN, None),
            (ROW_DOWN, ROW_VEC, self.w_down),
        ):
            low, high = max(first, row), min(last, row + value.shape[0])
            if low < high:
                piece = value[low - row : high - row, :]
                if matrix is None:
                    self.flat[block, low:high, :] = piece
                else:
                    matrix[low - first : high - first, lanes] = piece

    def finish_gather(self, plane, part=0):
        self.gather_core(plane, part, 1 - self.c).wait_recv()
        for place in range(8):
            y, c, x = place // 4, (place // 2) % 2, place % 2
            chunk = 8 * plane + place
            for block in self.blocks(plane, part):
                frame = self.land[plane, block, c, 2 * y + x]
                begin = chunk * STEP + (FRAME - STEP if chunk else 0)
                self.keep(block, begin, frame[begin - chunk * STEP : STEP, :])
                if chunk:
                    before = (chunk - 1) % 8
                    spot = 2 * (before // 4) + before % 2
                    tail = self.land[(chunk - 1) // 8, block, (before // 2) % 2, spot, STEP:, :]
                    self.keep(block, chunk * STEP, tail + frame[: FRAME - STEP, :])

    def drain_gather(self):
        @pl.when(self.corner & (self.z == PLANES - 1))
        def _():
            for step in (1, 2, 3):
                self.vectors_line(step).wait_send()

        @pl.when(self.corner)
        def _():
            for step in range(1, 8):
                self.vectors_plane(step).wait_send()

        for plane in range(PLANES):
            for part in range(PAIRS if plane == 0 else 1):

                @pl.when(self.z == plane)
                def _():
                    for step in (1, 2, 3):
                        self.gather_line(plane, part, step).wait_send()

                if plane == 0:
                    for step in (1, 2, 3):
                        self.gather_all(part, step, self.spot).wait_send()
                else:
                    for step in (1, 2):
                        self.gather_next(plane, step, self.spot).wait_send()
                        self.gather_half(plane, step, self.spot).wait_send()
                self.gather_core(plane, part, self.c).wait_send()


    def sum_core(self, plane, part, y):
        row = pl.multiple_of(STEP * (8 * plane + 4 * y + 2 * (1 - self.c)), 16)
        parts, item = self.parts(plane, part), 2 * self.item(plane, part) + y
        return self.copy(
            self.grads.at[parts, pl.ds(row, TWO)],
            self.core_land.at[plane % 3, y, parts],
            self.sum_core_send.at[item],
            self.sum_core_recv.at[item],
            self.core_peer(),
        )

    def sum_all(self, part, step):
        index = 3 * part + step - 1
        return self.copy(
            self.land.at[0, pl.ds(part, 1), 0, self.spot_of(step)],
            self.all_land.at[step - 1, pl.ds(part, 1)],
            self.sum_flat_send.at[index],
            self.sum_flat_recv.at[index],
            self.chip_peer(step),
        )

    def sum_half(self, plane, step):
        index = 5 + 4 * plane + step - 1
        return self.copy(
            self.land.at[plane, :, 0, self.spot_of(3), pl.ds((step - 1) * HALF, HALF)],
            self.half_land.at[plane - 1, step - 1],
            self.sum_flat_send.at[index],
            self.sum_flat_recv.at[index],
            self.chip_peer(step),
        )

    def sum_next(self, plane, step):
        index = 5 + 4 * plane + step + 1
        return self.copy(
            self.land.at[plane, :, 0, self.spot_of(step)],
            self.next_land.at[plane - 1, step - 1],
            self.sum_flat_send.at[index],
            self.sum_flat_recv.at[index],
            self.chip_peer(step),
        )

    def sum_line(self, plane, part, slot):
        parts, item = self.parts(plane, part), self.item(plane, part)
        return self.copy(
            self.plane_sum.at[plane, parts],
            self.line_land.at[slot, parts],
            self.sum_line_send.at[item],
            self.sum_line_recv.at[3 * part + slot],
            self.device(plane, self.y, self.c, self.x),
        )

    def reduce_core(self, plane, part=0):
        for y in (0, 1):
            self.sum_core(plane, part, y).start()

    def add_core(self, plane, part):
        for y in (0, 1):
            self.sum_core(plane, part, y).wait_recv()
            for block in self.blocks(plane, part):
                for x in (0, 1):
                    row = pl.multiple_of(STEP * (8 * plane + 4 * y + 2 * self.c + x), 16)
                    own = self.grads[block, pl.ds(row, FRAME), :]
                    other = self.core_land[plane % 3, y, block, x * STEP : x * STEP + FRAME, :]
                    self.land[plane, block, 0, 2 * y + x] = own + other

    def reduce_all(self, part):
        self.add_core(0, part)
        for step in (3, 2, 1):
            self.sum_all(part, step).start()

    def reduce_halves(self, plane):
        self.add_core(plane, 0)
        for step in (1, 2):
            self.sum_half(plane, step).start()

    def reduce_next(self, plane):
        for step in (1, 2):
            self.sum_half(plane, step).wait_recv()
            rows = slice((step - 1) * HALF, step * HALF)
            spot = self.spot_of(3 - step)
            for block in range(PAIRS):
                own = self.land[plane, block, 0, spot, rows, :]
                self.land[plane, block, 0, spot, rows, :] = own + self.half_land[plane - 1, step - 1, block]
            self.sum_next(plane, 3 - step).start()

    def reduce_line(self, plane, part=0):
        if plane == 0:
            for step in (1, 2, 3):
                self.sum_all(part, step).wait_recv()
        else:
            for step in (1, 2):
                self.sum_next(plane, step).wait_recv()
        for block in self.blocks(plane, part):
            total = self.land[plane, block, 0, self.spot]
            if plane == 0:
                total = (total + self.all_land[0, block]) + (self.all_land[1, block] + self.all_land[2, block])
            else:
                total = total + (self.next_land[plane - 1, 0, block] + self.next_land[plane - 1, 1, block])
            self.plane_sum[plane, block] = total

        @pl.when(self.z != plane)
        def _():
            self.sum_line(plane, part, (self.z - plane + 2 * PLANES - 1) % PLANES).start()


    def last_all(self, step, piece):
        index = 3 * piece + step - 1
        return self.copy(
            self.land.at[0, pl.ds(PAIRS - 1, 1), 0, self.spot_of(step), pl.ds(*PIECES[piece])],
            self.all_land.at[step - 1, pl.ds(PAIRS - 1, 1), pl.ds(*PIECES[piece])],
            self.last_flat_send.at[index],
            self.last_flat_recv.at[index],
            self.chip_peer(step),
        )

    def last_line(self, slot, piece):
        return self.copy(
            self.plane_sum.at[0, pl.ds(PAIRS - 1, 1), pl.ds(*PIECES[piece])],
            self.line_land.at[slot, pl.ds(PAIRS - 1, 1), pl.ds(*PIECES[piece])],
            self.last_line_send.at[piece],
            self.last_line_recv.at[3 * piece + slot],
            self.device(0, self.y, self.c, self.x),
        )

    def reduce_last_all(self):
        self.add_core(0, PAIRS - 1)
        for piece in range(len(PIECES)):
            for step in (3, 2, 1):
                self.last_all(step, piece).start()

    def reduce_last_line(self):
        block = PAIRS - 1
        for piece, (first, size) in enumerate(PIECES):
            rows = slice(first, first + size)
            for step in (1, 2, 3):
                self.last_all(step, piece).wait_recv()
            total = self.land[0, block, 0, self.spot, rows, :] + self.all_land[0, block, rows, :]
            total = total + (self.all_land[1, block, rows, :] + self.all_land[2, block, rows, :])
            self.plane_sum[0, block, rows, :] = total

            @pl.when(self.z != 0)
            def _():
                self.last_line((self.z + 2 * PLANES - 1) % PLANES, piece).start()

    def finish_last_line(self):
        block = PAIRS - 1

        @pl.when(self.z == 0)
        def _():
            for piece, (first, size) in enumerate(PIECES):
                rows = slice(first, first + size)
                for slot in range(3):
                    self.last_line(slot, piece).wait_recv()
                total = self.plane_sum[0, block, rows, :].astype(F32)
                for slot in range(3):
                    total = total + self.line_land[slot, block, rows, :].astype(F32)
                self.total[block, rows, :] = total

    def drain_last(self):
        for piece in range(len(PIECES)):

            @pl.when(self.z != 0)
            def _():
                self.last_line(0, piece).wait_send()

            for step in (1, 2, 3):
                self.last_all(step, piece).wait_send()
        for y in (0, 1):
            self.sum_core(0, PAIRS - 1, y).wait_send()

    def vector_core(self):
        peer = self.core_peer()
        return self.copy(self.grad_vecs, self.vec_core, self.vec_send.at[0], self.vec_recv.at[0], peer)

    def vector_flat(self, slot):
        peer = self.device(self.z, 1, 1, 1)
        return self.copy(self.vec_sum, self.vec_flat.at[slot], self.vec_send.at[1], self.vec_recv.at[1 + slot], peer)

    def vector_line(self, slot):
        peer = self.device(PLANES - 1, 1, 1, 1)
        return self.copy(self.vec_sum, self.vec_line.at[slot], self.vec_send.at[2], self.vec_recv.at[4 + slot], peer)

    def reduce_vectors_core(self):
        @pl.when(self.c == 0)
        def _():
            self.vector_core().start()

    def reduce_vectors_flat(self):
        @pl.when(self.c == 1)
        def _():
            self.vector_core().wait_recv()
            self.vec_sum[...] = self.grad_vecs[...] + self.vec_core[...]

            @pl.when(self.spot != 3)
            def _():
                self.vector_flat(2 - self.spot).start()

    def reduce_vectors_line(self):
        @pl.when(self.corner)
        def _():
            for slot in range(3):
                self.vector_flat(slot).wait_recv()
            self.vec_sum[...] = self.vec_sum[...] + self.vec_flat[0] + self.vec_flat[1] + self.vec_flat[2]

            @pl.when(self.z != PLANES - 1)
            def _():
                self.vector_line(self.z).start()

    def finish_vectors(self):
        @pl.when(self.corner & (self.z == PLANES - 1))
        def _():
            total = self.vec_sum[...]
            for slot in range(3):
                self.vector_line(slot).wait_recv()
                total = total + self.vec_line[slot]
            for block in range(PAIRS):
                self.total[block, STEP:, :] = total[:, block * 128 : block * 128 + 128]

        @pl.when(self.c == 0)
        def _():
            self.vector_core().wait_send()

        @pl.when((self.c == 1) & (self.spot != 3))
        def _():
            self.vector_flat(0).wait_send()

        @pl.when(self.corner & (self.z != PLANES - 1))
        def _():
            self.vector_line(0).wait_send()

    def finish_line(self, plane, part=0):
        @pl.when(self.z == plane)
        def _():
            for slot in range(3):
                self.sum_line(plane, part, slot).wait_recv()
            for block in self.blocks(plane, part):
                total = self.plane_sum[plane, block].astype(F32)
                for slot in range(3):
                    total = total + self.line_land[slot, block].astype(F32)
                self.total[block] = total

    def drain_sum(self, plane, part=0):
        @pl.when(self.z != plane)
        def _():
            self.sum_line(plane, part, 0).wait_send()

        if plane == 0:
            for step in (1, 2, 3):
                self.sum_all(part, step).wait_send()
        else:
            for step in (1, 2):
                self.sum_half(plane, step).wait_send()
                self.sum_next(plane, step).wait_send()
        for y in (0, 1):
            self.sum_core(plane, part, y).wait_send()

    def unframe(self, parts, last):
        rows = self.shard_sum.shape[1]
        up, across = self.offsets()
        gap = iota((rows, FRAME), 0) + up - 3 * iota((rows, FRAME), 1)
        here = self.shard_sum[0] if last else jnp.zeros((rows, 128), F32)
        carried = self.shard_sum[1] if last else jnp.zeros((rows, 128), F32)
        for block in parts:
            total = self.total[block]
            high = total.astype(BF)
            both = jnp.concatenate([high, (total - high.astype(F32)).astype(BF)], axis=1)
            moved = dot(jnp.where(gap == block, 1.0, 0.0).astype(BF), both)
            here = here + (moved[:, :128] + moved[:, 128:])
            moved = dot(jnp.where(gap == block - 1, 1.0, 0.0).astype(BF), both)
            carried = carried + (moved[:, :128] + moved[:, 128:])
        if last:
            mixed = jnp.where(iota((rows, 128), 1) >= across, here, carried)
            mixed = pltpu.roll(mixed, (128 - across) % 128, 1)
            count = self.own_grad.shape[0]
            full, rest = count // 128, count % 128
            self.own_grad[pl.ds(0, full * 128)] = mixed[:full, :].reshape(full * 128)
            if rest:
                self.own_grad[pl.ds(full * 128, rest)] = mixed[full, :rest]
        else:
            self.shard_sum[0] = here
            self.shard_sum[1] = carried


def exchange_refs(count):
    vmem, dma = pltpu.VMEM, pltpu.SemaphoreType.DMA
    return {
        "grads": vmem((PAIRS, ALL_ROWS, 128), BF),
        "grad_vecs": vmem((16, D), F32),
        "land": vmem((PLANES, PAIRS, 2, 4, FRAME, 128), BF),
        "core_land": vmem((3, 2, PAIRS, TWO, 128), BF),
        "all_land": vmem((3, PAIRS, FRAME, 128), BF),
        "half_land": vmem((PLANES - 1, 2, PAIRS, HALF, 128), BF),
        "next_land": vmem((PLANES - 1, 2, PAIRS, FRAME, 128), BF),
        "plane_sum": vmem((PLANES, PAIRS, FRAME, 128), BF),
        "line_land": vmem((3, PAIRS, FRAME, 128), BF),
        "total": vmem((PAIRS, FRAME, 128), F32),
        "shard_flat": vmem((count,), BF),
        "shard_sum": vmem((2, -(-count // 1024) * 8, 128), F32),
        "vec_par": vmem((PAIRS, 16, 128), BF),
        "vec_core": vmem((16, D), F32),
        "vec_sum": vmem((16, D), F32),
        "vec_flat": vmem((3, 16, D), F32),
        "vec_line": vmem((3, 16, D), F32),
        "line_send": dma((PAIRS, 3)),
        "line_recv": dma((6,)),
        "flat_send": dma((21,)),
        "flat_recv": dma((21,)),
        "core_send": dma((6,)),
        "core_recv": dma((6,)),
        "sum_core_send": dma((12,)),
        "sum_core_recv": dma((12,)),
        "sum_flat_send": dma((21,)),
        "sum_flat_recv": dma((21,)),
        "sum_line_send": dma((6,)),
        "sum_line_recv": dma((9,)),
        "last_flat_send": dma((3 * len(PIECES),)),
        "last_flat_recv": dma((3 * len(PIECES),)),
        "last_line_send": dma((len(PIECES),)),
        "last_line_recv": dma((3 * len(PIECES),)),
        "par_send": dma((10,)),
        "par_recv": dma((2,)),
        "vec_send": dma((3,)),
        "vec_recv": dma((7,)),
    }


def whole_kernel(names, *refs):
    refs = dict(zip(names, refs))
    refs["flat"] = refs["grads"]
    layer, swap = Layer(refs), Exchange(refs)
    swap.params_copy().start()
    layer.load()
    swap.greet()
    swap.frame_own()
    layer.start()
    swap.greeted()
    swap.send_vectors_line()
    for part in range(PAIRS):
        swap.send_line(0, part, (3, 2, 1))
    swap.send_line(3, 0, (1, 2, 3))
    swap.send_line(2, 0, (3, 2, 1))
    swap.send_line(1, 0, (3,))
    own, second, third = swap.plane_order()
    swap.own_first(lambda: swap.send_next(own))
    swap.send_all(0)
    swap.send_line(1, 0, (2, 1))
    swap.send_vectors_plane()
    swap.send_all(1)
    swap.send_core(0, 0)
    swap.own_first(lambda: swap.send_halves(own))
    swap.send_all(2)
    swap.others_first(lambda: swap.receive_line(own), lambda: swap.send_next(own))
    swap.finish_vectors_plane()
    layer.load_vectors()
    swap.finish_gather(0, 0)
    layer.query_key_value(0)
    layer.attend_first(0)
    swap.receive_line(second)
    swap.send_next(second)
    swap.send_core(0, 1)


    @pl.loop(0, PAIRS)
    def _(pair):
        layer.attend_step(2 * pair, 2 * pair + 1)

        @pl.when(pair == 0)
        def _():
            swap.others_first(lambda: swap.send_halves(own))
            swap.receive_line(third)
            swap.send_next(third)

        @pl.when(pair == 1)
        def _():
            swap.send_halves(second)

        @pl.when(pair == 2)
        def _():
            swap.send_halves(third)

        @pl.when(pair < PAIRS - 1)
        def _():
            swap.finish_gather(0, pair + 1)
            layer.query_key_value(pair + 1)

        layer.attend_step(2 * pair + 1, jnp.minimum(2 * pair + 2, HEADS - 1))

        @pl.when(pair == 0)
        def _():
            swap.send_core(0, 2)

        @pl.when(pair == 1)
        def _():
            swap.send_core(own)

    swap.send_core(second)
    swap.send_core(third)
    swap.finish_gather(1)
    layer.after_attention()
    layer.up_weights(0)
    swap.finish_gather(2)
    layer.up_weights(D // 2)

    layer.feed_forward(lambda: swap.finish_gather(3))
    for block in range(PAIRS):
        layer.grads[block, ROW_VEC:, :] = jnp.zeros((ALL_ROWS - ROW_VEC, 128), BF)
    layer.down_grad(D, FF)
    swap.reduce_core(3)
    layer.down_grad(0, D)
    swap.drain_gather()
    layer.hidden_grad()
    swap.reduce_halves(3)
    layer.up_grad(D // 2)
    swap.reduce_core(2)
    layer.first_norm_grad((0,))
    layer.up_grad(0)
    swap.reduce_next(3)
    swap.reduce_halves(2)
    layer.first_norm_grad((1, 2))
    layer.out_grad()
    swap.reduce_core(1)


    @pl.loop(0, PAIRS)
    def _(pair):
        def early():
            @pl.when(pair == 0)
            def _():
                swap.reduce_halves(1)

        def late():
            @pl.when(pair == 0)
            def _():
                swap.reduce_next(2)

            @pl.when(pair == PAIRS - 1)
            def _():
                swap.reduce_line(0, 0)

            @pl.when(pair > 0)
            def _():
                swap.reduce_all(pair - 1)

        layer.pair_backward(pair, {3: early, 7: late})
        swap.reduce_core(0, pair)

        @pl.when(pair == 0)
        def _():
            swap.reduce_next(1)
            swap.reduce_line(3)

        @pl.when(pair == 1)
        def _():
            swap.reduce_line(2)
            swap.reduce_line(1)

    layer.vector_grads()
    swap.reduce_vectors_core()

    def last_flat():
        swap.reduce_last_all()
        swap.reduce_vectors_flat()
        swap.reduce_line(0, 1)

    layer.input_grad_step({1: last_flat})
    swap.reduce_last_line()
    swap.reduce_vectors_line()
    for plane in (1, 2, 3):
        swap.drain_sum(plane)
        swap.finish_line(plane)
    for part in (0, 1):
        swap.drain_sum(0, part)
        swap.finish_line(0, part)
    swap.finish_vectors()
    swap.unframe((0, 1), False)
    swap.drain_last()
    swap.finish_last_line()
    swap.unframe((2,), True)


def whole_layer(tokens, cotangent, own_params, subnets, lengths):
    rows = tokens.shape[0]
    scratch = scratch_refs() | exchange_refs(own_params.shape[0])
    inputs = ["tokens", "cotangent", "own_params", "subnets", "lengths"]
    outputs = ["layer_out", "input_grad", "own_grad"]
    spaces = [pl.ANY] * 3 + [pltpu.SMEM] * 2
    return pl.pallas_call(
        functools.partial(whole_kernel, inputs + outputs + list(scratch)),
        out_shape=(
            pltpu.VMEM((rows, D), BF),
            pltpu.VMEM((rows, D), F32),
            pltpu.VMEM(own_params.shape, F32),
        ),
        in_specs=[pl.BlockSpec(memory_space=space) for space in spaces],
        out_specs=[pl.BlockSpec(memory_space=pltpu.VMEM)] * 3,
        scratch_shapes=list(scratch.values()),
        compiler_params=pltpu.CompilerParams(
            vmem_limit_bytes=VMEM_LIMIT, collective_id=0, has_side_effects=True
        ),
    )(tokens, cotangent, own_params, subnets, lengths)


def emit_kernel(*refs):
    sems, half = refs[-1], len(refs) // 2
    copies = [pltpu.make_async_copy(refs[i], refs[half + i], sems.at[i]) for i in range(half)]
    for copy in copies:
        copy.start()
    for copy in copies:
        copy.wait()


def emit(*arrays):
    return pl.pallas_call(
        emit_kernel,
        out_shape=[jax.ShapeDtypeStruct(array.shape, array.dtype) for array in arrays],
        in_specs=[pl.BlockSpec(memory_space=pltpu.VMEM)] * len(arrays),
        out_specs=[pl.BlockSpec(memory_space=pl.ANY)] * len(arrays),
        scratch_shapes=[pltpu.SemaphoreType.DMA((len(arrays),))],
        compiler_params=pltpu.CompilerParams(vmem_limit_bytes=8 * 2**20),
    )(*arrays)


def local_kernel(names, *refs):
    refs = dict(zip(names, refs))
    refs["vec_par"] = refs["flat"].at[:, ROW_VEC:, :]
    layer = Layer(refs)
    layer.load()
    layer.start()
    layer.load_vectors()
    for part in range(PAIRS):
        lanes = slice(part * 128, part * 128 + 128)
        layer.w_out[:, lanes] = layer.flat[part, ROW_O:ROW_UP, :]
        layer.w_down[:, lanes] = layer.flat[part, ROW_DOWN:ROW_VEC, :]
    for pair in range(PAIRS):
        layer.query_key_value(pair)
    layer.attend_first(0)

    @pl.loop(0, HEADS)
    def _(head):
        layer.attend_step(head, jnp.minimum(head + 1, HEADS - 1))

    layer.after_attention()
    layer.up_weights(0)
    layer.up_weights(D // 2)
    layer.feed_forward(lambda: None)
    layer.down_grad(0, FF)
    layer.hidden_grad()
    layer.up_grad(0)
    layer.up_grad(D // 2)
    layer.first_norm_grad(range(LIVE // TILE))
    layer.out_grad()
    @pl.loop(0, PAIRS)
    def _(pair):
        layer.pair_backward(pair, {})

    layer.input_grad_step({})
    layer.vector_grads()
    for block in range(PAIRS):
        layer.grads[block, ROW_VEC:, :] = layer.grad_vecs[:, block * 128 : block * 128 + 128].astype(BF)


def local_layer(tokens, cotangent, flat, subnets, lengths):
    rows = tokens.shape[0]
    scratch = scratch_refs() | {"grad_vecs": pltpu.VMEM((16, D), F32)}
    inputs = ["tokens", "cotangent", "flat", "subnets", "lengths"]
    outputs = ["layer_out", "input_grad", "grads"]
    spaces = [pl.ANY] * 2 + [pltpu.VMEM] + [pltpu.SMEM] * 2
    return pl.pallas_call(
        functools.partial(local_kernel, inputs + outputs + list(scratch)),
        out_shape=(
            jax.ShapeDtypeStruct((rows, D), BF),
            jax.ShapeDtypeStruct((rows, D), F32),
            jax.ShapeDtypeStruct((PAIRS, ALL_ROWS, 128), BF),
        ),
        in_specs=[pl.BlockSpec(memory_space=space) for space in spaces],
        out_specs=[pl.BlockSpec(memory_space=pltpu.VMEM)] * 3,
        scratch_shapes=list(scratch.values()),
        compiler_params=pltpu.CompilerParams(vmem_limit_bytes=VMEM_LIMIT),
    )(tokens, cotangent, flat, subnets, lengths)


def on_device(tokens, cotangent, params, subnets, lengths):
    flat = lax.all_gather(params, ("group", "item"), axis=0, tiled=True)
    flat = flat.reshape(-1, D)
    whole = flat.shape[0]
    flat = jnp.pad(flat, ((0, ALL_ROWS - whole), (0, 0)))
    flat = jnp.swapaxes(flat.reshape(ALL_ROWS, PAIRS, 128), 0, 1)
    layer_out, input_grad, grads = local_layer(tokens[0], cotangent[0], flat, subnets, lengths[0])
    grad = jnp.swapaxes(grads[:, :whole], 0, 1).astype(F32).reshape(-1)
    param_grad = lax.psum_scatter(grad, ("group", "item"), scatter_dimension=0, tiled=True)
    return layer_out[None], input_grad[None], param_grad


def on_known_device(tokens, cotangent, params, subnets, lengths):
    results = whole_layer(tokens[0], cotangent[0], params, subnets, lengths[0])
    layer_out, input_grad, own_grad = emit(*results)
    return layer_out[None], input_grad[None], own_grad


def solution(mesh):
    in_specs = (
        P("group", "item", None),
        P("group", "item", None),
        P(("group", "item")),
        P("group", None),
        P("group", "item", None),
    )
    out_specs = (P("group", "item", None), P("group", "item", None), P(("group", "item")))
    known = mesh.shape["group"] == 16 and mesh.shape["item"] == 2
    return jax.shard_map(
        on_known_device if known else on_device, mesh=mesh, in_specs=in_specs, out_specs=out_specs, check_vma=False
    )
```
